32 devices in a mesh: ctx: 4 (over x, core), tp: 8 (over z, y).
Axes of the slice: x: 2, y: 2, z: 4, core: 2. Of those that a mesh axis runs over, the one named last changes fastest.
Arguments:
- lin_query: bfloat16 [2048, 8, 128], P('ctx', 'tp'), may hold values from -6 to 6
- lin_key: bfloat16 [2048, 8, 128], P('ctx', 'tp'), may hold values from -6 to 6
- lin_value: bfloat16 [2048, 8, 128], P('ctx', 'tp'), may hold values from -6 to 6
- log_decay: float32 [8, 2048], P('tp', 'ctx'), may hold values from -2 to 0, as said below
- soft_query: bfloat16 [2048, 8, 128], P('ctx', 'tp'), may hold values from -12 to 12
- soft_key: bfloat16 [2048, 8, 128], P('ctx', 'tp'), may hold values from -4 to 4
- soft_value: bfloat16 [2048, 8, 128], P('ctx', 'tp'), may hold values from -6 to 6
Outputs:
- linear_out: bfloat16 [2048, 8, 128], P('ctx', 'tp')
- softmax_out: bfloat16 [2048, 8, 128], P('ctx', 'tp')
The draws below stay inside these ranges and needn't reach their ends.
Inputs may be any that keep to these rules, and one draw needn't show every extreme that they name: `log_decay`: every entry is negative.
All inputs are finite; a program needn't handle non-finite values.
Results may differ from the reference program's by a relative error of at most 0.0055.
Values may be sent and summed in bfloat16 or wider, within the bound.
No kernel may reach another device: no remote copies, remote signals or barrier semaphores. Data moves between devices by JAX's collectives and lax.ppermute only.
A program may use at most 64 MiB of HBM per device.

```python
import math
import jax
import jax.numpy as jnp
from jax import lax

E = 128
TOK_DEV = 512
NUM_ATTN_GROUPS = 8
SEQUENCE_SPAN = 2048


def draw_log_decay(key, part):

    def sub(number):
        return jax.random.fold_in(key, number)
    fast = jax.random.bernoulli(sub(1), 0.5, (NUM_ATTN_GROUPS,))
    fast_rate = jax.random.uniform(sub(2), (NUM_ATTN_GROUPS,), jnp.float32, 1.0 / 50.0, 1.0 / 30.0)
    slow_rate = jax.random.uniform(sub(3), (NUM_ATTN_GROUPS,), jnp.float32, 0.02, 0.2) / SEQUENCE_SPAN
    base = jnp.where(fast, fast_rate, slow_rate)
    block_factor = jnp.exp(jax.random.uniform(sub(4), (NUM_ATTN_GROUPS, SEQUENCE_SPAN // TOK_DEV), jnp.float32, math.log(0.5), math.log(2.0)))
    token_factor = jnp.exp(jax.random.uniform(sub(5), (NUM_ATTN_GROUPS, SEQUENCE_SPAN), jnp.float32, math.log(1.0 / 3.0), math.log(3.0)))
    fading_speed = base[:, None] * jnp.repeat(block_factor, TOK_DEV, axis=1) * token_factor
    sequence_indices = jax.random.randint(sub(6), (NUM_ATTN_GROUPS, 3), 0, SEQUENCE_SPAN)
    fading_levels = jax.random.uniform(sub(7), (NUM_ATTN_GROUPS, 3), jnp.float32, math.log(0.6), math.log(0.8))
    sequence_segments = jnp.zeros((NUM_ATTN_GROUPS, SEQUENCE_SPAN), jnp.float32).at[jnp.arange(NUM_ATTN_GROUPS)[:, None], sequence_indices].add(fading_levels)
    return -fading_speed + sequence_segments


def query_key_pair(key):
    base_key = jax.random.fold_in(key, 4242)
    query = jnp.clip(jax.random.normal(jax.random.fold_in(base_key, 1), (SEQUENCE_SPAN, NUM_ATTN_GROUPS, E), jnp.float32), -4.0, 4.0)
    keys = jnp.clip(jax.random.normal(jax.random.fold_in(base_key, 2), (SEQUENCE_SPAN, NUM_ATTN_GROUPS, E), jnp.float32), -4.0, 4.0)
    return (query, keys)


def draw_soft_query(key, part):
    return query_key_pair(key)[0].astype(jnp.bfloat16)


def draw_soft_key(key, part):
    return query_key_pair(key)[1].astype(jnp.bfloat16)


def shard_levels(key, dims, split, least, largest):
    factor_of = 1.0
    for dim, shards_of in split:
        heights = jax.random.uniform(jax.random.fold_in(jax.random.fold_in(key, 6), dim), (shards_of,), jnp.float32, least / len(split), largest / len(split))
        factor_of = factor_of * jnp.repeat(jnp.exp(heights), dims[dim] // shards_of).reshape((-1,) + (1,) * (len(dims) - 1 - dim))
    return factor_of


def gaussian(own_key, shape, scale, most, cuts=(), dtype=jnp.bfloat16):
    factor_of = shard_levels(own_key, shape, cuts, -0.22, 0.18) if cuts else 1.0
    array = jax.random.normal(own_key, shape, jnp.float32) * scale * factor_of
    return jnp.minimum(jnp.maximum(array, -most), most).astype(dtype)


def setup_inputs(seed: int = 0) -> dict:
    key_of = jax.random.split(jax.random.key(seed), 8)
    lin_query = gaussian(key_of[0], (SEQUENCE_SPAN, NUM_ATTN_GROUPS, E), 1.0, 6.0, ((0, 4), (1, 8)))
    lin_key = gaussian(key_of[1], (SEQUENCE_SPAN, NUM_ATTN_GROUPS, E), 1.0, 6.0, ((0, 4), (1, 8)))
    lin_value = gaussian(key_of[2], (SEQUENCE_SPAN, NUM_ATTN_GROUPS, E), 1.0, 6.0, ((0, 4), (1, 8)))
    log_decay = draw_log_decay(jax.random.fold_in(key_of[7], 71), 0)
    soft_query = draw_soft_query(jax.random.fold_in(key_of[7], 71), 0)
    soft_key = draw_soft_key(jax.random.fold_in(key_of[7], 71), 0)
    soft_value = gaussian(key_of[6], (SEQUENCE_SPAN, NUM_ATTN_GROUPS, E), 1.0, 6.0, ((0, 4), (1, 8)))
    return dict(lin_query=lin_query, lin_key=lin_key, lin_value=lin_value, log_decay=log_decay, soft_query=soft_query, soft_key=soft_key, soft_value=soft_value)


def lightning(lin_query, lin_key, lin_value, log_decay):
    blocks = SEQUENCE_SPAN // TOK_DEV
    heads = lin_query.shape[1]
    width = lin_query.shape[2]
    qb = lin_query.reshape(blocks, TOK_DEV, heads, width)
    kb = lin_key.reshape(blocks, TOK_DEV, heads, width)
    vb = lin_value.reshape(blocks, TOK_DEV, heads, width)
    lb = jnp.transpose(log_decay.reshape(heads, blocks, TOK_DEV), (1, 0, 2))
    lower = jnp.arange(TOK_DEV)[:, None] >= jnp.arange(TOK_DEV)[None, :]

    def advance(state, inputs):
        query, key, value, logs = inputs
        cum = jnp.cumsum(logs, axis=1)
        diff = cum[:, :, None] - cum[:, None, :]
        mask = jnp.exp(jnp.where(lower[None], diff, -1e+30))
        scores = jnp.einsum('thd,shd->hts', query.astype(jnp.float32), key.astype(jnp.float32))
        weights = (scores * mask).astype(jnp.bfloat16)
        intra = jnp.einsum('hts,she->the', weights.astype(jnp.float32), value.astype(jnp.float32))
        rounded = lax.optimization_barrier(state.astype(jnp.bfloat16))
        inter = jnp.einsum('thd,hde->the', query.astype(jnp.float32), rounded.astype(jnp.float32))
        inter = inter * jnp.exp(cum).T[:, :, None]
        raw = intra + inter
        normed = raw * lax.rsqrt(lax.optimization_barrier(jnp.mean(raw * raw, axis=-1, keepdims=True)) + 1e-06)
        last = cum[:, -1]
        decayed = (key.astype(jnp.float32) * jnp.exp(last[None, :] - cum.T)[:, :, None]).astype(jnp.bfloat16)
        local = jnp.einsum('thd,the->hde', decayed.astype(jnp.float32), value.astype(jnp.float32))
        new_state = jnp.exp(last)[:, None, None] * state + local
        return (new_state, normed.astype(jnp.bfloat16))
    start = jnp.zeros((heads, width, width), jnp.float32)
    final, outs = lax.scan(advance, start, (qb, kb, vb, lb))
    return outs.reshape(SEQUENCE_SPAN, heads, width)

def softmax_layer(soft_query, soft_key, soft_value):
    width = soft_query.shape[2]
    scale = 1.0 / jnp.sqrt(jnp.float32(width))
    blocks = SEQUENCE_SPAN // TOK_DEV
    key_pos = jnp.arange(SEQUENCE_SPAN)

    def one_head(inputs):
        query, key, value = inputs
        qb = query.reshape(blocks, TOK_DEV, width)

        def one_block(pair):
            index, rows = pair
            q_pos = index * TOK_DEV + jnp.arange(TOK_DEV)
            scores = jnp.dot(rows, key.T, preferred_element_type=jnp.float32) * scale
            mask = q_pos[:, None] >= key_pos[None, :]
            scores = jnp.where(mask, scores, -1e+30)
            top = lax.optimization_barrier(jnp.max(scores, axis=1, keepdims=True))
            probs = jnp.where(mask, jnp.exp(scores - top), 0.0)
            total = lax.optimization_barrier(jnp.sum(probs, axis=1, keepdims=True))
            summed = jnp.dot(probs.astype(jnp.bfloat16), value, preferred_element_type=jnp.float32)
            return (summed / total).astype(jnp.bfloat16)
        outs = lax.map(one_block, (jnp.arange(blocks), qb))
        return outs.reshape(SEQUENCE_SPAN, width)
    per_head = lax.map(one_head, (jnp.moveaxis(soft_query, 1, 0), jnp.moveaxis(soft_key, 1, 0), jnp.moveaxis(soft_value, 1, 0)))
    return jnp.moveaxis(per_head, 0, 1)

def reference(lin_query, lin_key, lin_value, log_decay, soft_query, soft_key, soft_value):
    linear_out = lightning(lin_query, lin_key, lin_value, log_decay)
    softmax_out = softmax_layer(soft_query, soft_key, soft_value)
    return (linear_out, softmax_out)
```

```python
import functools
import math

import jax
import jax.numpy as jnp
from jax import lax
from jax.experimental import pallas as pl
from jax.experimental.pallas import tpu as pltpu
from jax.sharding import PartitionSpec as P

NEG = -1e30
TINY = 1e-6
PAD = 16
F32 = jnp.float32
BF16 = jnp.bfloat16
VMEM = pltpu.VMEM


def dot(a, b, contract):
    return lax.dot_general(a, b, (contract, ((), ())), preferred_element_type=F32)


def dot_nn(a, b):
    return dot(a, b, ((1,), (0,)))


def dot_nt(a, b):
    return dot(a, b, ((1,), (1,)))


def dot_tn(a, b):
    return dot(a, b, ((0,), (0,)))


def three_parts(x):
    high = x.astype(BF16)
    rest = x - high.astype(F32)
    middle = rest.astype(BF16)
    low = (rest - middle.astype(F32)).astype(BF16)
    return high, middle, low


def iota(shape, dim):
    return lax.broadcasted_iota(jnp.int32, shape, dim)


def select_rows(parts, rows, width):
    row = iota((rows, width), 0)
    out = jnp.zeros((rows, width), F32)
    for number, part in enumerate(parts):
        out = jnp.where(row == number, part.astype(F32), out)
    return out.astype(BF16)


def state_kernel(decay_ref, key_ref, value_ref, soft_value_ref, pack_ref, cum_row_ref, cum_col_ref):
    rows, width = key_ref.shape
    parts = select_rows(three_parts(decay_ref[...]), PAD, rows)
    upto = (iota((rows, rows), 0) <= iota((rows, rows), 1)).astype(F32).astype(BF16)
    cum_row = jnp.sum(dot_nn(parts, upto), axis=0, keepdims=True)
    cum_row_ref[...] = cum_row
    cum_col = jnp.transpose(jnp.broadcast_to(cum_row, (width, rows)))
    cum_col_ref[...] = cum_col
    total = cum_col[rows - 1 :, :]
    decayed = (key_ref[...].astype(F32) * jnp.exp(total - cum_col)).astype(BF16)
    state = dot_tn(decayed, value_ref[...])
    high = state.astype(BF16)
    pack_ref[:rows, :] = soft_value_ref[...]
    pack_ref[rows : rows + width, :] = high
    pack_ref[rows + width : rows + 2 * width, :] = (state - high.astype(F32)).astype(BF16)
    pack_ref[rows + 2 * width :, :] = select_rows(three_parts(total), PAD, width)


def local_kernel(
    scale, step,
    lin_q_ref, lin_k_ref, lin_v_ref, cum_row_ref, cum_col_ref, q_ref, k_ref, v_ref,
    intra_ref, top_ref, total_ref, summed_ref,
):
    rows, width = lin_q_ref.shape
    lower = iota((step, step), 0) >= iota((step, step), 1)
    for start in range(0, rows, step):
        stop = start + step
        mine = pl.ds(start, step)
        scores = dot_nt(lin_q_ref[mine, :], lin_k_ref[:stop, :])
        cum_t = cum_col_ref[mine, :1]
        weights = []
        for left in range(0, stop, step):
            diff = cum_t - cum_row_ref[:, left : left + step]
            if left == start:
                diff = jnp.where(lower, diff, NEG)
            weights.append((scores[:, left : left + step] * jnp.exp(diff)).astype(BF16))
        weights = jnp.concatenate(weights, axis=1) if len(weights) > 1 else weights[0]
        intra_ref[mine, :] = dot_nn(weights, lin_v_ref[:stop, :])

        scores = dot_nt(q_ref[mine, :], k_ref[:stop, :])
        last = jnp.where(lower, scores[:, start:], NEG)
        scores = jnp.concatenate([scores[:, :start], last], axis=1) if start else last
        top = jnp.max(scores, axis=1, keepdims=True)
        probs = jnp.exp2((scores - top) * scale)
        total = jnp.sum(probs, axis=1, keepdims=True)
        top_ref[mine, :] = jnp.broadcast_to(top, (step, width))
        total_ref[mine, :] = jnp.broadcast_to(total, (step, width))
        summed_ref[mine, :] = dot_nn(probs.astype(BF16), v_ref[:stop, :])


def block_numbers(axis, cores, chips):
    position = lax.axis_index(axis)
    if cores == 1:
        return position, [position - apart for apart in range(1, chips)]
    other = lax.rem(position, 2)
    partner = position + 1 - 2 * other
    numbers = [jnp.where(other == 1, position - 1, -1)]
    for apart in range(1, chips):
        numbers += [position - 2 * apart, partner - 2 * apart]
    return position, numbers


def score_kernel(scale, step, axis, cores, chips, q_ref, top_ref, total_ref, *refs):
    key_refs, (probs_ref, factor_ref, sum_ref) = refs[:-3], refs[-3:]
    rows, width = q_ref.shape
    _, numbers = block_numbers(axis, cores, chips)
    away = [jnp.where(number >= 0, 0.0, NEG) for number in numbers]
    for start in range(0, rows, step):
        mine = pl.ds(start, step)
        query = q_ref[mine, :]
        old = top_ref[mine, :1]
        scores = [dot_nt(query, key_ref[...]) for key_ref in key_refs]
        top = old
        for score, off in zip(scores, away):
            top = jnp.maximum(top, jnp.max(score, axis=1, keepdims=True) + off)
        factor = jnp.exp2((old - top) * scale)
        total = total_ref[mine, :1] * factor
        for number, (score, off) in enumerate(zip(scores, away)):
            probs = jnp.exp2((score - (top - off)) * scale)
            total = total + jnp.sum(probs, axis=1, keepdims=True)
            probs_ref[mine, number * rows : (number + 1) * rows] = probs.astype(BF16)
        factor_ref[mine, :] = jnp.broadcast_to(factor, (step, width))
        sum_ref[mine, :] = jnp.broadcast_to(total, (step, width))


def finish_kernel(
    step, axis, cores, chips,
    lin_q_ref, intra_ref, cum_col_ref, summed_ref, probs_ref, factor_ref, sum_ref, *refs,
):
    pack_refs, (linear_ref, softmax_ref) = refs[:-2], refs[-2:]
    rows, width = lin_q_ref.shape
    position, numbers = block_numbers(axis, cores, chips)
    totals, states = [], []
    for pack_ref in pack_refs:
        tail = pack_ref[rows + 2 * width :, :].astype(F32)
        totals.append(tail[0:1] + tail[1:2] + tail[2:3])
        states.append(
            pack_ref[rows : rows + width, :].astype(F32)
            + pack_ref[rows + width : rows + 2 * width, :].astype(F32)
        )
    carried = jnp.zeros((width, width), F32)
    for number, state in zip(numbers, states):
        between = jnp.where(number >= 0, 0.0, NEG)
        for other, total in zip(numbers, totals):
            between = between + jnp.where(other > number, 1.0, 0.0) * total
        carried = carried + jnp.exp(between) * state
    carried = carried.astype(BF16)
    for start in range(0, rows, step):
        mine = pl.ds(start, step)
        summed = summed_ref[mine, :] * factor_ref[mine, :]
        for number, pack_ref in enumerate(pack_refs):
            summed = summed + dot_nn(
                probs_ref[mine, number * rows : (number + 1) * rows], pack_ref[:rows, :]
            )
        softmax_ref[mine, :] = (summed / sum_ref[mine, :]).astype(BF16)
        inter = dot_nn(lin_q_ref[mine, :], carried)
        raw = intra_ref[mine, :] + inter * jnp.exp(cum_col_ref[mine, :])
        square = jnp.sum(raw * raw, axis=1, keepdims=True) * (1.0 / width)
        linear_ref[mine, :] = (raw * lax.rsqrt(square + TINY)).astype(BF16)


def call(body, operands, outs, flops):
    size = sum(math.prod(x.shape) * x.dtype.itemsize for x in (*operands, *outs))
    return pl.pallas_call(
        body,
        out_shape=tuple(outs),
        in_specs=[pl.BlockSpec(memory_space=VMEM)] * len(operands),
        out_specs=tuple(pl.BlockSpec(memory_space=VMEM) for _ in outs),
        cost_estimate=pl.CostEstimate(flops=flops, bytes_accessed=size, transcendentals=0),
    )(*operands)


def on_device(axis, lin_query, lin_key, lin_value, log_decay, soft_query, soft_key, soft_value):
    rows, heads, width = lin_query.shape
    count = lax.axis_size(axis)
    cores = 2 if count % 2 == 0 else 1
    chips = count // cores

    def to_partner(x):
        return lax.ppermute(x, axis, [(2 * chip, 2 * chip + 1) for chip in range(chips)])

    def across(x, apart):
        apart = apart * cores
        return lax.ppermute(x, axis, [(i, i + apart) for i in range(count - apart)])

    def swapped(x):
        return lax.ppermute(x, axis, [(i, i ^ 1) for i in range(count)])

    def spread(x):
        own = [to_partner(x)] if cores == 2 else []
        far = [across(x, apart) for apart in range(1, chips)]
        out = list(own)
        for block in far:
            out.append(block)
            if cores == 2:
                out.append(swapped(block))
        return out

    def one_head(lq, lk, lv, decay, sq, sk, sv):
        step = math.gcd(rows, 128)
        scale = math.log2(math.e) / math.sqrt(width)
        shape = jax.ShapeDtypeStruct
        flat = shape((rows, width), F32)
        keys = spread(sk)
        pack, cum_row, cum_col = call(
            state_kernel,
            (decay, lk, lv, sv),
            (shape((rows + 2 * width + PAD, width), BF16), shape((1, rows), F32), flat),
            2 * rows * width * width,
        )
        packs = spread(pack)
        intra, top, total, summed = call(
            functools.partial(local_kernel, scale, step),
            (lq, lk, lv, cum_row, cum_col, sq, sk, sv),
            (flat, flat, flat, flat),
            8 * rows * rows * width,
        )
        blocks = len(keys)
        ring = (axis, cores, chips)
        probs, factor, sums = call(
            functools.partial(score_kernel, scale, step, *ring),
            (sq, top, total, *keys),
            (shape((rows, blocks * rows), BF16), flat, flat),
            2 * blocks * rows * rows * width,
        )
        out = shape((rows, width), BF16)
        return call(
            functools.partial(finish_kernel, step, *ring),
            (lq, intra, cum_col, summed, probs, factor, sums, *packs),
            (out, out),
            2 * blocks * rows * rows * width,
        )

    outs = [
        one_head(
            *(x[:, head] for x in (lin_query, lin_key, lin_value)),
            log_decay[head : head + 1],
            *(x[:, head] for x in (soft_query, soft_key, soft_value)),
        )
        for head in range(heads)
    ]
    linear = jnp.stack([pair[0] for pair in outs], axis=1)
    softmax = jnp.stack([pair[1] for pair in outs], axis=1)
    return linear, softmax


def solution(mesh):
    block = P("ctx", "tp", None)
    return jax.shard_map(
        functools.partial(on_device, "ctx"),
        mesh=mesh,
        in_specs=(block, block, block, P("tp", "ctx"), block, block, block),
        out_specs=(block, block),
        check_vma=False,
    )
```

```python
import functools
import math

import jax
import jax.numpy as jnp
from jax import lax
from jax.experimental import pallas as pl
from jax.experimental.pallas import tpu as pltpu
from jax.sharding import PartitionSpec as P

NEG = -1e30
TINY = 1e-6
PAD = 16
F32 = jnp.float32
BF16 = jnp.bfloat16
VMEM = pltpu.VMEM


def dot(a, b):
    return lax.dot_general(a, b, (((1,), (0,)), ((), ())), preferred_element_type=F32)


def three_parts(x):
    high = x.astype(BF16)
    rest = x - high.astype(F32)
    middle = rest.astype(BF16)
    low = (rest - middle.astype(F32)).astype(BF16)
    return high, middle, low


def iota(shape, dim):
    return lax.broadcasted_iota(jnp.int32, shape, dim)


def select_rows(parts, rows, width):
    row = iota((rows, width), 0)
    out = jnp.zeros((rows, width), F32)
    for number, part in enumerate(parts):
        out = jnp.where(row == number, part.astype(F32), out)
    return out.astype(BF16)


def side_by_side(ref, rows, width):
    pieces = [ref[left : left + width, :] for left in range(0, rows, width)]
    return pieces[0] if len(pieces) == 1 else jnp.concatenate(pieces, axis=1)


def state_kernel(
    decay_ref, key_ref, value_ref, soft_value_ref, pack_ref, cum_row_ref, cum_col_ref, value_t_ref
):
    rows, width = key_ref.shape
    parts = select_rows(three_parts(decay_ref[...]), PAD, rows)
    upto = (iota((rows, rows), 0) <= iota((rows, rows), 1)).astype(F32).astype(BF16)
    cum_row = jnp.sum(dot(parts, upto), axis=0, keepdims=True)
    cum_row_ref[...] = cum_row
    cum_col = jnp.transpose(jnp.broadcast_to(cum_row, (width, rows)))
    cum_col_ref[...] = cum_col
    total = cum_col[rows - 1 :, :]
    decayed = (key_ref[...].astype(F32) * jnp.exp(total - cum_col)).astype(BF16)
    value_t = jnp.transpose(value_ref[...])
    value_t_ref[...] = value_t
    state_t = dot(value_t, decayed)
    high = state_t.astype(BF16)
    for left in range(0, rows, width):
        pack_ref[left : left + width, :] = jnp.transpose(soft_value_ref[left : left + width, :])
    pack_ref[rows : rows + width, :] = high
    pack_ref[rows + width : rows + 2 * width, :] = (state_t - high.astype(F32)).astype(BF16)
    pack_ref[rows + 2 * width :, :] = select_rows(three_parts(total), PAD, width)


def local_kernel(
    scale, step,
    lin_q_ref, lin_k_ref, lin_vt_ref, cum_row_ref, cum_col_ref, q_ref, k_ref, pack_ref,
    lin_qt_ref, qt_ref, intra_ref, top_ref, total_ref, summed_ref,
):
    rows, width = lin_q_ref.shape
    lin_qt_ref[...] = jnp.transpose(lin_q_ref[...])
    qt_ref[...] = jnp.transpose(q_ref[...])
    soft_vt = side_by_side(pack_ref, rows, width)
    keep = iota((step, step), 0) <= iota((step, step), 1)
    for start in range(0, rows, step):
        stop = start + step
        scores = dot(k_ref[:stop, :], qt_ref[:, start:stop])
        last = jnp.where(keep, scores[start:, :], NEG)
        scores = jnp.concatenate([scores[:start, :], last], axis=0) if start else last
        top = jnp.max(scores, axis=0, keepdims=True)
        probs = jnp.exp2((scores - top) * scale)
        top_ref[:, start:stop] = top
        total_ref[:, start:stop] = jnp.sum(probs, axis=0, keepdims=True)
        summed_ref[:, start:stop] = dot(soft_vt[:, :stop], probs.astype(BF16))

        scores = dot(lin_k_ref[:stop, :], lin_qt_ref[:, start:stop])
        cum_t = cum_row_ref[:, start:stop]
        cum_s = jnp.concatenate([cum_col_ref[:stop, :]] * (step // width), axis=1)
        diff = cum_t - cum_s
        last = jnp.where(keep, diff[start:, :], NEG)
        diff = jnp.concatenate([diff[:start, :], last], axis=0) if start else last
        weights = (scores * jnp.exp(diff)).astype(BF16)
        intra_ref[:, start:stop] = dot(lin_vt_ref[:, :stop], weights)


def block_numbers(axis, cores, chips):
    position = lax.axis_index(axis)
    if cores == 1:
        return position, [position - apart for apart in range(1, chips)]
    other = lax.rem(position, 2)
    partner = position + 1 - 2 * other
    numbers = [jnp.where(other == 1, position - 1, -1)]
    for apart in range(1, chips):
        numbers += [position - 2 * apart, partner - 2 * apart]
    return position, numbers


def by_chip(position, cores, count, body):
    pl.when(position >= cores)(lambda: body(count))
    pl.when(position < cores)(lambda: body(cores - 1))


def score_kernel(scale, step, axis, cores, chips, qt_ref, top_ref, total_ref, *refs):
    key_refs, (probs_ref, factor_ref, sum_ref) = refs[:-3], refs[-3:]
    rows = qt_ref.shape[1]
    position, numbers = block_numbers(axis, cores, chips)
    away = [jnp.where(number >= 0, 0.0, NEG) for number in numbers]

    def body(count):
        for start in range(0, rows, step):
            mine = slice(start, start + step)
            query = qt_ref[:, mine]
            old = top_ref[:, mine]
            scores = [dot(key_refs[i][...], query) for i in range(count)]
            top = old
            for score, off in zip(scores, away):
                top = jnp.maximum(top, jnp.max(score, axis=0, keepdims=True) + off)
            factor = jnp.exp2((old - top) * scale)
            total = total_ref[:, mine] * factor
            for number, (score, off) in enumerate(zip(scores, away)):
                probs = jnp.exp2((score - (top - off)) * scale)
                total = total + jnp.sum(probs, axis=0, keepdims=True)
                probs_ref[number * rows : (number + 1) * rows, mine] = probs.astype(BF16)
            factor_ref[:, mine] = factor
            sum_ref[:, mine] = total

    by_chip(position, cores, len(key_refs), body)


def finish_kernel(
    step, axis, cores, chips,
    lin_qt_ref, intra_ref, cum_row_ref, summed_ref, probs_ref, factor_ref, sum_ref, *refs,
):
    pack_refs, (linear_ref, softmax_ref) = refs[:-2], refs[-2:]
    width, rows = lin_qt_ref.shape
    position, numbers = block_numbers(axis, cores, chips)

    def body(count):
        totals, states = [], []
        for pack_ref in pack_refs[:count]:
            tail = pack_ref[rows + 2 * width :, :].astype(F32)
            totals.append(tail[0:1] + tail[1:2] + tail[2:3])
            states.append(
                pack_ref[rows : rows + width, :].astype(F32)
                + pack_ref[rows + width : rows + 2 * width, :].astype(F32)
            )
        carried = jnp.zeros((width, width), F32)
        for number, state in zip(numbers, states):
            between = jnp.where(number >= 0, 0.0, NEG)
            for other, total in zip(numbers, totals):
                between = between + jnp.where(other > number, 1.0, 0.0) * total
            carried = carried + jnp.exp(between) * state
        carried = carried.astype(BF16)
        values = [side_by_side(pack_ref, rows, width) for pack_ref in pack_refs[:count]]
        for start in range(0, rows, step):
            mine = slice(start, start + step)
            summed = summed_ref[:, mine] * factor_ref[:, mine]
            for number, value in enumerate(values):
                summed = summed + dot(value, probs_ref[number * rows : (number + 1) * rows, mine])
            softmax_ref[mine, :] = jnp.transpose(summed / sum_ref[:, mine]).astype(BF16)
            inter = dot(carried, lin_qt_ref[:, mine])
            raw = intra_ref[:, mine] + inter * jnp.exp(cum_row_ref[:, mine])
            square = jnp.sum(raw * raw, axis=0, keepdims=True) * (1.0 / width)
            linear_ref[mine, :] = jnp.transpose(raw * lax.rsqrt(square + TINY)).astype(BF16)

    by_chip(position, cores, len(pack_refs), body)


def keep_in_hbm(x):
    return pltpu.with_memory_space_constraint(x, pltpu.HBM)


def kept_in_vmem(x):
    return VMEM(x.shape, x.dtype)


def call(body, operands, outs, last=False):
    size = sum(math.prod(x.shape) * x.dtype.itemsize for x in (*operands, *outs))
    if not last:
        outs = [kept_in_vmem(x) for x in outs]
    return pl.pallas_call(
        body,
        out_shape=tuple(outs),
        in_specs=[pl.BlockSpec(memory_space=VMEM)] * len(operands),
        out_specs=tuple(pl.BlockSpec(memory_space=VMEM) for _ in outs),
        cost_estimate=pl.CostEstimate(flops=0, bytes_accessed=size, transcendentals=0),
    )(*operands)


def on_device(axis, lin_query, lin_key, lin_value, log_decay, soft_query, soft_key, soft_value):
    rows, heads, width = lin_query.shape
    count = lax.axis_size(axis)
    cores = 2 if count % 2 == 0 else 1
    chips = count // cores

    def across(x, apart):
        return lax.ppermute(x, axis, [(i, (i + apart * cores) % count) for i in range(count)])

    def swapped(x, after=None):
        if after is not None:
            x, _ = lax.optimization_barrier((x, after))
        return lax.ppermute(x, axis, [(i, i ^ 1) for i in range(count)])

    def spread(x):
        far = [across(x, apart) for apart in range(1, chips)]
        own = [swapped(x)] if cores == 2 else []
        return own, far

    def complete(of, after):
        own, far = of
        out = list(own)
        for block in far:
            out.append(block)
            if cores == 2:
                out.append(swapped(block, after))
        return out

    def one_head(lq, lk, lv, decay, sq, sk, sv):
        step = math.gcd(rows, 256)
        scale = math.log2(math.e) / math.sqrt(width)

        def shape(*dims, dtype=F32):
            return jax.ShapeDtypeStruct(dims, dtype)

        row, flat, flat16 = shape(1, rows), shape(width, rows), shape(width, rows, dtype=BF16)
        keys = spread(sk)
        lq, lk, lv, decay, sq, sk, sv = map(keep_in_hbm, (lq, lk, lv, decay, sq, sk, sv))
        pack, cum_row, cum_col, lin_vt = call(
            state_kernel,
            (decay, lk, lv, sv),
            (shape(rows + 2 * width + PAD, width, dtype=BF16), row, shape(rows, width), flat16),
        )
        packs = spread(pack)
        lin_qt, qt, intra, top, total, summed = call(
            functools.partial(local_kernel, scale, step),
            (lq, lk, lin_vt, cum_row, cum_col, sq, sk, pack),
            (flat16, flat16, flat, row, row, flat),
        )
        ring = (axis, cores, chips)
        keys = complete(keys, intra)
        probs, factor, sums = call(
            functools.partial(score_kernel, scale, step, *ring),
            (qt, top, total, *keys),
            (shape(len(keys) * rows, rows, dtype=BF16), row, row),
        )
        out = shape(rows, width, dtype=BF16)
        packs = complete(packs, factor)
        return call(
            functools.partial(finish_kernel, step, *ring),
            (lin_qt, intra, cum_row, summed, probs, factor, sums, *packs),
            (out, out),
            last=True,
        )

    outs = [
        one_head(
            *(x[:, head] for x in (lin_query, lin_key, lin_value)),
            log_decay[head : head + 1],
            *(x[:, head] for x in (soft_query, soft_key, soft_value)),
        )
        for head in range(heads)
    ]
    linear = jnp.stack([pair[0] for pair in outs], axis=1)
    softmax = jnp.stack([pair[1] for pair in outs], axis=1)
    return linear, softmax


def solution(mesh):
    block = P("ctx", "tp", None)
    return jax.shard_map(
        functools.partial(on_device, "ctx"),
        mesh=mesh,
        in_specs=(block, block, block, P("tp", "ctx"), block, block, block),
        out_specs=(block, block),
        check_vma=False,
    )
```

```python
import functools
import math

import jax
import jax.numpy as jnp
from jax import lax
from jax.experimental import pallas as pl
from jax.experimental.pallas import tpu as pltpu
from jax.sharding import PartitionSpec as P

NEG = -1e30
TINY = 1e-6
PAD = 16
F32 = jnp.float32
BF16 = jnp.bfloat16
VMEM = pltpu.VMEM


def dot(a, b):
    return lax.dot_general(a, b, (((1,), (0,)), ((), ())), preferred_element_type=F32)


def three_parts(x):
    high = x.astype(BF16)
    rest = x - high.astype(F32)
    middle = rest.astype(BF16)
    low = (rest - middle.astype(F32)).astype(BF16)
    return high, middle, low


def iota(shape, dim):
    return lax.broadcasted_iota(jnp.int32, shape, dim)


def select_rows(parts, rows, width):
    row = iota((rows, width), 0)
    out = jnp.zeros((rows, width), F32)
    for number, part in enumerate(parts):
        out = jnp.where(row == number, part.astype(F32), out)
    return out.astype(BF16)


def side_by_side(ref, rows, width):
    pieces = [ref[left : left + width, :] for left in range(0, rows, width)]
    return pieces[0] if len(pieces) == 1 else jnp.concatenate(pieces, axis=1)


def state_kernel(
    decay_ref, key_ref, value_ref, soft_value_ref, pack_ref, cum_row_ref, cum_col_ref, value_t_ref
):
    rows, width = key_ref.shape
    parts = select_rows(three_parts(decay_ref[...]), PAD, rows)
    upto = (iota((rows, rows), 0) <= iota((rows, rows), 1)).astype(F32).astype(BF16)
    cum_row = jnp.sum(dot(parts, upto), axis=0, keepdims=True)
    cum_row_ref[...] = cum_row
    cum_col = jnp.transpose(jnp.broadcast_to(cum_row, (width, rows)))
    cum_col_ref[...] = cum_col
    total = cum_col[rows - 1 :, :]
    decayed = (key_ref[...].astype(F32) * jnp.exp(total - cum_col)).astype(BF16)
    value_t = jnp.transpose(value_ref[...])
    value_t_ref[...] = value_t
    state_t = dot(value_t, decayed)
    high = state_t.astype(BF16)
    for left in range(0, rows, width):
        pack_ref[left : left + width, :] = jnp.transpose(soft_value_ref[left : left + width, :])
    pack_ref[rows : rows + width, :] = high
    pack_ref[rows + width : rows + 2 * width, :] = (state_t - high.astype(F32)).astype(BF16)
    pack_ref[rows + 2 * width :, :] = select_rows(three_parts(total), PAD, width)


def local_kernel(
    scale, step,
    lin_q_ref, lin_k_ref, q_ref, k_ref, lin_vt_ref, cum_row_ref, cum_col_ref, pack_ref,
    lin_qt_ref, qt_ref, intra_ref, top_ref, total_ref, summed_ref,
):
    rows, width = lin_q_ref.shape
    lin_qt_ref[...] = jnp.transpose(lin_q_ref[...])
    qt_ref[...] = jnp.transpose(q_ref[...])
    soft_vt = side_by_side(pack_ref, rows, width)
    keep = iota((step, step), 0) <= iota((step, step), 1)
    for start in range(0, rows, step):
        stop = start + step
        scores = dot(k_ref[:stop, :], qt_ref[:, start:stop])
        last = jnp.where(keep, scores[start:, :], NEG)
        scores = jnp.concatenate([scores[:start, :], last], axis=0) if start else last
        top = jnp.max(scores, axis=0, keepdims=True)
        probs = jnp.exp2((scores - top) * scale)
        top_ref[:, start:stop] = top
        total_ref[:, start:stop] = jnp.sum(probs, axis=0, keepdims=True)
        summed_ref[:, start:stop] = dot(soft_vt[:, :stop], probs.astype(BF16))

        scores = dot(lin_k_ref[:stop, :], lin_qt_ref[:, start:stop])
        cum_t = cum_row_ref[:, start:stop]
        cum_s = jnp.concatenate([cum_col_ref[:stop, :]] * (step // width), axis=1)
        diff = cum_t - cum_s
        last = jnp.where(keep, diff[start:, :], NEG)
        diff = jnp.concatenate([diff[:start, :], last], axis=0) if start else last
        weights = (scores * jnp.exp(diff)).astype(BF16)
        intra_ref[:, start:stop] = dot(lin_vt_ref[:, :stop], weights)


def block_numbers(axis, cores, chips):
    position = lax.axis_index(axis)
    if cores == 1:
        return position, [position - apart for apart in range(1, chips)]
    other = lax.rem(position, 2)
    partner = position + 1 - 2 * other
    numbers = [jnp.where(other == 1, position - 1, -1)]
    for apart in range(1, chips):
        numbers += [position - 2 * apart, partner - 2 * apart]
    return position, numbers


def by_chip(position, cores, count, body):
    pl.when(position >= cores)(lambda: body(count))
    pl.when(position < cores)(lambda: body(cores - 1))


def score_kernel(scale, step, axis, cores, chips, qt_ref, top_ref, total_ref, *refs):
    key_refs, (probs_ref, factor_ref, sum_ref) = refs[:-3], refs[-3:]
    rows = qt_ref.shape[1]
    position, numbers = block_numbers(axis, cores, chips)
    away = [jnp.where(number >= 0, 0.0, NEG) for number in numbers]

    def body(count):
        for start in range(0, rows, step):
            mine = slice(start, start + step)
            query = qt_ref[:, mine]
            old = top_ref[:, mine]
            scores = [dot(key_refs[i][...], query) for i in range(count)]
            top = old
            for score, off in zip(scores, away):
                top = jnp.maximum(top, jnp.max(score, axis=0, keepdims=True) + off)
            factor = jnp.exp2((old - top) * scale)
            total = total_ref[:, mine] * factor
            for number, (score, off) in enumerate(zip(scores, away)):
                probs = jnp.exp2((score - (top - off)) * scale)
                total = total + jnp.sum(probs, axis=0, keepdims=True)
                probs_ref[number * rows : (number + 1) * rows, mine] = probs.astype(BF16)
            factor_ref[:, mine] = factor
            sum_ref[:, mine] = total

    by_chip(position, cores, len(key_refs), body)


def finish_kernel(
    step, axis, cores, chips,
    lin_qt_ref, intra_ref, cum_row_ref, summed_ref, probs_ref, factor_ref, sum_ref, *refs,
):
    pack_refs, (linear_ref, softmax_ref) = refs[:-2], refs[-2:]
    width, rows = lin_qt_ref.shape
    position, numbers = block_numbers(axis, cores, chips)

    def body(count):
        totals, states = [], []
        for pack_ref in pack_refs[:count]:
            tail = pack_ref[rows + 2 * width :, :].astype(F32)
            totals.append(tail[0:1] + tail[1:2] + tail[2:3])
            states.append(
                pack_ref[rows : rows + width, :].astype(F32)
                + pack_ref[rows + width : rows + 2 * width, :].astype(F32)
            )
        carried = jnp.zeros((width, width), F32)
        for number, state in zip(numbers, states):
            between = jnp.where(number >= 0, 0.0, NEG)
            for other, total in zip(numbers, totals):
                between = between + jnp.where(other > number, 1.0, 0.0) * total
            carried = carried + jnp.exp(between) * state
        carried = carried.astype(BF16)
        values = [side_by_side(pack_ref, rows, width) for pack_ref in pack_refs[:count]]
        for start in range(0, rows, step):
            mine = slice(start, start + step)
            summed = summed_ref[:, mine] * factor_ref[:, mine]
            for number, value in enumerate(values):
                summed = summed + dot(value, probs_ref[number * rows : (number + 1) * rows, mine])
            softmax_ref[mine, :] = jnp.transpose(summed / sum_ref[:, mine]).astype(BF16)
            inter = dot(carried, lin_qt_ref[:, mine])
            raw = intra_ref[:, mine] + inter * jnp.exp(cum_row_ref[:, mine])
            square = jnp.sum(raw * raw, axis=0, keepdims=True) * (1.0 / width)
            linear_ref[mine, :] = jnp.transpose(raw * lax.rsqrt(square + TINY)).astype(BF16)

    by_chip(position, cores, len(pack_refs), body)


def keep_in_hbm(x):
    return pltpu.with_memory_space_constraint(x, pltpu.HBM)


def keep_in_vmem(x):
    return pltpu.with_memory_space_constraint(x, VMEM)


def kept_in_vmem(x):
    return VMEM(x.shape, x.dtype)


def call(body, given, operands, outs, last=False):
    size = sum(math.prod(x.shape) * x.dtype.itemsize for x in (*given, *operands, *outs))
    operands = [*map(keep_in_hbm, given), *map(keep_in_vmem, operands)]
    if not last:
        outs = [kept_in_vmem(x) for x in outs]
    return pl.pallas_call(
        body,
        out_shape=tuple(outs),
        in_specs=[pl.BlockSpec(memory_space=VMEM)] * len(operands),
        out_specs=tuple(pl.BlockSpec(memory_space=VMEM) for _ in outs),
        cost_estimate=pl.CostEstimate(flops=0, bytes_accessed=size, transcendentals=0),
    )(*operands)


def on_device(axis, lin_query, lin_key, lin_value, log_decay, soft_query, soft_key, soft_value):
    rows, heads, width = lin_query.shape
    count = lax.axis_size(axis)
    cores = 2 if count % 2 == 0 else 1
    chips = count // cores

    def across(x, apart):
        return lax.ppermute(x, axis, [(i, (i + apart * cores) % count) for i in range(count)])

    def swapped(x, after=None):
        if after is not None:
            x, _ = lax.optimization_barrier((x, after))
        return lax.ppermute(x, axis, [(i, i ^ 1) for i in range(count)])

    def spread(x):
        far = [across(x, apart) for apart in range(1, chips)]
        own = [swapped(x)] if cores == 2 else []
        return own, far

    def complete(of, after):
        own, far = of
        out = list(own)
        for block in far:
            out.append(block)
            if cores == 2:
                out.append(swapped(block, after))
        return out

    def one_head(lq, lk, lv, decay, sq, sk, sv):
        step = math.gcd(rows, 256)
        scale = math.log2(math.e) / math.sqrt(width)

        def shape(*dims, dtype=F32):
            return jax.ShapeDtypeStruct(dims, dtype)

        row, flat, flat16 = shape(1, rows), shape(width, rows), shape(width, rows, dtype=BF16)
        keys = spread(sk)
        pack, cum_row, cum_col, lin_vt = call(
            state_kernel,
            (decay, lk, lv, sv),
            (),
            (shape(rows + 2 * width + PAD, width, dtype=BF16), row, shape(rows, width), flat16),
        )
        packs = spread(pack)
        lin_qt, qt, intra, top, total, summed = call(
            functools.partial(local_kernel, scale, step),
            (lq, lk, sq, sk),
            (lin_vt, cum_row, cum_col, pack),
            (flat16, flat16, flat, row, row, flat),
        )
        ring = (axis, cores, chips)
        keys = complete(keys, intra)
        probs, factor, sums = call(
            functools.partial(score_kernel, scale, step, *ring),
            (),
            (qt, top, total, *keys),
            (shape(len(keys) * rows, rows, dtype=BF16), row, row),
        )
        out = shape(rows, width, dtype=BF16)
        packs = complete(packs, factor)
        return call(
            functools.partial(finish_kernel, step, *ring),
            (),
            (lin_qt, intra, cum_row, summed, probs, factor, sums, *packs),
            (out, out),
            last=True,
        )

    outs = [
        one_head(
            *(x[:, head] for x in (lin_query, lin_key, lin_value)),
            log_decay[head : head + 1],
            *(x[:, head] for x in (soft_query, soft_key, soft_value)),
        )
        for head in range(heads)
    ]
    linear = jnp.stack([pair[0] for pair in outs], axis=1)
    softmax = jnp.stack([pair[1] for pair in outs], axis=1)
    return linear, softmax


def solution(mesh):
    block = P("ctx", "tp", None)
    return jax.shard_map(
        functools.partial(on_device, "ctx"),
        mesh=mesh,
        in_specs=(block, block, block, P("tp", "ctx"), block, block, block),
        out_specs=(block, block),
        check_vma=False,
    )
```

```python
import functools
import math

import jax
import jax.numpy as jnp
from jax import lax
from jax.experimental import pallas as pl
from jax.experimental.pallas import tpu as pltpu
from jax.sharding import PartitionSpec as P

NEG = -1e30
TINY = 1e-6
PAD = 16
KERNEL_VMEM = 16 * 2**20
F32 = jnp.float32
BF16 = jnp.bfloat16
VMEM = pltpu.VMEM


def dot(a, b):
    return lax.dot_general(a, b, (((1,), (0,)), ((), ())), preferred_element_type=F32)


def three_parts(x):
    high = x.astype(BF16)
    rest = x - high.astype(F32)
    middle = rest.astype(BF16)
    low = (rest - middle.astype(F32)).astype(BF16)
    return high, middle, low


def iota(shape, dim):
    return lax.broadcasted_iota(jnp.int32, shape, dim)


def select_rows(parts, rows, width):
    row = iota((rows, width), 0)
    out = jnp.zeros((rows, width), F32)
    for number, part in enumerate(parts):
        out = jnp.where(row == number, part.astype(F32), out)
    return out.astype(BF16)


def side_by_side(ref, rows, width):
    pieces = [ref[left : left + width, :] for left in range(0, rows, width)]
    return pieces[0] if len(pieces) == 1 else jnp.concatenate(pieces, axis=1)


def state_kernel(
    decay_ref, key_ref, value_ref, soft_value_ref, pack_ref, cum_row_ref, cum_col_ref, value_t_ref
):
    rows, width = key_ref.shape
    parts = select_rows(three_parts(decay_ref[...]), PAD, rows)
    upto = (iota((rows, rows), 0) <= iota((rows, rows), 1)).astype(F32).astype(BF16)
    cum_row = jnp.sum(dot(parts, upto), axis=0, keepdims=True)
    cum_row_ref[...] = cum_row
    cum_col = jnp.transpose(jnp.broadcast_to(cum_row, (width, rows)))
    cum_col_ref[...] = cum_col
    total = cum_col[rows - 1 :, :]
    decayed = (key_ref[...].astype(F32) * jnp.exp(total - cum_col)).astype(BF16)
    value_t = jnp.transpose(value_ref[...])
    value_t_ref[...] = value_t
    state_t = dot(value_t, decayed)
    high = state_t.astype(BF16)
    for left in range(0, rows, width):
        pack_ref[left : left + width, :] = jnp.transpose(soft_value_ref[left : left + width, :])
    pack_ref[rows : rows + width, :] = high
    pack_ref[rows + width : rows + 2 * width, :] = (state_t - high.astype(F32)).astype(BF16)
    pack_ref[rows + 2 * width :, :] = select_rows(three_parts(total), PAD, width)


def local_kernel(
    scale, step,
    lin_q_ref, lin_k_ref, q_ref, k_ref, lin_vt_ref, cum_row_ref, cum_col_ref, pack_ref,
    lin_qt_ref, qt_ref, intra_ref, top_ref, total_ref, summed_ref,
):
    rows, width = lin_q_ref.shape
    lin_qt_ref[...] = jnp.transpose(lin_q_ref[...])
    qt_ref[...] = jnp.transpose(q_ref[...])
    soft_vt = side_by_side(pack_ref, rows, width)
    keep = iota((step, step), 0) <= iota((step, step), 1)
    for start in range(0, rows, step):
        stop = start + step
        scores = dot(k_ref[:stop, :], qt_ref[:, start:stop])
        last = jnp.where(keep, scores[start:, :], NEG)
        scores = jnp.concatenate([scores[:start, :], last], axis=0) if start else last
        top = jnp.max(scores, axis=0, keepdims=True)
        probs = jnp.exp2((scores - top) * scale)
        top_ref[:, start:stop] = top
        total_ref[:, start:stop] = jnp.sum(probs, axis=0, keepdims=True)
        summed_ref[:, start:stop] = dot(soft_vt[:, :stop], probs.astype(BF16))

        scores = dot(lin_k_ref[:stop, :], lin_qt_ref[:, start:stop])
        cum_t = cum_row_ref[:, start:stop]
        cum_s = jnp.concatenate([cum_col_ref[:stop, :]] * (step // width), axis=1)
        diff = cum_t - cum_s
        last = jnp.where(keep, diff[start:, :], NEG)
        diff = jnp.concatenate([diff[:start, :], last], axis=0) if start else last
        weights = (scores * jnp.exp(diff)).astype(BF16)
        intra_ref[:, start:stop] = dot(lin_vt_ref[:, :stop], weights)


def block_numbers(axis, cores, chips):
    position = lax.axis_index(axis)
    if cores == 1:
        return position, [position - apart for apart in range(1, chips)]
    other = lax.rem(position, 2)
    partner = position + 1 - 2 * other
    numbers = [jnp.where(other == 1, position - 1, -1)]
    for apart in range(1, chips):
        numbers += [position - 2 * apart, partner - 2 * apart]
    return position, numbers


def by_chip(position, cores, count, body):
    pl.when(position >= cores)(lambda: body(count))
    pl.when(position < cores)(lambda: body(cores - 1))


def score_kernel(scale, step, axis, cores, chips, qt_ref, top_ref, total_ref, *refs):
    key_refs, (probs_ref, factor_ref, sum_ref) = refs[:-3], refs[-3:]
    rows = qt_ref.shape[1]
    position, numbers = block_numbers(axis, cores, chips)
    away = [jnp.where(number >= 0, 0.0, NEG) for number in numbers]

    def body(count):
        for start in range(0, rows, step):
            mine = slice(start, start + step)
            query = qt_ref[:, mine]
            old = top_ref[:, mine]
            scores = [dot(key_refs[i][...], query) for i in range(count)]
            top = old
            for score, off in zip(scores, away):
                top = jnp.maximum(top, jnp.max(score, axis=0, keepdims=True) + off)
            factor = jnp.exp2((old - top) * scale)
            total = total_ref[:, mine] * factor
            for number, (score, off) in enumerate(zip(scores, away)):
                probs = jnp.exp2((score - (top - off)) * scale)
                total = total + jnp.sum(probs, axis=0, keepdims=True)
                probs_ref[number * rows : (number + 1) * rows, mine] = probs.astype(BF16)
            factor_ref[:, mine] = factor
            sum_ref[:, mine] = total

    by_chip(position, cores, len(key_refs), body)


def finish_kernel(
    step, axis, cores, chips,
    lin_qt_ref, intra_ref, cum_row_ref, summed_ref, probs_ref, factor_ref, sum_ref, *refs,
):
    pack_refs, (linear_ref, softmax_ref) = refs[:-2], refs[-2:]
    width, rows = lin_qt_ref.shape
    position, numbers = block_numbers(axis, cores, chips)

    def body(count):
        totals, states = [], []
        for pack_ref in pack_refs[:count]:
            tail = pack_ref[rows + 2 * width :, :].astype(F32)
            totals.append(tail[0:1] + tail[1:2] + tail[2:3])
            states.append(
                pack_ref[rows : rows + width, :].astype(F32)
                + pack_ref[rows + width : rows + 2 * width, :].astype(F32)
            )
        carried = jnp.zeros((width, width), F32)
        for number, state in zip(numbers, states):
            between = jnp.where(number >= 0, 0.0, NEG)
            for other, total in zip(numbers, totals):
                between = between + jnp.where(other > number, 1.0, 0.0) * total
            carried = carried + jnp.exp(between) * state
        carried = carried.astype(BF16)
        values = [side_by_side(pack_ref, rows, width) for pack_ref in pack_refs[:count]]
        for start in range(0, rows, step):
            mine = slice(start, start + step)
            summed = summed_ref[:, mine] * factor_ref[:, mine]
            for number, value in enumerate(values):
                summed = summed + dot(value, probs_ref[number * rows : (number + 1) * rows, mine])
            softmax_ref[mine, :] = jnp.transpose(summed / sum_ref[:, mine]).astype(BF16)
            inter = dot(carried, lin_qt_ref[:, mine])
            raw = intra_ref[:, mine] + inter * jnp.exp(cum_row_ref[:, mine])
            square = jnp.sum(raw * raw, axis=0, keepdims=True) * (1.0 / width)
            linear_ref[mine, :] = jnp.transpose(raw * lax.rsqrt(square + TINY)).astype(BF16)

    by_chip(position, cores, len(pack_refs), body)


def keep_in_hbm(x):
    return pltpu.with_memory_space_constraint(x, pltpu.HBM)


def keep_in_vmem(x):
    return pltpu.with_memory_space_constraint(x, VMEM)


def kept_in_vmem(x):
    return VMEM(x.shape, x.dtype)


def call(body, given, operands, outs, last=False):
    size = sum(math.prod(x.shape) * x.dtype.itemsize for x in (*given, *operands, *outs))
    operands = [*map(keep_in_hbm, given), *map(keep_in_vmem, operands)]
    if not last:
        outs = [kept_in_vmem(x) for x in outs]
    return pl.pallas_call(
        body,
        out_shape=tuple(outs),
        in_specs=[pl.BlockSpec(memory_space=VMEM)] * len(operands),
        out_specs=tuple(pl.BlockSpec(memory_space=VMEM) for _ in outs),
        cost_estimate=pl.CostEstimate(flops=0, bytes_accessed=size, transcendentals=0),
        compiler_params=pltpu.CompilerParams(vmem_limit_bytes=KERNEL_VMEM),
    )(*operands)


def on_device(axis, lin_query, lin_key, lin_value, log_decay, soft_query, soft_key, soft_value):
    rows, heads, width = lin_query.shape
    count = lax.axis_size(axis)
    cores = 2 if count % 2 == 0 else 1
    chips = count // cores

    def across(x, apart):
        return lax.ppermute(x, axis, [(i, (i + apart * cores) % count) for i in range(count)])

    def swapped(x, after=None):
        if after is not None:
            x, _ = lax.optimization_barrier((x, after))
        return lax.ppermute(x, axis, [(i, i ^ 1) for i in range(count)])

    def spread(x):
        far = [across(x, apart) for apart in range(1, chips)]
        own = [swapped(x)] if cores == 2 else []
        return own, far

    def complete(of, after):
        own, far = of
        out = list(own)
        for block in far:
            out.append(block)
            if cores == 2:
                out.append(swapped(block, after))
        return out

    def one_head(lq, lk, lv, decay, sq, sk, sv):
        step = math.gcd(rows, 256)
        scale = math.log2(math.e) / math.sqrt(width)

        def shape(*dims, dtype=F32):
            return jax.ShapeDtypeStruct(dims, dtype)

        row, flat, flat16 = shape(1, rows), shape(width, rows), shape(width, rows, dtype=BF16)
        keys = spread(sk)
        pack, cum_row, cum_col, lin_vt = call(
            state_kernel,
            (decay, lk, lv, sv),
            (),
            (shape(rows + 2 * width + PAD, width, dtype=BF16), row, shape(rows, width), flat16),
        )
        packs = spread(pack)
        lin_qt, qt, intra, top, total, summed = call(
            functools.partial(local_kernel, scale, step),
            (lq, lk, sq, sk),
            (lin_vt, cum_row, cum_col, pack),
            (flat16, flat16, flat, row, row, flat),
        )
        ring = (axis, cores, chips)
        keys = complete(keys, intra)
        probs, factor, sums = call(
            functools.partial(score_kernel, scale, step, *ring),
            (),
            (qt, top, total, *keys),
            (shape(len(keys) * rows, rows, dtype=BF16), row, row),
        )
        out = shape(rows, width, dtype=BF16)
        packs = complete(packs, factor)
        return call(
            functools.partial(finish_kernel, step, *ring),
            (),
            (lin_qt, intra, cum_row, summed, probs, factor, sums, *packs),
            (out, out),
            last=True,
        )

    outs = [
        one_head(
            *(x[:, head] for x in (lin_query, lin_key, lin_value)),
            log_decay[head : head + 1],
            *(x[:, head] for x in (soft_query, soft_key, soft_value)),
        )
        for head in range(heads)
    ]
    linear = jnp.stack([pair[0] for pair in outs], axis=1)
    softmax = jnp.stack([pair[1] for pair in outs], axis=1)
    return linear, softmax


def solution(mesh):
    block = P("ctx", "tp", None)
    return jax.shard_map(
        functools.partial(on_device, "ctx"),
        mesh=mesh,
        in_specs=(block, block, block, P("tp", "ctx"), block, block, block),
        out_specs=(block, block),
        check_vma=False,
    )
```

```python
import functools
import math

import jax
import jax.numpy as jnp
from jax import lax
from jax.experimental import pallas as pl
from jax.experimental.pallas import tpu as pltpu
from jax.sharding import PartitionSpec as P

NEG = -1e30
TINY = 1e-6
PAD = 16
KERNEL_VMEM = 16 * 2**20
F32 = jnp.float32
BF16 = jnp.bfloat16
VMEM = pltpu.VMEM


def dot(a, b):
    return lax.dot_general(a, b, (((1,), (0,)), ((), ())), preferred_element_type=F32)


def three_parts(x):
    high = x.astype(BF16)
    rest = x - high.astype(F32)
    middle = rest.astype(BF16)
    low = (rest - middle.astype(F32)).astype(BF16)
    return high, middle, low


def iota(shape, dim):
    return lax.broadcasted_iota(jnp.int32, shape, dim)


def select_rows(parts, rows, width):
    row = iota((rows, width), 0)
    out = jnp.zeros((rows, width), F32)
    for number, part in enumerate(parts):
        out = jnp.where(row == number, part.astype(F32), out)
    return out.astype(BF16)


def side_by_side(ref, rows, width):
    pieces = [ref[left : left + width, :] for left in range(0, rows, width)]
    return pieces[0] if len(pieces) == 1 else jnp.concatenate(pieces, axis=1)


def state_kernel(
    decay_ref, key_ref, value_ref, soft_value_ref, pack_ref, cum_row_ref, cum_col_ref, value_t_ref
):
    rows, width = key_ref.shape
    parts = select_rows(three_parts(decay_ref[...]), PAD, rows)
    upto = (iota((rows, rows), 0) <= iota((rows, rows), 1)).astype(F32).astype(BF16)
    cum_row = jnp.sum(dot(parts, upto), axis=0, keepdims=True)
    cum_row_ref[...] = cum_row
    cum_col = jnp.transpose(jnp.broadcast_to(cum_row, (width, rows)))
    cum_col_ref[...] = cum_col
    total = cum_col[rows - 1 :, :]
    decayed = (key_ref[...].astype(F32) * jnp.exp(total - cum_col)).astype(BF16)
    value_t = jnp.transpose(value_ref[...])
    value_t_ref[...] = value_t
    state_t = dot(value_t, decayed)
    for left in range(0, rows, width):
        pack_ref[left : left + width, :] = jnp.transpose(soft_value_ref[left : left + width, :])
    pack_ref[rows : rows + width, :] = state_t.astype(BF16)
    pack_ref[rows + width :, :] = select_rows(three_parts(total), PAD, width)


def soft_kernel(scale, step, q_ref, k_ref, pack_ref, qt_ref, top_ref, total_ref, summed_ref):
    rows, width = q_ref.shape
    qt_ref[...] = jnp.transpose(q_ref[...])
    value_t = side_by_side(pack_ref, rows, width)
    keep = iota((step, step), 0) <= iota((step, step), 1)
    for start in range(0, rows, step):
        stop = start + step
        scores = dot(k_ref[:stop, :], qt_ref[:, start:stop])
        last = jnp.where(keep, scores[start:, :], NEG)
        scores = jnp.concatenate([scores[:start, :], last], axis=0) if start else last
        top = jnp.max(scores, axis=0, keepdims=True)
        probs = jnp.exp2((scores - top) * scale)
        top_ref[:, start:stop] = top
        total_ref[:, start:stop] = jnp.sum(probs, axis=0, keepdims=True)
        summed_ref[:, start:stop] = dot(value_t[:, :stop], probs.astype(BF16))


def linear_kernel(step, q_ref, k_ref, value_t_ref, cum_row_ref, cum_col_ref, qt_ref, intra_ref):
    rows, width = q_ref.shape
    qt_ref[...] = jnp.transpose(q_ref[...])
    keep = iota((step, step), 0) <= iota((step, step), 1)
    for start in range(0, rows, step):
        stop = start + step
        scores = dot(k_ref[:stop, :], qt_ref[:, start:stop])
        cum_t = cum_row_ref[:, start:stop]
        cum_s = jnp.concatenate([cum_col_ref[:stop, :]] * (step // width), axis=1)
        diff = cum_t - cum_s
        last = jnp.where(keep, diff[start:, :], NEG)
        diff = jnp.concatenate([diff[:start, :], last], axis=0) if start else last
        weights = (scores * jnp.exp(diff)).astype(BF16)
        intra_ref[:, start:stop] = dot(value_t_ref[:, :stop], weights)


def block_numbers(axis, cores, chips):
    position = lax.axis_index(axis)
    if cores == 1:
        return position, [position - apart for apart in range(1, chips)]
    other = lax.rem(position, 2)
    partner = position + 1 - 2 * other
    numbers = [jnp.where(other == 1, position - 1, -1)]
    for apart in range(1, chips):
        numbers += [position - 2 * apart, partner - 2 * apart]
    return position, numbers


def by_chip(position, cores, count, body):
    pl.when(position >= cores)(lambda: body(count))
    pl.when(position < cores)(lambda: body(cores - 1))


def score_kernel(scale, step, axis, cores, chips, qt_ref, top_ref, total_ref, *refs):
    key_refs, (probs_ref, factor_ref, sum_ref) = refs[:-3], refs[-3:]
    rows = qt_ref.shape[1]
    position, numbers = block_numbers(axis, cores, chips)
    away = [jnp.where(number >= 0, 0.0, NEG) for number in numbers]

    def body(count):
        for start in range(0, rows, step):
            mine = slice(start, start + step)
            query = qt_ref[:, mine]
            old = top_ref[:, mine]
            scores = [dot(key_refs[i][...], query) for i in range(count)]
            top = old
            for score, off in zip(scores, away):
                top = jnp.maximum(top, jnp.max(score, axis=0, keepdims=True) + off)
            factor = jnp.exp2((old - top) * scale)
            total = total_ref[:, mine] * factor
            for number, (score, off) in enumerate(zip(scores, away)):
                probs = jnp.exp2((score - (top - off)) * scale)
                total = total + jnp.sum(probs, axis=0, keepdims=True)
                probs_ref[number * rows : (number + 1) * rows, mine] = probs.astype(BF16)
            factor_ref[:, mine] = factor
            sum_ref[:, mine] = total

    by_chip(position, cores, len(key_refs), body)


def carried_state(numbers, pack_refs, rows, width):
    totals, states = [], []
    for pack_ref in pack_refs:
        tail = pack_ref[rows + width :, :].astype(F32)
        totals.append(tail[0:1] + tail[1:2] + tail[2:3])
        states.append(pack_ref[rows : rows + width, :].astype(F32))
    carried = jnp.zeros((width, width), F32)
    for number, state in zip(numbers, states):
        between = jnp.where(number >= 0, 0.0, NEG)
        for other, total in zip(numbers, totals):
            between = between + jnp.where(other > number, 1.0, 0.0) * total
        carried = carried + jnp.exp(between) * state
    return carried.astype(BF16)


def weighted_values(pack_refs, places, probs_ref, mine, rows, width):
    out = None
    for place, pack_ref in zip(places, pack_refs):
        value_t = side_by_side(pack_ref, rows, width)
        term = dot(value_t, probs_ref[place * rows : (place + 1) * rows, mine])
        out = term if out is None else out + term
    return out


def write_out(step, numbers, places, pack_refs, linear_packs, refs, outs, buffers, sems):
    lin_qt_ref, intra_ref, cum_row_ref, summed_ref, factor_ref, sum_ref, probs_ref = refs
    width, rows = lin_qt_ref.shape
    linear_buffer, softmax_buffer = buffers
    softmax_copy, linear_copy = (
        pltpu.make_async_copy(buffer, out, sems.at[place])
        for place, (buffer, out) in enumerate(((softmax_buffer, outs[1]), (linear_buffer, outs[0])))
    )
    for start in range(0, rows, step):
        mine = slice(start, start + step)
        summed = summed_ref[:, mine]
        if factor_ref is not None:
            summed = summed * factor_ref[:, mine]
        more = weighted_values(pack_refs, places, probs_ref, mine, rows, width)
        summed = summed if more is None else summed + more
        softmax_buffer[mine, :] = jnp.transpose((summed / sum_ref[:, mine]).astype(BF16))
    softmax_copy.start()
    carried = carried_state(numbers, linear_packs, rows, width)
    for start in range(0, rows, step):
        mine = slice(start, start + step)
        inter = dot(carried, lin_qt_ref[:, mine])
        raw = intra_ref[:, mine] + inter * jnp.exp(cum_row_ref[:, mine])
        square = jnp.sum(raw * raw, axis=0, keepdims=True) * (1.0 / width)
        linear_buffer[mine, :] = jnp.transpose((raw * lax.rsqrt(square + TINY)).astype(BF16))
    linear_copy.start()
    softmax_copy.wait()
    linear_copy.wait()


def early_kernel(step, axis, cores, chips, places, *refs):
    head, refs = refs[:7], refs[7:]
    packs, (linear_ref, softmax_ref, sofar_ref, *scratch) = refs[: len(places)], refs[len(places) :]
    lin_qt_ref, intra_ref, cum_row_ref, summed_ref, factor_ref, sum_ref, probs_ref = head
    width, rows = lin_qt_ref.shape
    position, numbers = block_numbers(axis, cores, chips)

    @pl.when(position >= cores)
    def _():
        for start in range(0, rows, step):
            mine = slice(start, start + step)
            sofar_ref[:, mine] = summed_ref[:, mine] * factor_ref[:, mine] + weighted_values(
                packs, places, probs_ref, mine, rows, width
            )

    @pl.when(position < cores)
    def _():
        own = cores - 1
        write_out(
            step, numbers[:own], places[:own], packs[:own], packs[:own], head,
            (linear_ref, softmax_ref), scratch[:2], scratch[2],
        )


def late_kernel(step, axis, cores, chips, early, late, *refs):
    lin_qt_ref, intra_ref, cum_row_ref, sofar_ref, sum_ref, probs_ref = refs[:6]
    count = len(early) + len(late)
    packs, (_, _, linear_ref, softmax_ref, *scratch) = refs[6 : 6 + count], refs[6 + count :]
    position, numbers = block_numbers(axis, cores, chips)

    @pl.when(position >= cores)
    def _():
        write_out(
            step, numbers, late, [packs[place] for place in late], packs,
            (lin_qt_ref, intra_ref, cum_row_ref, sofar_ref, None, sum_ref, probs_ref),
            (linear_ref, softmax_ref), scratch[:2], scratch[2],
        )


def keep_in_hbm(x):
    return pltpu.with_memory_space_constraint(x, pltpu.HBM)


def keep_in_vmem(x):
    return pltpu.with_memory_space_constraint(x, VMEM)


def kept_in_vmem(x):
    return VMEM(x.shape, x.dtype)


def kept_in_hbm(x):
    return pltpu.HBM(x.shape, x.dtype)


def call(body, given, operands, outs, written=(), resumed=()):
    size = sum(math.prod(x.shape) * x.dtype.itemsize for x in (*given, *operands, *outs))
    inside, outside = pl.BlockSpec(memory_space=VMEM), pl.BlockSpec(memory_space=pl.ANY)
    first = len(given) + len(operands)
    scratch = [VMEM(x.shape, x.dtype) for x in written]
    return pl.pallas_call(
        body,
        out_shape=(*map(kept_in_hbm, written), *map(kept_in_vmem, outs)),
        in_specs=[inside] * first + [outside] * len(resumed),
        out_specs=(*[outside] * len(written), *[inside] * len(outs)),
        scratch_shapes=[*scratch, pltpu.SemaphoreType.DMA((2,))] if written else [],
        input_output_aliases={first + place: place for place in range(len(resumed))},
        cost_estimate=pl.CostEstimate(flops=0, bytes_accessed=size, transcendentals=0),
        compiler_params=pltpu.CompilerParams(vmem_limit_bytes=KERNEL_VMEM),
    )(*map(keep_in_hbm, given), *map(keep_in_vmem, operands), *map(keep_in_hbm, resumed))


def on_device(axis, lin_query, lin_key, lin_value, log_decay, soft_query, soft_key, soft_value):
    rows, heads, width = lin_query.shape
    count = lax.axis_size(axis)
    cores = 2 if count % 2 == 0 else 1
    chips = count // cores

    def across(x, apart):
        return lax.ppermute(x, axis, [(i, (i + apart * cores) % count) for i in range(count)])

    def swapped(x, after=None):
        if after is not None:
            x, _ = lax.optimization_barrier((x, after))
        return lax.ppermute(x, axis, [(i, i ^ 1) for i in range(count)])

    def spread(x):
        far = [across(x, apart) for apart in range(1, chips)]
        own = [swapped(x)] if cores == 2 else []
        return own, far

    def complete(of, after):
        own, far = of
        out = list(own)
        for block in far:
            out.append(block)
            if cores == 2:
                out.append(swapped(block, after))
        return out

    def one_head(lq, lk, lv, decay, sq, sk, sv):
        step = math.gcd(rows, 256)
        scale = math.log2(math.e) / math.sqrt(width)

        def shape(*dims, dtype=F32):
            return jax.ShapeDtypeStruct(dims, dtype)

        row, flat, flat16 = shape(1, rows), shape(width, rows), shape(width, rows, dtype=BF16)
        keys = spread(sk)
        pack, cum_row, cum_col, lin_vt = call(
            state_kernel,
            (decay, lk, lv, sv),
            (),
            (shape(rows + width + PAD, width, dtype=BF16), row, shape(rows, width), flat16),
        )
        packs = spread(pack)
        qt, top, total, summed = call(
            functools.partial(soft_kernel, scale, step), (sq, sk), (pack,), (flat16, row, row, flat)
        )
        ring = (axis, cores, chips)
        keys = complete(keys, summed)
        (lq, lk), _ = lax.optimization_barrier(((lq, lk), keys[cores - 1 :: cores]))
        lin_qt, intra = call(
            functools.partial(linear_kernel, step), (lq, lk), (lin_vt, cum_row, cum_col), (flat16, flat)
        )
        top, _ = lax.optimization_barrier((top, intra))
        probs, factor, sums = call(
            functools.partial(score_kernel, scale, step, *ring),
            (),
            (qt, top, total, *keys),
            (shape(len(keys) * rows, rows, dtype=BF16), row, row),
        )
        out = shape(rows, width, dtype=BF16)
        packs = complete(packs, factor)
        late = tuple(range(cores, len(packs), cores)) if cores == 2 else ()
        early = tuple(place for place in range(len(packs)) if place not in late)
        *began, sofar = call(
            functools.partial(early_kernel, step, *ring, early),
            (),
            (lin_qt, intra, cum_row, summed, factor, sums, probs, *(packs[place] for place in early)),
            (flat,),
            written=(out, out),
        )
        return call(
            functools.partial(late_kernel, step, *ring, early, late),
            (),
            (lin_qt, intra, cum_row, sofar, sums, probs, *packs),
            (),
            written=(out, out),
            resumed=began,
        )

    outs = [
        one_head(
            *(x[:, head] for x in (lin_query, lin_key, lin_value)),
            log_decay[head : head + 1],
            *(x[:, head] for x in (soft_query, soft_key, soft_value)),
        )
        for head in range(heads)
    ]
    linear = jnp.stack([pair[0] for pair in outs], axis=1)
    softmax = jnp.stack([pair[1] for pair in outs], axis=1)
    return linear, softmax


def solution(mesh):
    block = P("ctx", "tp", None)
    return jax.shard_map(
        functools.partial(on_device, "ctx"),
        mesh=mesh,
        in_specs=(block, block, block, P("tp", "ctx"), block, block, block),
        out_specs=(block, block),
        check_vma=False,
    )
```

```python
import functools
import math

import jax
import jax.numpy as jnp
from jax import lax
from jax.experimental import pallas as pl
from jax.experimental.pallas import tpu as pltpu
from jax.sharding import PartitionSpec as P

NEG = -1e30
TINY = 1e-6
PAD = 16
KERNEL_VMEM = 16 * 2**20
F32 = jnp.float32
BF16 = jnp.bfloat16
VMEM = pltpu.VMEM


def dot(a, b):
    return lax.dot_general(a, b, (((1,), (0,)), ((), ())), preferred_element_type=F32)


def three_parts(x):
    high = x.astype(BF16)
    rest = x - high.astype(F32)
    middle = rest.astype(BF16)
    low = (rest - middle.astype(F32)).astype(BF16)
    return high, middle, low


def iota(shape, dim):
    return lax.broadcasted_iota(jnp.int32, shape, dim)


def select_rows(parts, rows, width):
    row = iota((rows, width), 0)
    out = jnp.zeros((rows, width), F32)
    for number, part in enumerate(parts):
        out = jnp.where(row == number, part.astype(F32), out)
    return out.astype(BF16)


def side_by_side(ref, rows, width):
    pieces = [ref[left : left + width, :] for left in range(0, rows, width)]
    return pieces[0] if len(pieces) == 1 else jnp.concatenate(pieces, axis=1)


def state_kernel(
    decay_hbm, key_hbm, value_hbm, soft_value_hbm, query_hbm, soft_query_hbm, soft_key_hbm,
    pack_ref, cum_row_ref, cum_col_ref, value_t_ref, key_ref, query_ref, soft_query_ref, soft_key_ref,
    decay_ref, value_ref, soft_value_ref, sems,
):
    copies = [
        pltpu.make_async_copy(source, target, sems.at[place])
        for place, (source, target) in enumerate(
            (
                (decay_hbm, decay_ref),
                (key_hbm, key_ref),
                (value_hbm, value_ref),
                (soft_value_hbm, soft_value_ref),
                (soft_query_hbm, soft_query_ref),
                (soft_key_hbm, soft_key_ref),
                (query_hbm, query_ref),
            )
        )
    ]
    for copy in copies:
        copy.start()
    rows, width = key_ref.shape
    upto = (iota((rows, rows), 0) <= iota((rows, rows), 1)).astype(F32).astype(BF16)
    copies[0].wait()
    parts = select_rows(three_parts(decay_ref[...]), PAD, rows)
    cum_row = jnp.sum(dot(parts, upto), axis=0, keepdims=True)
    cum_row_ref[...] = cum_row
    cum_col = jnp.transpose(jnp.broadcast_to(cum_row, (width, rows)))
    cum_col_ref[...] = cum_col
    total = cum_col[rows - 1 :, :]
    for copy in copies[1:4]:
        copy.wait()
    decayed = (key_ref[...].astype(F32) * jnp.exp(total - cum_col)).astype(BF16)
    value_t = jnp.transpose(value_ref[...])
    value_t_ref[...] = value_t
    state_t = dot(value_t, decayed)
    for left in range(0, rows, width):
        pack_ref[left : left + width, :] = jnp.transpose(soft_value_ref[left : left + width, :])
    pack_ref[rows : rows + width, :] = state_t.astype(BF16)
    pack_ref[rows + width :, :] = select_rows(three_parts(total), PAD, width)
    for copy in copies[4:]:
        copy.wait()


def soft_kernel(scale, step, q_ref, k_ref, pack_ref, qt_ref, top_ref, total_ref, summed_ref):
    rows, width = q_ref.shape
    qt_ref[...] = jnp.transpose(q_ref[...])
    value_t = side_by_side(pack_ref, rows, width)
    keep = iota((step, step), 0) <= iota((step, step), 1)
    for start in range(0, rows, step):
        stop = start + step
        scores = dot(k_ref[:stop, :], qt_ref[:, start:stop])
        last = jnp.where(keep, scores[start:, :], NEG)
        scores = jnp.concatenate([scores[:start, :], last], axis=0) if start else last
        top = jnp.max(scores, axis=0, keepdims=True)
        probs = jnp.exp2((scores - top) * scale)
        top_ref[:, start:stop] = top
        total_ref[:, start:stop] = jnp.sum(probs, axis=0, keepdims=True)
        summed_ref[:, start:stop] = dot(value_t[:, :stop], probs.astype(BF16))


def linear_kernel(step, q_ref, k_ref, value_t_ref, cum_row_ref, cum_col_ref, qt_ref, intra_ref):
    rows, width = q_ref.shape
    qt_ref[...] = jnp.transpose(q_ref[...])
    keep = iota((step, step), 0) <= iota((step, step), 1)
    for start in range(0, rows, step):
        stop = start + step
        scores = dot(k_ref[:stop, :], qt_ref[:, start:stop])
        cum_t = cum_row_ref[:, start:stop]
        cum_s = jnp.concatenate([cum_col_ref[:stop, :]] * (step // width), axis=1)
        diff = cum_t - cum_s
        last = jnp.where(keep, diff[start:, :], NEG)
        diff = jnp.concatenate([diff[:start, :], last], axis=0) if start else last
        weights = (scores * jnp.exp(diff)).astype(BF16)
        intra_ref[:, start:stop] = dot(value_t_ref[:, :stop], weights)


def block_numbers(axis, cores, chips):
    position = lax.axis_index(axis)
    if cores == 1:
        return position, [position - apart for apart in range(1, chips)]
    other = lax.rem(position, 2)
    partner = position + 1 - 2 * other
    numbers = [jnp.where(other == 1, position - 1, -1)]
    for apart in range(1, chips):
        numbers += [position - 2 * apart, partner - 2 * apart]
    return position, numbers


def by_chip(position, cores, count, body):
    pl.when(position >= cores)(lambda: body(count))
    pl.when(position < cores)(lambda: body(cores - 1))


def score_kernel(scale, step, axis, cores, chips, qt_ref, top_ref, total_ref, *refs):
    key_refs, (probs_ref, factor_ref, sum_ref) = refs[:-3], refs[-3:]
    rows = qt_ref.shape[1]
    position, numbers = block_numbers(axis, cores, chips)
    away = [jnp.where(number >= 0, 0.0, NEG) for number in numbers]

    def body(count):
        for start in range(0, rows, step):
            mine = slice(start, start + step)
            query = qt_ref[:, mine]
            old = top_ref[:, mine]
            scores = [dot(key_refs[i][...], query) for i in range(count)]
            top = old
            for score, off in zip(scores, away):
                top = jnp.maximum(top, jnp.max(score, axis=0, keepdims=True) + off)
            factor = jnp.exp2((old - top) * scale)
            total = total_ref[:, mine] * factor
            for number, (score, off) in enumerate(zip(scores, away)):
                probs = jnp.exp2((score - (top - off)) * scale)
                total = total + jnp.sum(probs, axis=0, keepdims=True)
                probs_ref[number * rows : (number + 1) * rows, mine] = probs.astype(BF16)
            factor_ref[:, mine] = factor
            sum_ref[:, mine] = total

    by_chip(position, cores, len(key_refs), body)


def carried_state(numbers, pack_refs, rows, width):
    totals, states = [], []
    for pack_ref in pack_refs:
        tail = pack_ref[rows + width :, :].astype(F32)
        totals.append(tail[0:1] + tail[1:2] + tail[2:3])
        states.append(pack_ref[rows : rows + width, :].astype(F32))
    carried = jnp.zeros((width, width), F32)
    for number, state in zip(numbers, states):
        between = jnp.where(number >= 0, 0.0, NEG)
        for other, total in zip(numbers, totals):
            between = between + jnp.where(other > number, 1.0, 0.0) * total
        carried = carried + jnp.exp(between) * state
    return carried.astype(BF16)


def weighted_values(pack_refs, places, probs_ref, mine, rows, width):
    out = None
    for place, pack_ref in zip(places, pack_refs):
        value_t = side_by_side(pack_ref, rows, width)
        term = dot(value_t, probs_ref[place * rows : (place + 1) * rows, mine])
        out = term if out is None else out + term
    return out


def write_out(step, numbers, places, pack_refs, linear_packs, refs, outs, buffers, sems):
    lin_qt_ref, intra_ref, cum_row_ref, summed_ref, factor_ref, sum_ref, probs_ref = refs
    width, rows = lin_qt_ref.shape
    linear_buffer, softmax_buffer = buffers
    softmax_copy, linear_copy = (
        pltpu.make_async_copy(buffer, out, sems.at[place])
        for place, (buffer, out) in enumerate(((softmax_buffer, outs[1]), (linear_buffer, outs[0])))
    )
    for start in range(0, rows, step):
        mine = slice(start, start + step)
        summed = summed_ref[:, mine]
        if factor_ref is not None:
            summed = summed * factor_ref[:, mine]
        more = weighted_values(pack_refs, places, probs_ref, mine, rows, width)
        summed = summed if more is None else summed + more
        softmax_buffer[mine, :] = jnp.transpose((summed / sum_ref[:, mine]).astype(BF16))
    softmax_copy.start()
    carried = carried_state(numbers, linear_packs, rows, width)
    for start in range(0, rows, step):
        mine = slice(start, start + step)
        inter = dot(carried, lin_qt_ref[:, mine])
        raw = intra_ref[:, mine] + inter * jnp.exp(cum_row_ref[:, mine])
        square = jnp.sum(raw * raw, axis=0, keepdims=True) * (1.0 / width)
        linear_buffer[mine, :] = jnp.transpose((raw * lax.rsqrt(square + TINY)).astype(BF16))
    linear_copy.start()
    softmax_copy.wait()
    linear_copy.wait()


def early_kernel(step, axis, cores, chips, places, *refs):
    head, refs = refs[:7], refs[7:]
    packs, (linear_ref, softmax_ref, sofar_ref, *scratch) = refs[: len(places)], refs[len(places) :]
    lin_qt_ref, intra_ref, cum_row_ref, summed_ref, factor_ref, sum_ref, probs_ref = head
    width, rows = lin_qt_ref.shape
    position, numbers = block_numbers(axis, cores, chips)

    @pl.when(position >= cores)
    def _():
        for start in range(0, rows, step):
            mine = slice(start, start + step)
            sofar_ref[:, mine] = summed_ref[:, mine] * factor_ref[:, mine] + weighted_values(
                packs, places, probs_ref, mine, rows, width
            )

    @pl.when(position < cores)
    def _():
        own = cores - 1
        write_out(
            step, numbers[:own], places[:own], packs[:own], packs[:own], head,
            (linear_ref, softmax_ref), scratch[:2], scratch[2],
        )


def late_kernel(step, axis, cores, chips, early, late, *refs):
    refs = refs[2:]
    lin_qt_ref, intra_ref, cum_row_ref, sofar_ref, sum_ref, probs_ref = refs[:6]
    count = len(early) + len(late)
    packs, (linear_ref, softmax_ref, *scratch) = refs[6 : 6 + count], refs[6 + count :]
    position, numbers = block_numbers(axis, cores, chips)

    @pl.when(position >= cores)
    def _():
        write_out(
            step, numbers, late, [packs[place] for place in late], packs,
            (lin_qt_ref, intra_ref, cum_row_ref, sofar_ref, None, sum_ref, probs_ref),
            (linear_ref, softmax_ref), scratch[:2], scratch[2],
        )


def keep_in_hbm(x):
    return pltpu.with_memory_space_constraint(x, pltpu.HBM)


def keep_in_vmem(x):
    return pltpu.with_memory_space_constraint(x, VMEM)


def kept_in_vmem(x):
    return VMEM(x.shape, x.dtype)


def kept_in_hbm(x):
    return pltpu.HBM(x.shape, x.dtype)


def call(body, operands, outs, given=(), written=(), resumed=(), scratch=()):
    size = sum(math.prod(x.shape) * x.dtype.itemsize for x in (*given, *operands, *outs))
    inside, outside = pl.BlockSpec(memory_space=VMEM), pl.BlockSpec(memory_space=pl.ANY)
    hbm = (*given, *resumed)
    scratch = [VMEM(x.shape, x.dtype) for x in (*scratch, *written)]
    moved = len(given) + len(written)
    return pl.pallas_call(
        body,
        out_shape=(*map(kept_in_hbm, written), *map(kept_in_vmem, outs)),
        in_specs=[outside] * len(hbm) + [inside] * len(operands),
        out_specs=(*[outside] * len(written), *[inside] * len(outs)),
        scratch_shapes=[*scratch, pltpu.SemaphoreType.DMA((moved,))] if moved else [],
        input_output_aliases={place: place for place in range(len(resumed))},
        cost_estimate=pl.CostEstimate(flops=0, bytes_accessed=size, transcendentals=0),
        compiler_params=pltpu.CompilerParams(vmem_limit_bytes=KERNEL_VMEM),
    )(*map(keep_in_hbm, hbm), *map(keep_in_vmem, operands))


def on_device(axis, lin_query, lin_key, lin_value, log_decay, soft_query, soft_key, soft_value):
    rows, heads, width = lin_query.shape
    count = lax.axis_size(axis)
    cores = 2 if count % 2 == 0 else 1
    chips = count // cores

    def across(x, apart):
        return lax.ppermute(x, axis, [(i, (i + apart * cores) % count) for i in range(count)])

    def swapped(x, after=None):
        if after is not None:
            x, _ = lax.optimization_barrier((x, after))
        return lax.ppermute(x, axis, [(i, i ^ 1) for i in range(count)])

    def spread(x):
        far = [across(x, apart) for apart in range(1, chips)]
        own = [swapped(x)] if cores == 2 else []
        return own, far

    def complete(of, after):
        own, far = of
        out = list(own)
        for block in far:
            out.append(block)
            if cores == 2:
                out.append(swapped(block, after))
        return out

    def one_head(lq, lk, lv, decay, sq, sk, sv):
        step = math.gcd(rows, 256)
        scale = math.log2(math.e) / math.sqrt(width)
        ring = (axis, cores, chips)

        def shape(*dims, dtype=F32):
            return jax.ShapeDtypeStruct(dims, dtype)

        row, flat, flat16 = shape(1, rows), shape(width, rows), shape(width, rows, dtype=BF16)
        block = shape(rows, width, dtype=BF16)
        keys = spread(sk)
        pack, cum_row, cum_col, lin_vt, lk, lq, sq, sk = call(
            state_kernel,
            (),
            (
                shape(rows + width + PAD, width, dtype=BF16), row, shape(rows, width), flat16,
                block, block, block, block,
            ),
            given=(decay, lk, lv, sv, lq, sq, sk),
            scratch=(row, block, block),
        )
        qt, top, total, summed = call(
            functools.partial(soft_kernel, scale, step), (sq, sk, pack), (flat16, row, row, flat)
        )
        (pack, lin_vt), _ = lax.optimization_barrier(((pack, lin_vt), summed))
        packs = spread(pack)
        keys = complete(keys, summed)
        (lq, lk), _ = lax.optimization_barrier(((lq, lk), keys[cores - 1 :: cores]))
        lin_qt, intra = call(
            functools.partial(linear_kernel, step), (lq, lk, lin_vt, cum_row, cum_col), (flat16, flat)
        )
        top, _ = lax.optimization_barrier((top, intra))
        probs, factor, sums = call(
            functools.partial(score_kernel, scale, step, *ring),
            (qt, top, total, *keys),
            (shape(len(keys) * rows, rows, dtype=BF16), row, row),
        )
        packs = complete(packs, factor)
        late = tuple(range(cores, len(packs), cores)) if cores == 2 else ()
        early = tuple(place for place in range(len(packs)) if place not in late)
        *began, sofar = call(
            functools.partial(early_kernel, step, *ring, early),
            (lin_qt, intra, cum_row, summed, factor, sums, probs, *(packs[place] for place in early)),
            (flat,),
            written=(block, block),
        )
        return call(
            functools.partial(late_kernel, step, *ring, early, late),
            (lin_qt, intra, cum_row, sofar, sums, probs, *packs),
            (),
            written=(block, block),
            resumed=began,
        )

    outs = [
        one_head(
            *(x[:, head] for x in (lin_query, lin_key, lin_value)),
            log_decay[head : head + 1],
            *(x[:, head] for x in (soft_query, soft_key, soft_value)),
        )
        for head in range(heads)
    ]
    linear = jnp.stack([pair[0] for pair in outs], axis=1)
    softmax = jnp.stack([pair[1] for pair in outs], axis=1)
    return linear, softmax


def solution(mesh):
    block = P("ctx", "tp", None)
    return jax.shard_map(
        functools.partial(on_device, "ctx"),
        mesh=mesh,
        in_specs=(block, block, block, P("tp", "ctx"), block, block, block),
        out_specs=(block, block),
        check_vma=False,
    )
```

```python
import functools
import math

import jax
import jax.numpy as jnp
from jax import lax
from jax.experimental import pallas as pl
from jax.experimental.pallas import tpu as pltpu
from jax.sharding import PartitionSpec as P

NEG = -1e30
TINY = 1e-6
PAD = 16
KERNEL_VMEM = 16 * 2**20
F32 = jnp.float32
BF16 = jnp.bfloat16
VMEM = pltpu.VMEM


def dot(a, b):
    return lax.dot_general(a, b, (((1,), (0,)), ((), ())), preferred_element_type=F32)


def three_parts(x):
    high = x.astype(BF16)
    rest = x - high.astype(F32)
    middle = rest.astype(BF16)
    low = (rest - middle.astype(F32)).astype(BF16)
    return high, middle, low


def iota(shape, dim):
    return lax.broadcasted_iota(jnp.int32, shape, dim)


def select_rows(parts, rows, width):
    row = iota((rows, width), 0)
    out = jnp.zeros((rows, width), F32)
    for number, part in enumerate(parts):
        out = jnp.where(row == number, part.astype(F32), out)
    return out.astype(BF16)


def side_by_side(ref, rows, width):
    pieces = [ref[left : left + width, :] for left in range(0, rows, width)]
    return pieces[0] if len(pieces) == 1 else jnp.concatenate(pieces, axis=1)


def state_kernel(
    decay_hbm, key_hbm, value_hbm, soft_value_hbm, query_hbm, soft_query_hbm, soft_key_hbm,
    pack_ref, cum_row_ref, cum_col_ref, value_t_ref, key_ref, query_ref, soft_query_ref, soft_key_ref,
    decay_ref, value_ref, soft_value_ref, sems,
):
    rows, width = key_ref.shape
    copies = [
        pltpu.make_async_copy(source, target, sems.at[place])
        for place, (source, target) in enumerate(
            (
                (decay_hbm, decay_ref),
                (key_hbm, key_ref),
                (value_hbm, value_ref),
                (soft_value_hbm, soft_value_ref),
                (soft_query_hbm, soft_query_ref),
                (soft_key_hbm, soft_key_ref),
                (query_hbm, query_ref),
            )
        )
    ]
    for copy in copies:
        copy.start()
    upto = (iota((rows, rows), 0) <= iota((rows, rows), 1)).astype(F32).astype(BF16)
    copies[0].wait()
    parts = select_rows(three_parts(decay_ref[...]), PAD, rows)
    cum_row = jnp.sum(dot(parts, upto), axis=0, keepdims=True)
    cum_row_ref[...] = cum_row
    cum_col = jnp.transpose(jnp.broadcast_to(cum_row, (width, rows)))
    cum_col_ref[...] = cum_col
    total = cum_col[rows - 1 :, :]
    for copy in copies[1:4]:
        copy.wait()
    decayed = (key_ref[...].astype(F32) * jnp.exp(total - cum_col)).astype(BF16)
    value_t = jnp.transpose(value_ref[...])
    value_t_ref[...] = value_t
    pack_ref[rows : rows + width, :] = dot(value_t, decayed).astype(BF16)
    pack_ref[rows + width :, :] = select_rows(three_parts(total), PAD, width)
    for left in range(0, rows, width):
        pack_ref[left : left + width, :] = jnp.transpose(soft_value_ref[left : left + width, :])
    for copy in copies[4:]:
        copy.wait()


def soft_kernel(scale, step, q_ref, k_ref, pack_ref, qt_ref, top_ref, total_ref, summed_ref):
    rows, width = q_ref.shape
    qt_ref[...] = jnp.transpose(q_ref[...])
    value_t = side_by_side(pack_ref, rows, width)
    keep = iota((step, step), 0) <= iota((step, step), 1)
    for start in range(0, rows, step):
        stop = start + step
        scores = dot(k_ref[:stop, :], qt_ref[:, start:stop])
        last = jnp.where(keep, scores[start:, :], NEG)
        scores = jnp.concatenate([scores[:start, :], last], axis=0) if start else last
        top = jnp.max(scores, axis=0, keepdims=True)
        probs = jnp.exp2((scores - top) * scale)
        top_ref[:, start:stop] = top
        total_ref[:, start:stop] = jnp.sum(probs, axis=0, keepdims=True)
        summed_ref[:, start:stop] = dot(value_t[:, :stop], probs.astype(BF16))


def linear_kernel(step, q_ref, k_ref, value_t_ref, cum_row_ref, cum_col_ref, qt_ref, intra_ref):
    rows, width = q_ref.shape
    qt_ref[...] = jnp.transpose(q_ref[...])
    keep = iota((step, step), 0) <= iota((step, step), 1)
    for start in range(0, rows, step):
        stop = start + step
        scores = dot(k_ref[:stop, :], qt_ref[:, start:stop])
        cum_t = cum_row_ref[:, start:stop]
        cum_s = jnp.concatenate([cum_col_ref[:stop, :]] * (step // width), axis=1)
        diff = cum_t - cum_s
        last = jnp.where(keep, diff[start:, :], NEG)
        diff = jnp.concatenate([diff[:start, :], last], axis=0) if start else last
        weights = (scores * jnp.exp(diff)).astype(BF16)
        intra_ref[:, start:stop] = dot(value_t_ref[:, :stop], weights)


def block_numbers(axis, cores, chips):
    position = lax.axis_index(axis)
    if cores == 1:
        return position, [position - apart for apart in range(1, chips)]
    other = lax.rem(position, 2)
    partner = position + 1 - 2 * other
    numbers = [jnp.where(other == 1, position - 1, -1)]
    for apart in range(1, chips):
        numbers += [position - 2 * apart, partner - 2 * apart]
    return position, numbers


def normalized(raw):
    square = jnp.sum(raw * raw, axis=0, keepdims=True) * (1.0 / raw.shape[0])
    return jnp.transpose((raw * lax.rsqrt(square + TINY)).astype(BF16))


def put_linear(step, carried, qt_ref, intra_ref, cum_row_ref, buffer):
    for start in range(0, qt_ref.shape[1], step):
        mine = slice(start, start + step)
        inter = dot(carried, qt_ref[:, mine])
        buffer[mine, :] = normalized(intra_ref[:, mine] + inter * jnp.exp(cum_row_ref[:, mine]))


def score_kernel(scale, step, axis, cores, chips, *refs):
    qt_ref, top_ref, total_ref, summed_ref, lin_qt_ref, intra_ref, cum_row_ref = refs[:7]
    near_packs, refs = refs[7 : 6 + cores], refs[6 + cores :]
    *key_refs, linear_ref, softmax_ref, probs_ref, factor_ref, sum_ref = refs[:-3]
    linear_buffer, softmax_buffer, sems = refs[-3:]
    width, rows = qt_ref.shape
    position, numbers = block_numbers(axis, cores, chips)
    away = [jnp.where(number >= 0, 0.0, NEG) for number in numbers]

    def weights(mine, keys):
        query = qt_ref[:, mine]
        old = top_ref[:, mine]
        scores = [dot(key, query) for key in keys]
        top = old
        for score, off in zip(scores, away):
            top = jnp.maximum(top, jnp.max(score, axis=0, keepdims=True) + off)
        factor = jnp.exp2((old - top) * scale)
        total = total_ref[:, mine] * factor
        probs = []
        for score, off in zip(scores, away):
            prob = jnp.exp2((score - (top - off)) * scale)
            total = total + jnp.sum(prob, axis=0, keepdims=True)
            probs.append(prob.astype(BF16))
        return probs, factor, total

    keys = [key_ref[...] for key_ref in key_refs]

    @pl.when(position >= cores)
    def _():
        for start in range(0, rows, step):
            mine = slice(start, start + step)
            probs, factor, total = weights(mine, keys)
            for place, prob in enumerate(probs):
                probs_ref[place * rows : (place + 1) * rows, mine] = prob
            factor_ref[:, mine] = factor
            sum_ref[:, mine] = total

    @pl.when(position < cores)
    def _():
        linear_copy = pltpu.make_async_copy(linear_buffer, linear_ref, sems.at[0])
        softmax_copy = pltpu.make_async_copy(softmax_buffer, softmax_ref, sems.at[1])
        for start in range(0, rows, step):
            mine = slice(start, start + step)
            probs, factor, total = weights(mine, keys[: cores - 1])
            summed = summed_ref[:, mine] * factor
            for pack_ref, prob in zip(near_packs, probs):
                summed = summed + dot(side_by_side(pack_ref, rows, width), prob)
            softmax_buffer[mine, :] = jnp.transpose((summed / total).astype(BF16))
        softmax_copy.start()
        carried = jnp.zeros((width, width), F32)
        for pack_ref in near_packs:
            carried = jnp.where(position == 1, pack_ref[rows : rows + width, :].astype(F32), carried)
        put_linear(step, carried.astype(BF16), lin_qt_ref, intra_ref, cum_row_ref, linear_buffer)
        linear_copy.start()
        softmax_copy.wait()
        linear_copy.wait()


def weighted_values(refs, places, probs_ref, mine, rows, width):
    out = None
    for place, ref in zip(places, refs):
        term = dot(side_by_side(ref, rows, width), probs_ref[place * rows : (place + 1) * rows, mine])
        out = term if out is None else out + term
    return out


def early_kernel(step, axis, cores, places, *refs):
    summed_ref, factor_ref, probs_ref, *packs, sofar_ref = refs
    width, rows = summed_ref.shape

    @pl.when(lax.axis_index(axis) >= cores)
    def _():
        for start in range(0, rows, step):
            mine = slice(start, start + step)
            sofar_ref[:, mine] = summed_ref[:, mine] * factor_ref[:, mine] + weighted_values(
                packs, places, probs_ref, mine, rows, width
            )


def carried_state(numbers, packs, rows, width):
    totals, states = [], []
    for pack_ref in packs:
        tail = pack_ref[rows + width : rows + width + PAD, :].astype(F32)
        totals.append(tail[0:1] + tail[1:2] + tail[2:3])
        states.append(pack_ref[rows : rows + width, :].astype(F32))
    carried = jnp.zeros((width, width), F32)
    for number, state in zip(numbers, states):
        between = jnp.where(number >= 0, 0.0, NEG)
        for other, total in zip(numbers, totals):
            between = between + jnp.where(other > number, 1.0, 0.0) * total
        carried = carried + jnp.exp(between) * state
    return carried.astype(BF16)


def late_kernel(step, axis, cores, chips, late, *refs):
    lin_qt_ref, intra_ref, cum_row_ref, sofar_ref, sum_ref, probs_ref = refs[2:8]
    *blocks, linear_ref, softmax_ref, linear_buffer, softmax_buffer, sems = refs[8:]
    width, rows = lin_qt_ref.shape
    position, numbers = block_numbers(axis, cores, chips)

    @pl.when(position >= cores)
    def _():
        linear_copy = pltpu.make_async_copy(linear_buffer, linear_ref, sems.at[0])
        softmax_copy = pltpu.make_async_copy(softmax_buffer, softmax_ref, sems.at[1])
        for start in range(0, rows, step):
            mine = slice(start, start + step)
            summed = sofar_ref[:, mine]
            if late:
                last = [blocks[place] for place in late]
                summed = summed + weighted_values(last, late, probs_ref, mine, rows, width)
            softmax_buffer[mine, :] = jnp.transpose((summed / sum_ref[:, mine]).astype(BF16))
        softmax_copy.start()
        carried = carried_state(numbers, blocks, rows, width)
        put_linear(step, carried, lin_qt_ref, intra_ref, cum_row_ref, linear_buffer)
        linear_copy.start()
        softmax_copy.wait()
        linear_copy.wait()


def keep_in_hbm(x):
    return pltpu.with_memory_space_constraint(x, pltpu.HBM)


def keep_in_vmem(x):
    return pltpu.with_memory_space_constraint(x, VMEM)


def kept_in_vmem(x):
    return VMEM(x.shape, x.dtype)


def kept_in_hbm(x):
    return pltpu.HBM(x.shape, x.dtype)


def call(body, operands, outs, given=(), written=(), resumed=(), scratch=()):
    size = sum(math.prod(x.shape) * x.dtype.itemsize for x in (*given, *operands, *outs))
    inside, outside = pl.BlockSpec(memory_space=VMEM), pl.BlockSpec(memory_space=pl.ANY)
    hbm = (*given, *resumed)
    scratch = [VMEM(x.shape, x.dtype) for x in (*scratch, *written)]
    moved = len(given) + len(written)
    return pl.pallas_call(
        body,
        out_shape=(*map(kept_in_hbm, written), *map(kept_in_vmem, outs)),
        in_specs=[outside] * len(hbm) + [inside] * len(operands),
        out_specs=(*[outside] * len(written), *[inside] * len(outs)),
        scratch_shapes=[*scratch, pltpu.SemaphoreType.DMA((moved,))] if moved else [],
        input_output_aliases={place: place for place in range(len(resumed))},
        cost_estimate=pl.CostEstimate(flops=0, bytes_accessed=size, transcendentals=0),
        compiler_params=pltpu.CompilerParams(vmem_limit_bytes=KERNEL_VMEM),
    )(*map(keep_in_hbm, hbm), *map(keep_in_vmem, operands))


def on_device(axis, lin_query, lin_key, lin_value, log_decay, soft_query, soft_key, soft_value):
    rows, heads, width = lin_query.shape
    count = lax.axis_size(axis)
    cores = 2 if count % 2 == 0 else 1
    chips = count // cores

    def across(x, apart):
        return lax.ppermute(x, axis, [(i, (i + apart * cores) % count) for i in range(count)])

    def swapped(x, apart=0, after=None):
        if after is not None:
            x, _ = lax.optimization_barrier((x, after))
        return lax.ppermute(x, axis, [(i, i ^ 1 if i >= apart * cores else i) for i in range(count)])

    def near(x):
        return [swapped(x)] if cores == 2 else []

    def far(x):
        return [across(x, apart) for apart in range(1, chips)]

    def completed(blocks, after):
        out = []
        for apart, block in enumerate(blocks, 1):
            out.append(block)
            if cores == 2:
                out.append(swapped(block, apart, after))
        return out

    def one_head(lq, lk, lv, decay, sq, sk, sv):
        step = math.gcd(rows, 256)
        scale = math.log2(math.e) / math.sqrt(width)
        ring = (axis, cores, chips)

        def shape(*dims, dtype=F32):
            return jax.ShapeDtypeStruct(dims, dtype)

        def half(*dims):
            return shape(*dims, dtype=BF16)

        row, flat, flat16, block = shape(1, rows), shape(width, rows), half(width, rows), half(rows, width)
        keys = far(sk)
        pack, cum_row, cum_col, lin_vt, lk, lq, sq, own_keys = call(
            state_kernel,
            (),
            (half(rows + width + PAD, width), row, shape(rows, width), flat16, block, block, block, block),
            given=(decay, lk, lv, sv, lq, sq, sk),
            scratch=(row, block, block),
        )
        qt, top, total, summed = call(
            functools.partial(soft_kernel, scale, step), (sq, own_keys, pack), (flat16, row, row, flat)
        )
        (pack, lin_vt), _ = lax.optimization_barrier(((pack, lin_vt), summed))
        packs, near_packs = far(pack), near(pack)
        (lq, lk), _ = lax.optimization_barrier(((lq, lk), keys))
        keys = [*near(sk), *completed(keys, summed)]
        lin_qt, intra = call(
            functools.partial(linear_kernel, step), (lq, lk, lin_vt, cum_row, cum_col), (flat16, flat)
        )
        top, _ = lax.optimization_barrier((top, intra))
        *began, probs, factor, sums = call(
            functools.partial(score_kernel, scale, step, *ring),
            (qt, top, total, summed, lin_qt, intra, cum_row, *near_packs, *keys),
            (half(len(keys) * rows, rows), row, row),
            written=(block, block),
        )
        blocks = [*near_packs, *completed(packs, factor)]
        late = tuple(range(cores, len(blocks), cores)) if cores == 2 else ()
        early = tuple(place for place in range(len(blocks)) if place not in late)
        (sofar,) = call(
            functools.partial(early_kernel, step, axis, cores, early),
            (summed, factor, probs, *(blocks[place] for place in early)),
            (flat,),
        )
        return call(
            functools.partial(late_kernel, step, *ring, late),
            (lin_qt, intra, cum_row, sofar, sums, probs, *blocks),
            (),
            written=(block, block),
            resumed=began,
        )

    outs = [
        one_head(
            *(x[:, head] for x in (lin_query, lin_key, lin_value)),
            log_decay[head : head + 1],
            *(x[:, head] for x in (soft_query, soft_key, soft_value)),
        )
        for head in range(heads)
    ]
    linear = jnp.stack([pair[0] for pair in outs], axis=1)
    softmax = jnp.stack([pair[1] for pair in outs], axis=1)
    return linear, softmax


def solution(mesh):
    block = P("ctx", "tp", None)
    return jax.shard_map(
        functools.partial(on_device, "ctx"),
        mesh=mesh,
        in_specs=(block, block, block, P("tp", "ctx"), block, block, block),
        out_specs=(block, block),
        check_vma=False,
    )
```

```python
import functools
import math

import jax
import jax.numpy as jnp
from jax import lax
from jax.experimental import pallas as pl
from jax.experimental.pallas import tpu as pltpu
from jax.sharding import PartitionSpec as P

NEG = -1e30
TINY = 1e-6
PAD = 16
KERNEL_VMEM = 16 * 2**20
F32 = jnp.float32
BF16 = jnp.bfloat16
VMEM = pltpu.VMEM


def dot(a, b):
    return lax.dot_general(a, b, (((1,), (0,)), ((), ())), preferred_element_type=F32)


def three_parts(x):
    high = x.astype(BF16)
    rest = x - high.astype(F32)
    middle = rest.astype(BF16)
    low = (rest - middle.astype(F32)).astype(BF16)
    return high, middle, low


def iota(shape, dim):
    return lax.broadcasted_iota(jnp.int32, shape, dim)


def select_rows(parts, rows, width):
    row = iota((rows, width), 0)
    out = jnp.zeros((rows, width), F32)
    for number, part in enumerate(parts):
        out = jnp.where(row == number, part.astype(F32), out)
    return out.astype(BF16)


def side_by_side(ref, rows, width):
    pieces = [ref[left : left + width, :] for left in range(0, rows, width)]
    return pieces[0] if len(pieces) == 1 else jnp.concatenate(pieces, axis=1)


def state_kernel(
    decay_hbm, key_hbm, value_hbm, soft_value_hbm, query_hbm, soft_query_hbm, soft_key_hbm,
    pack_ref, cum_row_ref, cum_col_ref, value_t_ref, key_ref, query_ref, soft_query_ref, soft_key_ref,
    decay_ref, value_ref, soft_value_ref, sems,
):
    rows, width = key_ref.shape
    copies = [
        pltpu.make_async_copy(source, target, sems.at[place])
        for place, (source, target) in enumerate(
            (
                (decay_hbm, decay_ref),
                (key_hbm, key_ref),
                (value_hbm, value_ref),
                (soft_value_hbm, soft_value_ref),
                (soft_query_hbm, soft_query_ref),
                (soft_key_hbm, soft_key_ref),
                (query_hbm, query_ref),
            )
        )
    ]
    for copy in copies:
        copy.start()
    upto = (iota((rows, rows), 0) <= iota((rows, rows), 1)).astype(F32).astype(BF16)
    copies[0].wait()
    parts = select_rows(three_parts(decay_ref[...]), PAD, rows)
    cum_row = jnp.sum(dot(parts, upto), axis=0, keepdims=True)
    cum_row_ref[...] = cum_row
    cum_col = jnp.transpose(jnp.broadcast_to(cum_row, (width, rows)))
    cum_col_ref[...] = cum_col
    total = cum_col[rows - 1 :, :]
    for copy in copies[1:4]:
        copy.wait()
    decayed = (key_ref[...].astype(F32) * jnp.exp(total - cum_col)).astype(BF16)
    value_t = jnp.transpose(value_ref[...])
    value_t_ref[...] = value_t
    pack_ref[rows : rows + width, :] = dot(value_t, decayed).astype(BF16)
    pack_ref[rows + width :, :] = select_rows(three_parts(total), PAD, width)
    for left in range(0, rows, width):
        pack_ref[left : left + width, :] = jnp.transpose(soft_value_ref[left : left + width, :])
    for copy in copies[4:]:
        copy.wait()


def soft_kernel(scale, step, q_ref, k_ref, pack_ref, qt_ref, top_ref, total_ref, summed_ref):
    rows, width = q_ref.shape
    qt_ref[...] = jnp.transpose(q_ref[...])
    value_t = side_by_side(pack_ref, rows, width)
    keep = iota((step, step), 0) <= iota((step, step), 1)
    for start in range(0, rows, step):
        stop = start + step
        scores = dot(k_ref[:stop, :], qt_ref[:, start:stop])
        last = jnp.where(keep, scores[start:, :], NEG)
        scores = jnp.concatenate([scores[:start, :], last], axis=0) if start else last
        top = jnp.max(scores, axis=0, keepdims=True)
        probs = jnp.exp2((scores - top) * scale)
        top_ref[:, start:stop] = top
        total_ref[:, start:stop] = jnp.sum(probs, axis=0, keepdims=True)
        summed_ref[:, start:stop] = dot(value_t[:, :stop], probs.astype(BF16))


def linear_kernel(step, q_ref, k_ref, value_t_ref, cum_row_ref, cum_col_ref, qt_ref, intra_ref):
    rows, width = q_ref.shape
    qt_ref[...] = jnp.transpose(q_ref[...])
    keep = iota((step, step), 0) <= iota((step, step), 1)
    for start in range(0, rows, step):
        stop = start + step
        scores = dot(k_ref[:stop, :], qt_ref[:, start:stop])
        cum_t = cum_row_ref[:, start:stop]
        cum_s = jnp.concatenate([cum_col_ref[:stop, :]] * (step // width), axis=1)
        diff = cum_t - cum_s
        last = jnp.where(keep, diff[start:, :], NEG)
        diff = jnp.concatenate([diff[:start, :], last], axis=0) if start else last
        weights = (scores * jnp.exp(diff)).astype(BF16)
        intra_ref[:, start:stop] = dot(value_t_ref[:, :stop], weights)


def block_numbers(axis, cores, chips):
    position = lax.axis_index(axis)
    if cores == 1:
        return position, [position - apart for apart in range(1, chips)]
    other = lax.rem(position, 2)
    partner = position + 1 - 2 * other
    numbers = [jnp.where(other == 1, position - 1, -1)]
    for apart in range(1, chips):
        numbers += [position - 2 * apart, partner - 2 * apart]
    return position, numbers


def normalized(raw):
    square = jnp.sum(raw * raw, axis=0, keepdims=True) * (1.0 / raw.shape[0])
    return jnp.transpose((raw * lax.rsqrt(square + TINY)).astype(BF16))


def put_linear(step, carried, qt_ref, intra_ref, cum_row_ref, buffer):
    for start in range(0, qt_ref.shape[1], step):
        mine = slice(start, start + step)
        inter = dot(carried, qt_ref[:, mine])
        buffer[mine, :] = normalized(intra_ref[:, mine] + inter * jnp.exp(cum_row_ref[:, mine]))


def score_kernel(scale, step, axis, cores, chips, *refs):
    qt_ref, top_ref, total_ref, summed_ref, lin_qt_ref, intra_ref, cum_row_ref = refs[:7]
    near_packs, refs = refs[7 : 6 + cores], refs[6 + cores :]
    *key_refs, linear_ref, softmax_ref, probs_ref, factor_ref, sum_ref = refs[:-3]
    linear_buffer, softmax_buffer, sems = refs[-3:]
    width, rows = qt_ref.shape
    position, numbers = block_numbers(axis, cores, chips)
    away = [jnp.where(number >= 0, 0.0, NEG) for number in numbers]

    def weights(mine, keys):
        query = qt_ref[:, mine]
        old = top_ref[:, mine]
        scores = [dot(key, query) for key in keys]
        top = old
        for score, off in zip(scores, away):
            top = jnp.maximum(top, jnp.max(score, axis=0, keepdims=True) + off)
        factor = jnp.exp2((old - top) * scale)
        total = total_ref[:, mine] * factor
        probs = []
        for score, off in zip(scores, away):
            prob = jnp.exp2((score - (top - off)) * scale)
            total = total + jnp.sum(prob, axis=0, keepdims=True)
            probs.append(prob.astype(BF16))
        return probs, factor, total

    keys = [key_ref[...] for key_ref in key_refs]

    @pl.when(position >= cores)
    def _():
        for start in range(0, rows, step):
            mine = slice(start, start + step)
            probs, factor, total = weights(mine, keys)
            for place, prob in enumerate(probs):
                probs_ref[place * rows : (place + 1) * rows, mine] = prob
            factor_ref[:, mine] = factor
            sum_ref[:, mine] = total

    @pl.when(position < cores)
    def _():
        linear_copy = pltpu.make_async_copy(linear_buffer, linear_ref, sems.at[0])
        softmax_copy = pltpu.make_async_copy(softmax_buffer, softmax_ref, sems.at[1])
        for start in range(0, rows, step):
            mine = slice(start, start + step)
            probs, factor, total = weights(mine, keys[: cores - 1])
            summed = summed_ref[:, mine] * factor
            for pack_ref, prob in zip(near_packs, probs):
                summed = summed + dot(side_by_side(pack_ref, rows, width), prob)
            softmax_buffer[mine, :] = jnp.transpose((summed / total).astype(BF16))
        softmax_copy.start()
        carried = jnp.zeros((width, width), F32)
        for pack_ref in near_packs:
            carried = jnp.where(position == 1, pack_ref[rows : rows + width, :].astype(F32), carried)
        put_linear(step, carried.astype(BF16), lin_qt_ref, intra_ref, cum_row_ref, linear_buffer)
        linear_copy.start()
        softmax_copy.wait()
        linear_copy.wait()


def weighted_values(refs, places, probs_ref, mine, rows, width):
    out = None
    for place, ref in zip(places, refs):
        term = dot(side_by_side(ref, rows, width), probs_ref[place * rows : (place + 1) * rows, mine])
        out = term if out is None else out + term
    return out


def early_kernel(step, axis, cores, places, *refs):
    summed_ref, factor_ref, probs_ref, *packs, sofar_ref = refs
    width, rows = summed_ref.shape

    @pl.when(lax.axis_index(axis) >= cores)
    def _():
        for start in range(0, rows, step):
            mine = slice(start, start + step)
            sofar_ref[:, mine] = summed_ref[:, mine] * factor_ref[:, mine] + weighted_values(
                packs, places, probs_ref, mine, rows, width
            )


def carried_state(numbers, packs, rows, width):
    totals, states = [], []
    for pack_ref in packs:
        tail = pack_ref[rows + width : rows + width + PAD, :].astype(F32)
        totals.append(tail[0:1] + tail[1:2] + tail[2:3])
        states.append(pack_ref[rows : rows + width, :].astype(F32))
    carried = jnp.zeros((width, width), F32)
    for number, state in zip(numbers, states):
        between = jnp.where(number >= 0, 0.0, NEG)
        for other, total in zip(numbers, totals):
            between = between + jnp.where(other > number, 1.0, 0.0) * total
        carried = carried + jnp.exp(between) * state
    return carried.astype(BF16)


def late_kernel(step, axis, cores, chips, late, *refs):
    lin_qt_ref, intra_ref, cum_row_ref, sofar_ref, sum_ref, probs_ref = refs[2:8]
    *blocks, linear_ref, softmax_ref, linear_buffer, softmax_buffer, sems = refs[8:]
    width, rows = lin_qt_ref.shape
    position, numbers = block_numbers(axis, cores, chips)

    @pl.when(position >= cores)
    def _():
        linear_copy = pltpu.make_async_copy(linear_buffer, linear_ref, sems.at[0])
        softmax_copy = pltpu.make_async_copy(softmax_buffer, softmax_ref, sems.at[1])
        for start in range(0, rows, step):
            mine = slice(start, start + step)
            summed = sofar_ref[:, mine]
            if late:
                last = [blocks[place] for place in late]
                summed = summed + weighted_values(last, late, probs_ref, mine, rows, width)
            softmax_buffer[mine, :] = jnp.transpose((summed / sum_ref[:, mine]).astype(BF16))
        softmax_copy.start()
        carried = carried_state(numbers, blocks, rows, width)
        put_linear(step, carried, lin_qt_ref, intra_ref, cum_row_ref, linear_buffer)
        linear_copy.start()
        softmax_copy.wait()
        linear_copy.wait()


def keep_in_hbm(x):
    return pltpu.with_memory_space_constraint(x, pltpu.HBM)


def keep_in_vmem(x):
    return pltpu.with_memory_space_constraint(x, VMEM)


def kept_in_vmem(x):
    return VMEM(x.shape, x.dtype)


def kept_in_hbm(x):
    return pltpu.HBM(x.shape, x.dtype)


def call(body, operands, outs, given=(), written=(), resumed=(), scratch=()):
    size = sum(math.prod(x.shape) * x.dtype.itemsize for x in (*given, *operands, *outs))
    inside, outside = pl.BlockSpec(memory_space=VMEM), pl.BlockSpec(memory_space=pl.ANY)
    hbm = (*given, *resumed)
    scratch = [VMEM(x.shape, x.dtype) for x in (*scratch, *written)]
    moved = len(given) + len(written)
    return pl.pallas_call(
        body,
        out_shape=(*map(kept_in_hbm, written), *map(kept_in_vmem, outs)),
        in_specs=[outside] * len(hbm) + [inside] * len(operands),
        out_specs=(*[outside] * len(written), *[inside] * len(outs)),
        scratch_shapes=[*scratch, pltpu.SemaphoreType.DMA((moved,))] if moved else [],
        input_output_aliases={place: place for place in range(len(resumed))},
        cost_estimate=pl.CostEstimate(flops=0, bytes_accessed=size, transcendentals=0),
        compiler_params=pltpu.CompilerParams(vmem_limit_bytes=KERNEL_VMEM),
    )(*map(keep_in_hbm, hbm), *map(keep_in_vmem, operands))


def on_device(axis, lin_query, lin_key, lin_value, log_decay, soft_query, soft_key, soft_value):
    rows, heads, width = lin_query.shape
    count = lax.axis_size(axis)
    cores = 2 if count % 2 == 0 else 1
    chips = count // cores

    def across(x, apart):
        return lax.ppermute(x, axis, [(i, (i + apart * cores) % count) for i in range(count)])

    def swapped(x, after=None):
        if after is not None:
            x, _ = lax.optimization_barrier((x, after))
        return lax.ppermute(x, axis, [(i, i ^ 1) for i in range(count)])

    def near(x):
        return [swapped(x)] if cores == 2 else []

    def far(x):
        return [across(x, apart) for apart in range(1, chips)]

    def completed(blocks, after):
        out = []
        for block in blocks:
            out.append(block)
            if cores == 2:
                out.append(swapped(block, after))
        return out

    def one_head(lq, lk, lv, decay, sq, sk, sv):
        step = math.gcd(rows, 256)
        scale = math.log2(math.e) / math.sqrt(width)
        ring = (axis, cores, chips)

        def shape(*dims, dtype=F32):
            return jax.ShapeDtypeStruct(dims, dtype)

        def half(*dims):
            return shape(*dims, dtype=BF16)

        row, flat, flat16, block = shape(1, rows), shape(width, rows), half(width, rows), half(rows, width)
        keys = far(sk)
        pack, cum_row, cum_col, lin_vt, lk, lq, sq, own_keys = call(
            state_kernel,
            (),
            (half(rows + width + PAD, width), row, shape(rows, width), flat16, block, block, block, block),
            given=(decay, lk, lv, sv, lq, sq, sk),
            scratch=(row, block, block),
        )
        qt, top, total, summed = call(
            functools.partial(soft_kernel, scale, step), (sq, own_keys, pack), (flat16, row, row, flat)
        )
        (pack, lin_vt), _ = lax.optimization_barrier(((pack, lin_vt), summed))
        packs, near_packs = far(pack), near(pack)
        (lq, lk), _ = lax.optimization_barrier(((lq, lk), keys))
        keys = [*near(sk), *completed(keys, summed)]
        lin_qt, intra = call(
            functools.partial(linear_kernel, step), (lq, lk, lin_vt, cum_row, cum_col), (flat16, flat)
        )
        top, _ = lax.optimization_barrier((top, intra))
        *began, probs, factor, sums = call(
            functools.partial(score_kernel, scale, step, *ring),
            (qt, top, total, summed, lin_qt, intra, cum_row, *near_packs, *keys),
            (half(len(keys) * rows, rows), row, row),
            written=(block, block),
        )
        blocks = [*near_packs, *completed(packs, factor)]
        late = tuple(range(cores, len(blocks), cores)) if cores == 2 else ()
        early = tuple(place for place in range(len(blocks)) if place not in late)
        (sofar,) = call(
            functools.partial(early_kernel, step, axis, cores, early),
            (summed, factor, probs, *(blocks[place] for place in early)),
            (flat,),
        )
        return call(
            functools.partial(late_kernel, step, *ring, late),
            (lin_qt, intra, cum_row, sofar, sums, probs, *blocks),
            (),
            written=(block, block),
            resumed=began,
        )

    outs = [
        one_head(
            *(x[:, head] for x in (lin_query, lin_key, lin_value)),
            log_decay[head : head + 1],
            *(x[:, head] for x in (soft_query, soft_key, soft_value)),
        )
        for head in range(heads)
    ]
    linear = jnp.stack([pair[0] for pair in outs], axis=1)
    softmax = jnp.stack([pair[1] for pair in outs], axis=1)
    return linear, softmax


def solution(mesh):
    block = P("ctx", "tp", None)
    return jax.shard_map(
        functools.partial(on_device, "ctx"),
        mesh=mesh,
        in_specs=(block, block, block, P("tp", "ctx"), block, block, block),
        out_specs=(block, block),
        check_vma=False,
    )
```

```python
import functools
import math

import jax
import jax.numpy as jnp
from jax import lax
from jax.experimental import pallas as pl
from jax.experimental.pallas import tpu as pltpu
from jax.sharding import PartitionSpec as P

NEG = -1e30
TINY = 1e-6
PAD = 16
KERNEL_VMEM = 16 * 2**20
F32 = jnp.float32
BF16 = jnp.bfloat16
VMEM = pltpu.VMEM


def dot(a, b):
    return lax.dot_general(a, b, (((1,), (0,)), ((), ())), preferred_element_type=F32)


def three_parts(x):
    high = x.astype(BF16)
    rest = x - high.astype(F32)
    middle = rest.astype(BF16)
    low = (rest - middle.astype(F32)).astype(BF16)
    return high, middle, low


def iota(shape, dim):
    return lax.broadcasted_iota(jnp.int32, shape, dim)


def select_rows(parts, rows, width):
    row = iota((rows, width), 0)
    out = jnp.zeros((rows, width), F32)
    for number, part in enumerate(parts):
        out = jnp.where(row == number, part.astype(F32), out)
    return out.astype(BF16)


def side_by_side(ref, rows, width):
    pieces = [ref[left : left + width, :] for left in range(0, rows, width)]
    return pieces[0] if len(pieces) == 1 else jnp.concatenate(pieces, axis=1)


def state_kernel(
    decay_hbm, key_hbm, value_hbm, soft_value_hbm, query_hbm, soft_query_hbm, soft_key_hbm,
    pack_ref, cum_row_ref, cum_col_ref, value_t_ref, key_ref, query_ref, soft_query_ref, soft_key_ref,
    decay_ref, value_ref, soft_value_ref, sems,
):
    copies = [
        pltpu.make_async_copy(source, target, sems.at[place])
        for place, (source, target) in enumerate(
            (
                (decay_hbm, decay_ref),
                (key_hbm, key_ref),
                (value_hbm, value_ref),
                (soft_value_hbm, soft_value_ref),
                (soft_query_hbm, soft_query_ref),
                (soft_key_hbm, soft_key_ref),
                (query_hbm, query_ref),
            )
        )
    ]
    for copy in copies:
        copy.start()
    rows, width = key_ref.shape
    upto = (iota((rows, rows), 0) <= iota((rows, rows), 1)).astype(F32).astype(BF16)
    copies[0].wait()
    parts = select_rows(three_parts(decay_ref[...]), PAD, rows)
    cum_row = jnp.sum(dot(parts, upto), axis=0, keepdims=True)
    cum_row_ref[...] = cum_row
    cum_col = jnp.transpose(jnp.broadcast_to(cum_row, (width, rows)))
    cum_col_ref[...] = cum_col
    total = cum_col[rows - 1 :, :]
    for copy in copies[1:4]:
        copy.wait()
    decayed = (key_ref[...].astype(F32) * jnp.exp(total - cum_col)).astype(BF16)
    value_t = jnp.transpose(value_ref[...])
    value_t_ref[...] = value_t
    state_t = dot(value_t, decayed)
    for left in range(0, rows, width):
        pack_ref[left : left + width, :] = jnp.transpose(soft_value_ref[left : left + width, :])
    pack_ref[rows : rows + width, :] = state_t.astype(BF16)
    pack_ref[rows + width :, :] = select_rows(three_parts(total), PAD, width)
    for copy in copies[4:]:
        copy.wait()


def soft_kernel(scale, step, q_ref, k_ref, pack_ref, qt_ref, top_ref, total_ref, summed_ref):
    rows, width = q_ref.shape
    qt_ref[...] = jnp.transpose(q_ref[...])
    value_t = side_by_side(pack_ref, rows, width)
    keep = iota((step, step), 0) <= iota((step, step), 1)
    for start in range(0, rows, step):
        stop = start + step
        scores = dot(k_ref[:stop, :], qt_ref[:, start:stop])
        last = jnp.where(keep, scores[start:, :], NEG)
        scores = jnp.concatenate([scores[:start, :], last], axis=0) if start else last
        top = jnp.max(scores, axis=0, keepdims=True)
        probs = jnp.exp2((scores - top) * scale)
        top_ref[:, start:stop] = top
        total_ref[:, start:stop] = jnp.sum(probs, axis=0, keepdims=True)
        summed_ref[:, start:stop] = dot(value_t[:, :stop], probs.astype(BF16))


def linear_kernel(step, q_ref, k_ref, value_t_ref, cum_row_ref, cum_col_ref, qt_ref, intra_ref):
    rows, width = q_ref.shape
    qt_ref[...] = jnp.transpose(q_ref[...])
    keep = iota((step, step), 0) <= iota((step, step), 1)
    for start in range(0, rows, step):
        stop = start + step
        scores = dot(k_ref[:stop, :], qt_ref[:, start:stop])
        cum_t = cum_row_ref[:, start:stop]
        cum_s = jnp.concatenate([cum_col_ref[:stop, :]] * (step // width), axis=1)
        diff = cum_t - cum_s
        last = jnp.where(keep, diff[start:, :], NEG)
        diff = jnp.concatenate([diff[:start, :], last], axis=0) if start else last
        weights = (scores * jnp.exp(diff)).astype(BF16)
        intra_ref[:, start:stop] = dot(value_t_ref[:, :stop], weights)


def block_numbers(axis, cores, chips):
    position = lax.axis_index(axis)
    if cores == 1:
        return position, [position - apart for apart in range(1, chips)]
    other = lax.rem(position, 2)
    partner = position + 1 - 2 * other
    numbers = [jnp.where(other == 1, position - 1, -1)]
    for apart in range(1, chips):
        numbers += [position - 2 * apart, partner - 2 * apart]
    return position, numbers


def by_chip(position, cores, count, body):
    pl.when(position >= cores)(lambda: body(count))
    pl.when(position < cores)(lambda: body(cores - 1))


def score_kernel(scale, step, axis, cores, chips, qt_ref, top_ref, total_ref, *refs):
    key_refs, (probs_ref, factor_ref, sum_ref) = refs[:-3], refs[-3:]
    rows = qt_ref.shape[1]
    position, numbers = block_numbers(axis, cores, chips)
    away = [jnp.where(number >= 0, 0.0, NEG) for number in numbers]

    def body(count):
        for start in range(0, rows, step):
            mine = slice(start, start + step)
            query = qt_ref[:, mine]
            old = top_ref[:, mine]
            scores = [dot(key_refs[i][...], query) for i in range(count)]
            top = old
            for score, off in zip(scores, away):
                top = jnp.maximum(top, jnp.max(score, axis=0, keepdims=True) + off)
            factor = jnp.exp2((old - top) * scale)
            total = total_ref[:, mine] * factor
            for number, (score, off) in enumerate(zip(scores, away)):
                probs = jnp.exp2((score - (top - off)) * scale)
                total = total + jnp.sum(probs, axis=0, keepdims=True)
                probs_ref[number * rows : (number + 1) * rows, mine] = probs.astype(BF16)
            factor_ref[:, mine] = factor
            sum_ref[:, mine] = total

    by_chip(position, cores, len(key_refs), body)


def carried_state(numbers, pack_refs, rows, width):
    totals, states = [], []
    for pack_ref in pack_refs:
        tail = pack_ref[rows + width :, :].astype(F32)
        totals.append(tail[0:1] + tail[1:2] + tail[2:3])
        states.append(pack_ref[rows : rows + width, :].astype(F32))
    carried = jnp.zeros((width, width), F32)
    for number, state in zip(numbers, states):
        between = jnp.where(number >= 0, 0.0, NEG)
        for other, total in zip(numbers, totals):
            between = between + jnp.where(other > number, 1.0, 0.0) * total
        carried = carried + jnp.exp(between) * state
    return carried.astype(BF16)


def weighted_values(pack_refs, places, probs_ref, mine, rows, width):
    out = None
    for place, pack_ref in zip(places, pack_refs):
        value_t = side_by_side(pack_ref, rows, width)
        term = dot(value_t, probs_ref[place * rows : (place + 1) * rows, mine])
        out = term if out is None else out + term
    return out


def write_out(step, numbers, places, pack_refs, linear_packs, refs, outs, buffers, sems):
    lin_qt_ref, intra_ref, cum_row_ref, summed_ref, factor_ref, sum_ref, probs_ref = refs
    width, rows = lin_qt_ref.shape
    linear_buffer, softmax_buffer = buffers
    softmax_copy, linear_copy = (
        pltpu.make_async_copy(buffer, out, sems.at[place])
        for place, (buffer, out) in enumerate(((softmax_buffer, outs[1]), (linear_buffer, outs[0])))
    )
    for start in range(0, rows, step):
        mine = slice(start, start + step)
        summed = summed_ref[:, mine]
        if factor_ref is not None:
            summed = summed * factor_ref[:, mine]
        more = weighted_values(pack_refs, places, probs_ref, mine, rows, width)
        summed = summed if more is None else summed + more
        softmax_buffer[mine, :] = jnp.transpose((summed / sum_ref[:, mine]).astype(BF16))
    softmax_copy.start()
    carried = carried_state(numbers, linear_packs, rows, width)
    for start in range(0, rows, step):
        mine = slice(start, start + step)
        inter = dot(carried, lin_qt_ref[:, mine])
        raw = intra_ref[:, mine] + inter * jnp.exp(cum_row_ref[:, mine])
        square = jnp.sum(raw * raw, axis=0, keepdims=True) * (1.0 / width)
        linear_buffer[mine, :] = jnp.transpose((raw * lax.rsqrt(square + TINY)).astype(BF16))
    linear_copy.start()
    softmax_copy.wait()
    linear_copy.wait()


def early_kernel(step, axis, cores, chips, places, *refs):
    head, refs = refs[:7], refs[7:]
    packs, (linear_ref, softmax_ref, sofar_ref, *scratch) = refs[: len(places)], refs[len(places) :]
    lin_qt_ref, intra_ref, cum_row_ref, summed_ref, factor_ref, sum_ref, probs_ref = head
    width, rows = lin_qt_ref.shape
    position, numbers = block_numbers(axis, cores, chips)

    @pl.when(position >= cores)
    def _():
        for start in range(0, rows, step):
            mine = slice(start, start + step)
            sofar_ref[:, mine] = summed_ref[:, mine] * factor_ref[:, mine] + weighted_values(
                packs, places, probs_ref, mine, rows, width
            )

    @pl.when(position < cores)
    def _():
        own = cores - 1
        write_out(
            step, numbers[:own], places[:own], packs[:own], packs[:own], head,
            (linear_ref, softmax_ref), scratch[:2], scratch[2],
        )


def late_kernel(step, axis, cores, chips, early, late, *refs):
    refs = refs[2:]
    lin_qt_ref, intra_ref, cum_row_ref, sofar_ref, sum_ref, probs_ref = refs[:6]
    count = len(early) + len(late)
    packs, (linear_ref, softmax_ref, *scratch) = refs[6 : 6 + count], refs[6 + count :]
    position, numbers = block_numbers(axis, cores, chips)

    @pl.when(position >= cores)
    def _():
        write_out(
            step, numbers, late, [packs[place] for place in late], packs,
            (lin_qt_ref, intra_ref, cum_row_ref, sofar_ref, None, sum_ref, probs_ref),
            (linear_ref, softmax_ref), scratch[:2], scratch[2],
        )


def keep_in_hbm(x):
    return pltpu.with_memory_space_constraint(x, pltpu.HBM)


def keep_in_vmem(x):
    return pltpu.with_memory_space_constraint(x, VMEM)


def kept_in_vmem(x):
    return VMEM(x.shape, x.dtype)


def kept_in_hbm(x):
    return pltpu.HBM(x.shape, x.dtype)


def call(body, operands, outs, given=(), written=(), resumed=(), scratch=()):
    size = sum(math.prod(x.shape) * x.dtype.itemsize for x in (*given, *operands, *outs))
    inside, outside = pl.BlockSpec(memory_space=VMEM), pl.BlockSpec(memory_space=pl.ANY)
    hbm = (*given, *resumed)
    scratch = [VMEM(x.shape, x.dtype) for x in (*scratch, *written)]
    moved = len(given) + len(written)
    return pl.pallas_call(
        body,
        out_shape=(*map(kept_in_hbm, written), *map(kept_in_vmem, outs)),
        in_specs=[outside] * len(hbm) + [inside] * len(operands),
        out_specs=(*[outside] * len(written), *[inside] * len(outs)),
        scratch_shapes=[*scratch, pltpu.SemaphoreType.DMA((moved,))] if moved else [],
        input_output_aliases={place: place for place in range(len(resumed))},
        cost_estimate=pl.CostEstimate(flops=0, bytes_accessed=size, transcendentals=0),
        compiler_params=pltpu.CompilerParams(vmem_limit_bytes=KERNEL_VMEM),
    )(*map(keep_in_hbm, hbm), *map(keep_in_vmem, operands))


def on_device(axis, lin_query, lin_key, lin_value, log_decay, soft_query, soft_key, soft_value):
    rows, heads, width = lin_query.shape
    count = lax.axis_size(axis)
    cores = 2 if count % 2 == 0 else 1
    chips = count // cores

    def across(x, apart):
        return lax.ppermute(x, axis, [(i, (i + apart * cores) % count) for i in range(count)])

    def onward(x, apart):
        return lax.ppermute(x, axis, [(i, i + apart * cores) for i in range(count - apart * cores)])

    def swapped(x, after=None):
        if after is not None:
            x, _ = lax.optimization_barrier((x, after))
        return lax.ppermute(x, axis, [(i, i ^ 1) for i in range(count)])

    def spread(x, send):
        far = [send(x, apart) for apart in range(1, chips)]
        own = [swapped(x)] if cores == 2 else []
        return own, far

    def complete(of, after):
        own, far = of
        out = list(own)
        for block in far:
            out.append(block)
            if cores == 2:
                out.append(swapped(block, after))
        return out

    def one_head(lq, lk, lv, decay, sq, sk, sv):
        step = math.gcd(rows, 256)
        scale = math.log2(math.e) / math.sqrt(width)
        ring = (axis, cores, chips)

        def shape(*dims, dtype=F32):
            return jax.ShapeDtypeStruct(dims, dtype)

        row, flat, flat16 = shape(1, rows), shape(width, rows), shape(width, rows, dtype=BF16)
        block = shape(rows, width, dtype=BF16)
        keys = spread(sk, across)
        pack, cum_row, cum_col, lin_vt, lk, lq, sq, sk = call(
            state_kernel,
            (),
            (
                shape(rows + width + PAD, width, dtype=BF16), row, shape(rows, width), flat16,
                block, block, block, block,
            ),
            given=(decay, lk, lv, sv, lq, sq, sk),
            scratch=(row, block, block),
        )
        qt, top, total, summed = call(
            functools.partial(soft_kernel, scale, step), (sq, sk, pack), (flat16, row, row, flat)
        )
        packs = spread(pack, onward)
        keys = complete(keys, summed)
        (lq, lk), _ = lax.optimization_barrier(((lq, lk), keys[cores - 1 :: cores]))
        lin_qt, intra = call(
            functools.partial(linear_kernel, step), (lq, lk, lin_vt, cum_row, cum_col), (flat16, flat)
        )
        top, _ = lax.optimization_barrier((top, intra))
        probs, factor, sums = call(
            functools.partial(score_kernel, scale, step, *ring),
            (qt, top, total, *keys),
            (shape(len(keys) * rows, rows, dtype=BF16), row, row),
        )
        packs = complete(packs, factor)
        late = tuple(range(cores, len(packs), cores)) if cores == 2 else ()
        early = tuple(place for place in range(len(packs)) if place not in late)
        *began, sofar = call(
            functools.partial(early_kernel, step, *ring, early),
            (lin_qt, intra, cum_row, summed, factor, sums, probs, *(packs[place] for place in early)),
            (flat,),
            written=(block, block),
        )
        return call(
            functools.partial(late_kernel, step, *ring, early, late),
            (lin_qt, intra, cum_row, sofar, sums, probs, *packs),
            (),
            written=(block, block),
            resumed=began,
        )

    outs = [
        one_head(
            *(x[:, head] for x in (lin_query, lin_key, lin_value)),
            log_decay[head : head + 1],
            *(x[:, head] for x in (soft_query, soft_key, soft_value)),
        )
        for head in range(heads)
    ]
    linear = jnp.stack([pair[0] for pair in outs], axis=1)
    softmax = jnp.stack([pair[1] for pair in outs], axis=1)
    return linear, softmax


def solution(mesh):
    block = P("ctx", "tp", None)
    return jax.shard_map(
        functools.partial(on_device, "ctx"),
        mesh=mesh,
        in_specs=(block, block, block, P("tp", "ctx"), block, block, block),
        out_specs=(block, block),
        check_vma=False,
    )
```

```python
import functools
import math

import jax
import jax.numpy as jnp
from jax import lax
from jax.experimental import pallas as pl
from jax.experimental.pallas import tpu as pltpu
from jax.sharding import PartitionSpec as P

NEG = -1e30
TINY = 1e-6
PAD = 16
KERNEL_VMEM = 16 * 2**20
F32 = jnp.float32
BF16 = jnp.bfloat16
VMEM = pltpu.VMEM


def dot(a, b):
    return lax.dot_general(a, b, (((1,), (0,)), ((), ())), preferred_element_type=F32)


def three_parts(x):
    high = x.astype(BF16)
    rest = x - high.astype(F32)
    middle = rest.astype(BF16)
    low = (rest - middle.astype(F32)).astype(BF16)
    return high, middle, low


def iota(shape, dim):
    return lax.broadcasted_iota(jnp.int32, shape, dim)


def select_rows(parts, rows, width):
    row = iota((rows, width), 0)
    out = jnp.zeros((rows, width), F32)
    for number, part in enumerate(parts):
        out = jnp.where(row == number, part.astype(F32), out)
    return out.astype(BF16)


def side_by_side(ref, rows, width):
    pieces = [ref[left : left + width, :] for left in range(0, rows, width)]
    return pieces[0] if len(pieces) == 1 else jnp.concatenate(pieces, axis=1)


def state_kernel(
    decay_hbm, key_hbm, value_hbm, soft_value_hbm, query_hbm, soft_query_hbm, soft_key_hbm,
    soft_vt_ref, state_ref, cum_row_ref, cum_col_ref, value_t_ref, key_ref, query_ref, soft_query_ref, soft_key_ref,
    decay_ref, value_ref, soft_value_ref, sems,
):
    copies = [
        pltpu.make_async_copy(source, target, sems.at[place])
        for place, (source, target) in enumerate(
            (
                (decay_hbm, decay_ref),
                (key_hbm, key_ref),
                (value_hbm, value_ref),
                (soft_value_hbm, soft_value_ref),
                (soft_query_hbm, soft_query_ref),
                (soft_key_hbm, soft_key_ref),
                (query_hbm, query_ref),
            )
        )
    ]
    for copy in copies:
        copy.start()
    rows, width = key_ref.shape
    upto = (iota((rows, rows), 0) <= iota((rows, rows), 1)).astype(F32).astype(BF16)
    copies[0].wait()
    parts = select_rows(three_parts(decay_ref[...]), PAD, rows)
    cum_row = jnp.sum(dot(parts, upto), axis=0, keepdims=True)
    cum_row_ref[...] = cum_row
    cum_col = jnp.transpose(jnp.broadcast_to(cum_row, (width, rows)))
    cum_col_ref[...] = cum_col
    total = cum_col[rows - 1 :, :]
    for copy in copies[1:4]:
        copy.wait()
    decayed = (key_ref[...].astype(F32) * jnp.exp(total - cum_col)).astype(BF16)
    value_t = jnp.transpose(value_ref[...])
    value_t_ref[...] = value_t
    state_ref[:width, :] = dot(value_t, decayed).astype(BF16)
    state_ref[width:, :] = select_rows(three_parts(total), PAD, width)
    for left in range(0, rows, width):
        soft_vt_ref[left : left + width, :] = jnp.transpose(soft_value_ref[left : left + width, :])
    for copy in copies[4:]:
        copy.wait()


def sum_of_parts(tail):
    tail = tail.astype(F32)
    return tail[0:1] + tail[1:2] + tail[2:3]


def combine_kernel(axis, cores, *refs):
    *state_refs, soft_vt_ref, pack_ref = refs
    rows, width = soft_vt_ref.shape
    share = width // cores
    pack_ref[:rows, :] = soft_vt_ref[...]
    states = [ref[:width, :].astype(F32) for ref in state_refs]
    totals = [sum_of_parts(ref[width:, :]) for ref in state_refs]
    state, total = states[0], totals[0]
    if cores == 2:
        upper = lax.rem(lax.axis_index(axis), 2) == 1
        first, second = jnp.where(upper, states[1], state), jnp.where(upper, state, states[1])
        state = jnp.exp(jnp.where(upper, total, totals[1])) * first + second
        state = jnp.where(upper, state[share:], state[:share])
        total = total + totals[1]
    pack_ref[rows : rows + share, :] = state.astype(BF16)
    if pack_ref.shape[0] > rows + share:
        pack_ref[rows + share :, :] = select_rows(three_parts(total), PAD, width)


def soft_kernel(scale, step, q_ref, k_ref, pack_ref, qt_ref, top_ref, total_ref, summed_ref):
    rows, width = q_ref.shape
    qt_ref[...] = jnp.transpose(q_ref[...])
    value_t = side_by_side(pack_ref, rows, width)
    keep = iota((step, step), 0) <= iota((step, step), 1)
    for start in range(0, rows, step):
        stop = start + step
        scores = dot(k_ref[:stop, :], qt_ref[:, start:stop])
        last = jnp.where(keep, scores[start:, :], NEG)
        scores = jnp.concatenate([scores[:start, :], last], axis=0) if start else last
        top = jnp.max(scores, axis=0, keepdims=True)
        probs = jnp.exp2((scores - top) * scale)
        top_ref[:, start:stop] = top
        total_ref[:, start:stop] = jnp.sum(probs, axis=0, keepdims=True)
        summed_ref[:, start:stop] = dot(value_t[:, :stop], probs.astype(BF16))


def linear_kernel(step, q_ref, k_ref, value_t_ref, cum_row_ref, cum_col_ref, qt_ref, intra_ref):
    rows, width = q_ref.shape
    qt_ref[...] = jnp.transpose(q_ref[...])
    keep = iota((step, step), 0) <= iota((step, step), 1)
    for start in range(0, rows, step):
        stop = start + step
        scores = dot(k_ref[:stop, :], qt_ref[:, start:stop])
        cum_t = cum_row_ref[:, start:stop]
        cum_s = jnp.concatenate([cum_col_ref[:stop, :]] * (step // width), axis=1)
        diff = cum_t - cum_s
        last = jnp.where(keep, diff[start:, :], NEG)
        diff = jnp.concatenate([diff[:start, :], last], axis=0) if start else last
        weights = (scores * jnp.exp(diff)).astype(BF16)
        intra_ref[:, start:stop] = dot(value_t_ref[:, :stop], weights)


def block_numbers(axis, cores, chips):
    position = lax.axis_index(axis)
    if cores == 1:
        return position, [position - apart for apart in range(1, chips)]
    other = lax.rem(position, 2)
    partner = position + 1 - 2 * other
    numbers = [jnp.where(other == 1, position - 1, -1)]
    for apart in range(1, chips):
        numbers += [position - 2 * apart, partner - 2 * apart]
    return position, numbers


def by_chip(position, cores, count, body):
    pl.when(position >= cores)(lambda: body(count))
    pl.when(position < cores)(lambda: body(cores - 1))


def score_kernel(scale, step, axis, cores, chips, qt_ref, top_ref, total_ref, *refs):
    key_refs, (probs_ref, factor_ref, sum_ref) = refs[:-3], refs[-3:]
    rows = qt_ref.shape[1]
    position, numbers = block_numbers(axis, cores, chips)
    away = [jnp.where(number >= 0, 0.0, NEG) for number in numbers]

    def body(count):
        for start in range(0, rows, step):
            mine = slice(start, start + step)
            query = qt_ref[:, mine]
            old = top_ref[:, mine]
            scores = [dot(key_refs[i][...], query) for i in range(count)]
            top = old
            for score, off in zip(scores, away):
                top = jnp.maximum(top, jnp.max(score, axis=0, keepdims=True) + off)
            factor = jnp.exp2((old - top) * scale)
            total = total_ref[:, mine] * factor
            for number, (score, off) in enumerate(zip(scores, away)):
                probs = jnp.exp2((score - (top - off)) * scale)
                total = total + jnp.sum(probs, axis=0, keepdims=True)
                probs_ref[number * rows : (number + 1) * rows, mine] = probs.astype(BF16)
            factor_ref[:, mine] = factor
            sum_ref[:, mine] = total

    by_chip(position, cores, len(key_refs), body)


def carried_state(position, cores, states, packs, rows, width):
    share = width // cores
    upper = lax.rem(position, 2) == 1
    chip = position // cores
    carried = jnp.zeros((width, width), F32)
    between = jnp.zeros((1, width), F32)
    for apart in range(1, len(packs) // cores + 1):
        parts = packs[(apart - 1) * cores : apart * cores]
        state = [part[rows : rows + share, :].astype(F32) for part in parts]
        if cores == 2:
            halves = jnp.where(upper, state[1], state[0]), jnp.where(upper, state[0], state[1])
            state = [jnp.concatenate(halves, axis=0)]
        carried = carried + jnp.exp(between + jnp.where(chip >= apart, 0.0, NEG)) * state[0]
        if apart * cores < len(packs):
            between = between + sum_of_parts(parts[0][rows + share :, :])
    for ref in states:
        passed = jnp.exp(sum_of_parts(ref[width:, :])) * carried + ref[:width, :].astype(F32)
        carried = jnp.where(upper, passed, carried)
    return carried.astype(BF16)


def weighted_values(pack_refs, places, probs_ref, mine, rows, width):
    out = None
    for place, pack_ref in zip(places, pack_refs):
        value_t = side_by_side(pack_ref, rows, width)
        term = dot(value_t, probs_ref[place * rows : (place + 1) * rows, mine])
        out = term if out is None else out + term
    return out


def write_out(step, carried, places, pack_refs, refs, outs, buffers, sems):
    lin_qt_ref, intra_ref, cum_row_ref, summed_ref, factor_ref, sum_ref, probs_ref = refs
    width, rows = lin_qt_ref.shape
    linear_buffer, softmax_buffer = buffers
    softmax_copy, linear_copy = (
        pltpu.make_async_copy(buffer, out, sems.at[place])
        for place, (buffer, out) in enumerate(((softmax_buffer, outs[1]), (linear_buffer, outs[0])))
    )
    for start in range(0, rows, step):
        mine = slice(start, start + step)
        summed = summed_ref[:, mine]
        if factor_ref is not None:
            summed = summed * factor_ref[:, mine]
        more = weighted_values(pack_refs, places, probs_ref, mine, rows, width)
        summed = summed if more is None else summed + more
        softmax_buffer[mine, :] = jnp.transpose((summed / sum_ref[:, mine]).astype(BF16))
    softmax_copy.start()
    carried = carried()
    for start in range(0, rows, step):
        mine = slice(start, start + step)
        inter = dot(carried, lin_qt_ref[:, mine])
        raw = intra_ref[:, mine] + inter * jnp.exp(cum_row_ref[:, mine])
        square = jnp.sum(raw * raw, axis=0, keepdims=True) * (1.0 / width)
        linear_buffer[mine, :] = jnp.transpose((raw * lax.rsqrt(square + TINY)).astype(BF16))
    linear_copy.start()
    softmax_copy.wait()
    linear_copy.wait()


def early_kernel(step, axis, cores, places, *refs):
    head, refs = refs[:7], refs[7:]
    states, refs = refs[: cores - 1], refs[cores - 1 :]
    values, (linear_ref, softmax_ref, sofar_ref, *scratch) = refs[: len(places)], refs[len(places) :]
    lin_qt_ref, intra_ref, cum_row_ref, summed_ref, factor_ref, sum_ref, probs_ref = head
    width, rows = lin_qt_ref.shape
    position = lax.axis_index(axis)

    @pl.when(position >= cores)
    def _():
        for start in range(0, rows, step):
            mine = slice(start, start + step)
            sofar_ref[:, mine] = summed_ref[:, mine] * factor_ref[:, mine] + weighted_values(
                values, places, probs_ref, mine, rows, width
            )

    @pl.when(position < cores)
    def _():
        own = cores - 1
        write_out(
            step, lambda: carried_state(position, cores, states, (), rows, width),
            places[:own], values[:own], head, (linear_ref, softmax_ref), scratch[:2], scratch[2],
        )


def late_kernel(step, axis, cores, late, *refs):
    refs = refs[2:]
    lin_qt_ref, intra_ref, cum_row_ref, sofar_ref, sum_ref, probs_ref = refs[:6]
    states, refs = refs[6 : 5 + cores], refs[5 + cores :]
    *packs, linear_ref, softmax_ref, linear_buffer, softmax_buffer, sems = refs
    width, rows = lin_qt_ref.shape
    position = lax.axis_index(axis)

    @pl.when(position >= cores)
    def _():
        write_out(
            step, lambda: carried_state(position, cores, states, packs, rows, width),
            late, packs[1::cores] if late else (),
            (lin_qt_ref, intra_ref, cum_row_ref, sofar_ref, None, sum_ref, probs_ref),
            (linear_ref, softmax_ref), (linear_buffer, softmax_buffer), sems,
        )


def keep_in_hbm(x):
    return pltpu.with_memory_space_constraint(x, pltpu.HBM)


def keep_in_vmem(x):
    return pltpu.with_memory_space_constraint(x, VMEM)


def kept_in_vmem(x):
    return VMEM(x.shape, x.dtype)


def kept_in_hbm(x):
    return pltpu.HBM(x.shape, x.dtype)


def call(body, operands, outs, given=(), written=(), resumed=(), scratch=()):
    size = sum(math.prod(x.shape) * x.dtype.itemsize for x in (*given, *operands, *outs))
    inside, outside = pl.BlockSpec(memory_space=VMEM), pl.BlockSpec(memory_space=pl.ANY)
    hbm = (*given, *resumed)
    scratch = [VMEM(x.shape, x.dtype) for x in (*scratch, *written)]
    moved = len(given) + len(written)
    return pl.pallas_call(
        body,
        out_shape=(*map(kept_in_hbm, written), *map(kept_in_vmem, outs)),
        in_specs=[outside] * len(hbm) + [inside] * len(operands),
        out_specs=(*[outside] * len(written), *[inside] * len(outs)),
        scratch_shapes=[*scratch, pltpu.SemaphoreType.DMA((moved,))] if moved else [],
        input_output_aliases={place: place for place in range(len(resumed))},
        cost_estimate=pl.CostEstimate(flops=0, bytes_accessed=size, transcendentals=0),
        compiler_params=pltpu.CompilerParams(vmem_limit_bytes=KERNEL_VMEM),
    )(*map(keep_in_hbm, hbm), *map(keep_in_vmem, operands))


def on_device(axis, lin_query, lin_key, lin_value, log_decay, soft_query, soft_key, soft_value):
    rows, heads, width = lin_query.shape
    count = lax.axis_size(axis)
    cores = 2 if count % 2 == 0 else 1
    chips = count // cores

    def across(x, apart):
        return lax.ppermute(x, axis, [(i, (i + apart * cores) % count) for i in range(count)])

    def swapped(x, after=None):
        if after is not None:
            x, _ = lax.optimization_barrier((x, after))
        return lax.ppermute(x, axis, [(i, i ^ 1) for i in range(count)])

    def near(x):
        return [swapped(x)] if cores == 2 else []

    def far(x):
        return [across(x, apart) for apart in range(1, chips)]

    def completed(blocks, after):
        out = []
        for block in blocks:
            out.append(block)
            if cores == 2:
                out.append(swapped(block, after))
        return out

    def one_head(lq, lk, lv, decay, sq, sk, sv):
        step = math.gcd(rows, 256)
        scale = math.log2(math.e) / math.sqrt(width)
        ring = (axis, cores, chips)

        def shape(*dims, dtype=F32):
            return jax.ShapeDtypeStruct(dims, dtype)

        def half(*dims):
            return shape(*dims, dtype=BF16)

        row, flat, flat16, block = shape(1, rows), shape(width, rows), half(width, rows), half(rows, width)
        packed = half(rows + width // cores + (PAD if chips > 2 else 0), width)
        keys = far(sk)
        soft_vt, state, cum_row, cum_col, lin_vt, lk, lq, sq, own_keys = call(
            state_kernel,
            (),
            (block, half(width + PAD, width), row, shape(rows, width), flat16, block, block, block, block),
            given=(decay, lk, lv, sv, lq, sq, sk),
            scratch=(row, block, block),
        )
        states = near(state)
        qt, top, total, summed = call(
            functools.partial(soft_kernel, scale, step), (sq, own_keys, soft_vt), (flat16, row, row, flat)
        )
        (states, lin_vt), _ = lax.optimization_barrier(((states, lin_vt), summed))
        (pack,) = call(
            functools.partial(combine_kernel, axis, cores), (state, *states, soft_vt), (packed,)
        )
        packs = far(pack)
        (lq, lk), _ = lax.optimization_barrier(((lq, lk), keys))
        keys, near_values = [*near(sk), *completed(keys, summed)], near(soft_vt)
        lin_qt, intra = call(
            functools.partial(linear_kernel, step), (lq, lk, lin_vt, cum_row, cum_col), (flat16, flat)
        )
        top, _ = lax.optimization_barrier((top, (intra, near_values)))
        probs, factor, sums = call(
            functools.partial(score_kernel, scale, step, *ring),
            (qt, top, total, *keys),
            (half(len(keys) * rows, rows), row, row),
        )
        packs = completed(packs, factor)
        blocks = [*near_values, *packs]
        late = tuple(range(cores, len(blocks), cores)) if cores == 2 else ()
        early = tuple(place for place in range(len(blocks)) if place not in late)
        *began, sofar = call(
            functools.partial(early_kernel, step, axis, cores, early),
            (
                lin_qt, intra, cum_row, summed, factor, sums, probs,
                *states, *(blocks[place] for place in early),
            ),
            (flat,),
            written=(block, block),
        )
        return call(
            functools.partial(late_kernel, step, axis, cores, late),
            (lin_qt, intra, cum_row, sofar, sums, probs, *states, *packs),
            (),
            written=(block, block),
            resumed=began,
        )

    outs = [
        one_head(
            *(x[:, head] for x in (lin_query, lin_key, lin_value)),
            log_decay[head : head + 1],
            *(x[:, head] for x in (soft_query, soft_key, soft_value)),
        )
        for head in range(heads)
    ]
    linear = jnp.stack([pair[0] for pair in outs], axis=1)
    softmax = jnp.stack([pair[1] for pair in outs], axis=1)
    return linear, softmax


def solution(mesh):
    block = P("ctx", "tp", None)
    return jax.shard_map(
        functools.partial(on_device, "ctx"),
        mesh=mesh,
        in_specs=(block, block, block, P("tp", "ctx"), block, block, block),
        out_specs=(block, block),
        check_vma=False,
    )
```

```python
import functools
import math

import jax
import jax.numpy as jnp
from jax import lax
from jax.experimental import pallas as pl
from jax.experimental.pallas import tpu as pltpu
from jax.sharding import PartitionSpec as P

NEG = -1e30
TINY = 1e-6
PAD = 16
KERNEL_VMEM = 16 * 2**20
F32 = jnp.float32
BF16 = jnp.bfloat16
VMEM = pltpu.VMEM


def dot(a, b):
    return lax.dot_general(a, b, (((1,), (0,)), ((), ())), preferred_element_type=F32)


def three_parts(x):
    high = x.astype(BF16)
    rest = x - high.astype(F32)
    middle = rest.astype(BF16)
    low = (rest - middle.astype(F32)).astype(BF16)
    return high, middle, low


def iota(shape, dim):
    return lax.broadcasted_iota(jnp.int32, shape, dim)


def select_rows(parts, rows, width):
    row = iota((rows, width), 0)
    out = jnp.zeros((rows, width), F32)
    for number, part in enumerate(parts):
        out = jnp.where(row == number, part.astype(F32), out)
    return out.astype(BF16)


def side_by_side(ref, rows, width):
    pieces = [ref[left : left + width, :] for left in range(0, rows, width)]
    return pieces[0] if len(pieces) == 1 else jnp.concatenate(pieces, axis=1)


def state_kernel(
    decay_hbm, key_hbm, value_hbm, soft_value_hbm, query_hbm, soft_query_hbm, soft_key_hbm,
    pack_ref, state_ref, cum_row_ref, cum_col_ref, value_t_ref, key_ref, query_ref, soft_query_ref, soft_key_ref,
    decay_ref, value_ref, soft_value_ref, sems,
):
    rows, width = key_ref.shape
    copies = [
        pltpu.make_async_copy(source, target, sems.at[place])
        for place, (source, target) in enumerate(
            (
                (decay_hbm, decay_ref),
                (key_hbm, key_ref),
                (value_hbm, value_ref),
                (soft_value_hbm, soft_value_ref),
                (soft_query_hbm, soft_query_ref),
                (soft_key_hbm, soft_key_ref),
                (query_hbm, query_ref),
            )
        )
    ]
    for copy in copies:
        copy.start()
    upto = (iota((rows, rows), 0) <= iota((rows, rows), 1)).astype(F32).astype(BF16)
    copies[0].wait()
    parts = select_rows(three_parts(decay_ref[...]), PAD, rows)
    cum_row = jnp.sum(dot(parts, upto), axis=0, keepdims=True)
    cum_row_ref[...] = cum_row
    cum_col = jnp.transpose(jnp.broadcast_to(cum_row, (width, rows)))
    cum_col_ref[...] = cum_col
    total = cum_col[rows - 1 :, :]
    for copy in copies[1:4]:
        copy.wait()
    decayed = (key_ref[...].astype(F32) * jnp.exp(total - cum_col)).astype(BF16)
    value_t = jnp.transpose(value_ref[...])
    value_t_ref[...] = value_t
    state_t = dot(value_t, decayed).astype(BF16)
    tail = select_rows(three_parts(total), PAD, width)
    state_ref[:width, :] = state_t
    state_ref[width:, :] = tail
    for left in range(0, rows, width):
        pack_ref[left : left + width, :] = jnp.transpose(soft_value_ref[left : left + width, :])
    pack_ref[rows : rows + width, :] = state_t
    pack_ref[rows + width :, :] = tail
    for copy in copies[4:]:
        copy.wait()


def soft_kernel(scale, step, q_ref, k_ref, pack_ref, qt_ref, top_ref, total_ref, summed_ref):
    rows, width = q_ref.shape
    qt_ref[...] = jnp.transpose(q_ref[...])
    value_t = side_by_side(pack_ref, rows, width)
    keep = iota((step, step), 0) <= iota((step, step), 1)
    for start in range(0, rows, step):
        stop = start + step
        scores = dot(k_ref[:stop, :], qt_ref[:, start:stop])
        last = jnp.where(keep, scores[start:, :], NEG)
        scores = jnp.concatenate([scores[:start, :], last], axis=0) if start else last
        top = jnp.max(scores, axis=0, keepdims=True)
        probs = jnp.exp2((scores - top) * scale)
        top_ref[:, start:stop] = top
        total_ref[:, start:stop] = jnp.sum(probs, axis=0, keepdims=True)
        summed_ref[:, start:stop] = dot(value_t[:, :stop], probs.astype(BF16))


def linear_kernel(step, q_ref, k_ref, value_t_ref, cum_row_ref, cum_col_ref, qt_ref, intra_ref):
    rows, width = q_ref.shape
    qt_ref[...] = jnp.transpose(q_ref[...])
    keep = iota((step, step), 0) <= iota((step, step), 1)
    for start in range(0, rows, step):
        stop = start + step
        scores = dot(k_ref[:stop, :], qt_ref[:, start:stop])
        cum_t = cum_row_ref[:, start:stop]
        cum_s = jnp.concatenate([cum_col_ref[:stop, :]] * (step // width), axis=1)
        diff = cum_t - cum_s
        last = jnp.where(keep, diff[start:, :], NEG)
        diff = jnp.concatenate([diff[:start, :], last], axis=0) if start else last
        weights = (scores * jnp.exp(diff)).astype(BF16)
        intra_ref[:, start:stop] = dot(value_t_ref[:, :stop], weights)


def block_numbers(axis, cores, chips):
    position = lax.axis_index(axis)
    if cores == 1:
        return position, [position - apart for apart in range(1, chips)]
    other = lax.rem(position, 2)
    partner = position + 1 - 2 * other
    numbers = [jnp.where(other == 1, position - 1, -1)]
    for apart in range(1, chips):
        numbers += [position - 2 * apart, partner - 2 * apart]
    return position, numbers


def by_chip(position, cores, count, body):
    pl.when(position >= cores)(lambda: body(count))
    pl.when(position < cores)(lambda: body(cores - 1))


def score_kernel(scale, step, axis, cores, chips, qt_ref, top_ref, total_ref, *refs):
    *key_refs, probs_ref, factor_ref, sum_ref = refs
    rows = qt_ref.shape[1]
    position, numbers = block_numbers(axis, cores, chips)
    away = [jnp.where(number >= 0, 0.0, NEG) for number in numbers]

    def body(count):
        for start in range(0, rows, step):
            mine = slice(start, start + step)
            query = qt_ref[:, mine]
            old = top_ref[:, mine]
            scores = [dot(key_ref[...], query) for key_ref in key_refs[:count]]
            top = old
            for score, off in zip(scores, away):
                top = jnp.maximum(top, jnp.max(score, axis=0, keepdims=True) + off)
            factor = jnp.exp2((old - top) * scale)
            total = total_ref[:, mine] * factor
            for number, (score, off) in enumerate(zip(scores, away)):
                probs = jnp.exp2((score - (top - off)) * scale)
                total = total + jnp.sum(probs, axis=0, keepdims=True)
                probs_ref[number * rows : (number + 1) * rows, mine] = probs.astype(BF16)
            factor_ref[:, mine] = factor
            sum_ref[:, mine] = total

    by_chip(position, cores, len(key_refs), body)


def carried_state(numbers, parts, width):
    totals, states = [], []
    for part in parts:
        tail = part[width:, :].astype(F32)
        totals.append(tail[0:1] + tail[1:2] + tail[2:3])
        states.append(part[:width, :].astype(F32))
    carried = jnp.zeros((width, width), F32)
    for number, state in zip(numbers, states):
        between = jnp.where(number >= 0, 0.0, NEG)
        for other, total in zip(numbers, totals):
            between = between + jnp.where(other > number, 1.0, 0.0) * total
        carried = carried + jnp.exp(between) * state
    return carried.astype(BF16)


def put_linear(step, carried, qt_ref, intra_ref, cum_row_ref, buffer):
    width, rows = qt_ref.shape
    for start in range(0, rows, step):
        mine = slice(start, start + step)
        inter = dot(carried, qt_ref[:, mine])
        raw = intra_ref[:, mine] + inter * jnp.exp(cum_row_ref[:, mine])
        square = jnp.sum(raw * raw, axis=0, keepdims=True) * (1.0 / width)
        buffer[mine, :] = jnp.transpose((raw * lax.rsqrt(square + TINY)).astype(BF16))


def put_softmax(step, sofar, values_t, places, probs_ref, sum_ref, buffer):
    rows = sum_ref.shape[1]
    for start in range(0, rows, step):
        mine = slice(start, start + step)
        summed = sofar(mine)
        for place, value_t in zip(places, values_t):
            summed = summed + dot(value_t, probs_ref[place * rows : (place + 1) * rows, mine])
        buffer[mine, :] = jnp.transpose((summed / sum_ref[:, mine]).astype(BF16))


def finish_kernel(step, axis, cores, chips, *refs):
    lin_qt_ref, intra_ref, cum_row_ref, summed_ref, factor_ref, sum_ref, probs_ref = refs[:7]
    *received, linear_ref, softmax_ref, linear_buffer, softmax_buffer, sems = refs[7:]
    near, received = received[: cores - 1], received[cores - 1 :]
    states, values = received[: len(received) // 2], received[len(received) // 2 :]
    width, rows = lin_qt_ref.shape
    position, numbers = block_numbers(axis, cores, chips)
    linear_copy = pltpu.make_async_copy(linear_buffer, linear_ref, sems.at[0])
    softmax_copy = pltpu.make_async_copy(softmax_buffer, softmax_ref, sems.at[1])

    def body(count):
        parts = [ref[rows:, :] for ref in near] + [ref[...] for ref in states]
        put_linear(
            step, carried_state(numbers, parts[:count], width), lin_qt_ref, intra_ref, cum_row_ref, linear_buffer
        )
        linear_copy.start()
        values_t = [side_by_side(ref, rows, width) for ref in near]
        values_t += [jnp.transpose(ref[...]) for ref in values[: count - len(near)]]
        put_softmax(
            step, lambda mine: summed_ref[:, mine] * factor_ref[:, mine],
            values_t, range(count), probs_ref, sum_ref, softmax_buffer,
        )
        softmax_copy.start()
        linear_copy.wait()
        softmax_copy.wait()

    by_chip(position, cores, len(near) + len(values), body)


def keep_in_hbm(x):
    return pltpu.with_memory_space_constraint(x, pltpu.HBM)


def keep_in_vmem(x):
    return pltpu.with_memory_space_constraint(x, VMEM)


def kept_in_vmem(x):
    return VMEM(x.shape, x.dtype)


def kept_in_hbm(x):
    return pltpu.HBM(x.shape, x.dtype)


def call(body, operands, outs, given=(), written=(), resumed=(), scratch=()):
    size = sum(math.prod(x.shape) * x.dtype.itemsize for x in (*given, *operands, *outs))
    inside, outside = pl.BlockSpec(memory_space=VMEM), pl.BlockSpec(memory_space=pl.ANY)
    hbm = (*given, *resumed)
    scratch = [VMEM(x.shape, x.dtype) for x in (*scratch, *written)]
    moved = len(given) + len(written)
    return pl.pallas_call(
        body,
        out_shape=(*map(kept_in_hbm, written), *map(kept_in_vmem, outs)),
        in_specs=[outside] * len(hbm) + [inside] * len(operands),
        out_specs=(*[outside] * len(written), *[inside] * len(outs)),
        scratch_shapes=[*scratch, pltpu.SemaphoreType.DMA((moved,))] if moved else [],
        input_output_aliases={place: place for place in range(len(resumed))},
        cost_estimate=pl.CostEstimate(flops=0, bytes_accessed=size, transcendentals=0),
        compiler_params=pltpu.CompilerParams(vmem_limit_bytes=KERNEL_VMEM),
    )(*map(keep_in_hbm, hbm), *map(keep_in_vmem, operands))


def on_device(axis, lin_query, lin_key, lin_value, log_decay, soft_query, soft_key, soft_value):
    rows, heads, width = lin_query.shape
    count = lax.axis_size(axis)
    cores = 2 if count % 2 == 0 else 1
    chips = count // cores

    def across(x, apart):
        return lax.ppermute(x, axis, [(i, (i + apart * cores) % count) for i in range(count)])

    def swapped(x):
        return lax.ppermute(x, axis, [(i, i ^ 1) for i in range(count)])

    def near(x):
        return [swapped(x)] if cores == 2 else []

    def far(x):
        return [across(x, apart) for apart in range(1, chips)]

    def completed(blocks, after=None):
        out = []
        for block in blocks:
            out.append(block)
            if cores == 2:
                if after is not None:
                    block, _ = lax.optimization_barrier((block, after))
                out.append(swapped(block))
        return out

    def one_head(lq, lk, lv, decay, sq, sk, sv):
        step = math.gcd(rows, 256)
        scale = math.log2(math.e) / math.sqrt(width)
        ring = (axis, cores, chips)

        def shape(*dims, dtype=F32):
            return jax.ShapeDtypeStruct(dims, dtype)

        def half(*dims):
            return shape(*dims, dtype=BF16)

        row, flat, flat16, block = shape(1, rows), shape(width, rows), half(width, rows), half(rows, width)
        keys, values = far(sk), far(sv)
        pack, state, cum_row, cum_col, lin_vt, lk, lq, sq, own_keys = call(
            state_kernel,
            (),
            (
                half(rows + width + PAD, width), half(width + PAD, width),
                row, shape(rows, width), flat16, block, block, block, block,
            ),
            given=(decay, lk, lv, sv, lq, sq, sk),
            scratch=(row, block, block),
        )
        states, near_packs = far(state), near(pack)
        qt, top, total, summed = call(
            functools.partial(soft_kernel, scale, step), (sq, own_keys, pack), (flat16, row, row, flat)
        )
        lin_qt, intra = call(
            functools.partial(linear_kernel, step), (lq, lk, lin_vt, cum_row, cum_col), (flat16, flat)
        )
        sent, _ = lax.optimization_barrier((sk, summed))
        keys = [*near(sent), *completed(keys, (summed, intra))]
        values, states = completed(values, (summed, intra, states)), completed(states, (summed, intra))
        probs, factor, sums = call(
            functools.partial(score_kernel, scale, step, *ring),
            (qt, top, total, *keys),
            (half(len(keys) * rows, rows), row, row),
        )
        return call(
            functools.partial(finish_kernel, step, *ring),
            (lin_qt, intra, cum_row, summed, factor, sums, probs, *near_packs, *states, *values),
            (),
            written=(block, block),
        )

    outs = [
        one_head(
            *(x[:, head] for x in (lin_query, lin_key, lin_value)),
            log_decay[head : head + 1],
            *(x[:, head] for x in (soft_query, soft_key, soft_value)),
        )
        for head in range(heads)
    ]
    linear = jnp.stack([pair[0] for pair in outs], axis=1)
    softmax = jnp.stack([pair[1] for pair in outs], axis=1)
    return linear, softmax


def solution(mesh):
    block = P("ctx", "tp", None)
    return jax.shard_map(
        functools.partial(on_device, "ctx"),
        mesh=mesh,
        in_specs=(block, block, block, P("tp", "ctx"), block, block, block),
        out_specs=(block, block),
        check_vma=False,
    )
```

```python
import functools
import math

import jax
import jax.numpy as jnp
from jax import lax
from jax.experimental import pallas as pl
from jax.experimental.pallas import tpu as pltpu
from jax.sharding import PartitionSpec as P

NEG = -1e30
TINY = 1e-6
PAD = 16
KERNEL_VMEM = 16 * 2**20
F32 = jnp.float32
BF16 = jnp.bfloat16
VMEM = pltpu.VMEM


def dot(a, b):
    return lax.dot_general(a, b, (((1,), (0,)), ((), ())), preferred_element_type=F32)


def three_parts(x):
    high = x.astype(BF16)
    rest = x - high.astype(F32)
    middle = rest.astype(BF16)
    low = (rest - middle.astype(F32)).astype(BF16)
    return high, middle, low


def iota(shape, dim):
    return lax.broadcasted_iota(jnp.int32, shape, dim)


def select_rows(parts, rows, width):
    row = iota((rows, width), 0)
    out = jnp.zeros((rows, width), F32)
    for number, part in enumerate(parts):
        out = jnp.where(row == number, part.astype(F32), out)
    return out.astype(BF16)


def side_by_side(ref, rows, width):
    pieces = [ref[left : left + width, :] for left in range(0, rows, width)]
    return pieces[0] if len(pieces) == 1 else jnp.concatenate(pieces, axis=1)


def state_kernel(
    decay_hbm, key_hbm, value_hbm, soft_value_hbm, query_hbm, soft_query_hbm, soft_key_hbm,
    soft_vt_ref, state_ref, cum_row_ref, cum_col_ref, value_t_ref, key_ref, query_ref, soft_query_ref, soft_key_ref,
    decay_ref, value_ref, soft_value_ref, sems,
):
    copies = [
        pltpu.make_async_copy(source, target, sems.at[place])
        for place, (source, target) in enumerate(
            (
                (decay_hbm, decay_ref),
                (key_hbm, key_ref),
                (value_hbm, value_ref),
                (soft_value_hbm, soft_value_ref),
                (soft_query_hbm, soft_query_ref),
                (soft_key_hbm, soft_key_ref),
                (query_hbm, query_ref),
            )
        )
    ]
    for copy in copies:
        copy.start()
    rows, width = key_ref.shape
    upto = (iota((rows, rows), 0) <= iota((rows, rows), 1)).astype(F32).astype(BF16)
    copies[0].wait()
    parts = select_rows(three_parts(decay_ref[...]), PAD, rows)
    cum_row = jnp.sum(dot(parts, upto), axis=0, keepdims=True)
    cum_row_ref[...] = cum_row
    cum_col = jnp.transpose(jnp.broadcast_to(cum_row, (width, rows)))
    cum_col_ref[...] = cum_col
    total = cum_col[rows - 1 :, :]
    for copy in copies[1:4]:
        copy.wait()
    decayed = (key_ref[...].astype(F32) * jnp.exp(total - cum_col)).astype(BF16)
    value_t = jnp.transpose(value_ref[...])
    value_t_ref[...] = value_t
    state_ref[:width, :] = dot(value_t, decayed).astype(BF16)
    state_ref[width:, :] = select_rows(three_parts(total), PAD, width)
    for left in range(0, rows, width):
        soft_vt_ref[left : left + width, :] = jnp.transpose(soft_value_ref[left : left + width, :])
    for copy in copies[4:]:
        copy.wait()


def sum_of_parts(tail):
    tail = tail.astype(F32)
    return tail[0:1] + tail[1:2] + tail[2:3]


def combine_kernel(axis, cores, *refs):
    *state_refs, soft_vt_ref, pack_ref = refs
    rows, width = soft_vt_ref.shape
    share = width // cores
    pack_ref[:rows, :] = soft_vt_ref[...]
    states = [ref[:width, :].astype(F32) for ref in state_refs]
    totals = [sum_of_parts(ref[width:, :]) for ref in state_refs]
    state, total = states[0], totals[0]
    if cores == 2:
        upper = lax.rem(lax.axis_index(axis), 2) == 1
        first, second = jnp.where(upper, states[1], state), jnp.where(upper, state, states[1])
        state = jnp.exp(jnp.where(upper, total, totals[1])) * first + second
        state = jnp.where(upper, state[share:], state[:share])
        total = total + totals[1]
    pack_ref[rows : rows + share, :] = state.astype(BF16)
    if pack_ref.shape[0] > rows + share:
        pack_ref[rows + share :, :] = select_rows(three_parts(total), PAD, width)


def sum_of_parts(tail):
    tail = tail.astype(F32)
    return tail[0:1] + tail[1:2] + tail[2:3]


def combine_kernel(axis, cores, *refs):
    *state_refs, share_ref = refs
    width = share_ref.shape[1]
    states = [ref[:width, :].astype(F32) for ref in state_refs]
    totals = [sum_of_parts(ref[width:, :]) for ref in state_refs]
    state, total = states[0], totals[0]
    if cores == 2:
        upper = lax.rem(lax.axis_index(axis), 2) == 1
        first, second = jnp.where(upper, states[1], state), jnp.where(upper, state, states[1])
        state = jnp.exp(jnp.where(upper, total, totals[1])) * first + second
        total = total + totals[1]
    share_ref[:width, :] = state.astype(BF16)
    if share_ref.shape[0] > width:
        share_ref[width:, :] = select_rows(three_parts(total), PAD, width)


def soft_kernel(scale, step, q_ref, k_ref, pack_ref, qt_ref, top_ref, total_ref, summed_ref):
    rows, width = q_ref.shape
    qt_ref[...] = jnp.transpose(q_ref[...])
    value_t = side_by_side(pack_ref, rows, width)
    keep = iota((step, step), 0) <= iota((step, step), 1)
    for start in range(0, rows, step):
        stop = start + step
        scores = dot(k_ref[:stop, :], qt_ref[:, start:stop])
        last = jnp.where(keep, scores[start:, :], NEG)
        scores = jnp.concatenate([scores[:start, :], last], axis=0) if start else last
        top = jnp.max(scores, axis=0, keepdims=True)
        probs = jnp.exp2((scores - top) * scale)
        top_ref[:, start:stop] = top
        total_ref[:, start:stop] = jnp.sum(probs, axis=0, keepdims=True)
        summed_ref[:, start:stop] = dot(value_t[:, :stop], probs.astype(BF16))


def linear_kernel(step, q_ref, k_ref, value_t_ref, cum_row_ref, cum_col_ref, qt_ref, intra_ref):
    rows, width = q_ref.shape
    qt_ref[...] = jnp.transpose(q_ref[...])
    keep = iota((step, step), 0) <= iota((step, step), 1)
    for start in range(0, rows, step):
        stop = start + step
        scores = dot(k_ref[:stop, :], qt_ref[:, start:stop])
        cum_t = cum_row_ref[:, start:stop]
        cum_s = jnp.concatenate([cum_col_ref[:stop, :]] * (step // width), axis=1)
        diff = cum_t - cum_s
        last = jnp.where(keep, diff[start:, :], NEG)
        diff = jnp.concatenate([diff[:start, :], last], axis=0) if start else last
        weights = (scores * jnp.exp(diff)).astype(BF16)
        intra_ref[:, start:stop] = dot(value_t_ref[:, :stop], weights)


def by_chip(position, cores, count, body):
    pl.when(position >= cores)(lambda: body(count))
    pl.when(position < cores)(lambda: body(cores - 1))


def score_kernel(scale, step, axis, cores, offsets, qt_ref, top_ref, total_ref, *refs):
    key_refs, (probs_ref, new_top_ref, factor_ref, sum_ref) = refs[:-4], refs[-4:]
    rows = qt_ref.shape[1]
    position = lax.axis_index(axis)
    chip = position // cores
    away = [
        jnp.where(position - chip * cores >= 1 if apart == 0 else chip >= apart, 0.0, NEG) for apart in offsets
    ]

    def body(count):
        for start in range(0, rows, step):
            mine = slice(start, start + step)
            query = qt_ref[:, mine]
            old = top_ref[:, mine]
            scores = [dot(key_ref[...], query) for key_ref in key_refs[:count]]
            top = old
            for score, off in zip(scores, away):
                top = jnp.maximum(top, jnp.max(score, axis=0, keepdims=True) + off)
            factor = jnp.exp2((old - top) * scale)
            total = total_ref[:, mine] * factor
            for place, (score, off) in enumerate(zip(scores, away)):
                probs = jnp.exp2((score - (top - off)) * scale)
                total = total + jnp.sum(probs, axis=0, keepdims=True)
                probs_ref[place * rows : (place + 1) * rows, mine] = probs.astype(BF16)
            new_top_ref[:, mine] = top
            factor_ref[:, mine] = factor
            sum_ref[:, mine] = total

    pl.when(chip >= 1)(lambda: body(len(offsets)))
    pl.when(chip < 1)(lambda: body(offsets.count(0)))


def carried_state(position, cores, near, shares, width):
    chip = position // cores
    carried = jnp.zeros((width, width), F32)
    between = jnp.zeros((1, width), F32)
    for apart, ref in enumerate(shares, 1):
        carried = carried + jnp.exp(between + jnp.where(chip >= apart, 0.0, NEG)) * ref[:width, :].astype(F32)
        if ref.shape[0] > width:
            between = between + sum_of_parts(ref[width:, :])
    for ref in near:
        passed = jnp.exp(sum_of_parts(ref[width:, :])) * carried + ref[:width, :].astype(F32)
        carried = jnp.where(position - chip * cores == 1, passed, carried)
    return carried.astype(BF16)


def put_linear(step, carried, qt_ref, intra_ref, cum_row_ref, buffer):
    width, rows = qt_ref.shape
    for start in range(0, rows, step):
        mine = slice(start, start + step)
        inter = dot(carried, qt_ref[:, mine])
        raw = intra_ref[:, mine] + inter * jnp.exp(cum_row_ref[:, mine])
        square = jnp.sum(raw * raw, axis=0, keepdims=True) * (1.0 / width)
        buffer[mine, :] = jnp.transpose((raw * lax.rsqrt(square + TINY)).astype(BF16))


def value_sum(values_t, probs_ref, mine):
    rows = values_t[0].shape[1]
    terms = [
        dot(value_t, probs_ref[place * rows : (place + 1) * rows, mine]) for place, value_t in enumerate(values_t)
    ]
    return functools.reduce(jnp.add, terms)


def early_kernel(step, axis, cores, counts, *refs):
    lin_qt_ref, intra_ref, cum_row_ref, summed_ref, factor_ref, sum_ref, probs_ref, late_factor_ref = refs[:8]
    linear_ref, softmax_ref, sofar_ref, linear_buffer, softmax_buffer, sems = refs[-6:]
    received, groups = list(refs[8:-6]), []
    for count in counts:
        groups.append(received[:count])
        received = received[count:]
    near_states, shares, near_values, values = groups
    width, rows = lin_qt_ref.shape
    position = lax.axis_index(axis)
    linear_copy = pltpu.make_async_copy(linear_buffer, linear_ref, sems.at[0])
    softmax_copy = pltpu.make_async_copy(softmax_buffer, softmax_ref, sems.at[1])

    def body(count):
        first = count == len(near_values)
        carried = carried_state(position, cores, near_states, () if first else shares, width)
        put_linear(step, carried, lin_qt_ref, intra_ref, cum_row_ref, linear_buffer)
        linear_copy.start()
        values_t = [side_by_side(ref, rows, width) for ref in near_values]
        values_t += [jnp.transpose(ref[...]) for ref in values[: count - len(near_values)]]
        for start in range(0, rows, step):
            mine = slice(start, start + step)
            summed = summed_ref[:, mine] * factor_ref[:, mine]
            if values_t:
                summed = summed + value_sum(values_t, probs_ref, mine)
            if first:
                softmax_buffer[mine, :] = jnp.transpose((summed / sum_ref[:, mine]).astype(BF16))
            else:
                sofar_ref[:, mine] = summed * late_factor_ref[:, mine]
        if first:
            softmax_copy.start()
            softmax_copy.wait()
        linear_copy.wait()

    by_chip(position, cores, len(near_values) + len(values), body)


def late_kernel(step, axis, cores, *refs):
    sofar_ref, sum_ref, probs_ref, *values, softmax_ref, softmax_buffer, sems = refs[1:]
    rows = sum_ref.shape[1]

    @pl.when(lax.axis_index(axis) >= cores)
    def _():
        softmax_copy = pltpu.make_async_copy(softmax_buffer, softmax_ref, sems.at[0])
        values_t = [jnp.transpose(ref[...]) for ref in values]
        for start in range(0, rows, step):
            mine = slice(start, start + step)
            summed = sofar_ref[:, mine]
            if values_t:
                summed = summed + value_sum(values_t, probs_ref, mine)
            softmax_buffer[mine, :] = jnp.transpose((summed / sum_ref[:, mine]).astype(BF16))
        softmax_copy.start()
        softmax_copy.wait()


def keep_in_hbm(x):
    return pltpu.with_memory_space_constraint(x, pltpu.HBM)


def keep_in_vmem(x):
    return pltpu.with_memory_space_constraint(x, VMEM)


def kept_in_vmem(x):
    return VMEM(x.shape, x.dtype)


def kept_in_hbm(x):
    return pltpu.HBM(x.shape, x.dtype)


def call(body, operands, outs, given=(), written=(), resumed=(), scratch=()):
    size = sum(math.prod(x.shape) * x.dtype.itemsize for x in (*given, *operands, *outs))
    inside, outside = pl.BlockSpec(memory_space=VMEM), pl.BlockSpec(memory_space=pl.ANY)
    hbm = (*given, *resumed)
    scratch = [VMEM(x.shape, x.dtype) for x in (*scratch, *written)]
    moved = len(given) + len(written)
    return pl.pallas_call(
        body,
        out_shape=(*map(kept_in_hbm, written), *map(kept_in_vmem, outs)),
        in_specs=[outside] * len(hbm) + [inside] * len(operands),
        out_specs=(*[outside] * len(written), *[inside] * len(outs)),
        scratch_shapes=[*scratch, pltpu.SemaphoreType.DMA((moved,))] if moved else [],
        input_output_aliases={place: place for place in range(len(resumed))},
        cost_estimate=pl.CostEstimate(flops=0, bytes_accessed=size, transcendentals=0),
        compiler_params=pltpu.CompilerParams(vmem_limit_bytes=KERNEL_VMEM),
    )(*map(keep_in_hbm, hbm), *map(keep_in_vmem, operands))


def on_device(axis, lin_query, lin_key, lin_value, log_decay, soft_query, soft_key, soft_value):
    rows, heads, width = lin_query.shape
    count = lax.axis_size(axis)
    cores = 2 if count % 2 == 0 else 1
    chips = count // cores

    def across(x, apart):
        return lax.ppermute(x, axis, [(i, (i + apart * cores) % count) for i in range(count)])

    def swapped(x):
        return lax.ppermute(x, axis, [(i, i ^ 1) for i in range(count)])

    def near(blocks):
        return [swapped(block) for block in blocks] if cores == 2 else []

    def far(x):
        return [across(x, apart) for apart in range(1, chips)]

    def passed(blocks, after):
        return near(lax.optimization_barrier((block, after))[0] for block in blocks)

    def one_head(lq, lk, lv, decay, sq, sk, sv):
        step = math.gcd(rows, 256)
        scale = math.log2(math.e) / math.sqrt(width)

        def shape(*dims, dtype=F32):
            return jax.ShapeDtypeStruct(dims, dtype)

        def half(*dims):
            return shape(*dims, dtype=BF16)

        row, flat, flat16, block = shape(1, rows), shape(width, rows), half(width, rows), half(rows, width)
        keys, values = far(sk), far(sv)
        soft_vt, state, cum_row, cum_col, lin_vt, lk, lq, sq, own_keys = call(
            state_kernel,
            (),
            (block, half(width + PAD, width), row, shape(rows, width), flat16, block, block, block, block),
            given=(decay, lk, lv, sv, lq, sq, sk),
            scratch=(row, block, block),
        )
        near_states, near_values = near([state]), near([soft_vt])
        qt, top, total, summed = call(
            functools.partial(soft_kernel, scale, step), (sq, own_keys, soft_vt), (flat16, row, row, flat)
        )
        near_states, _ = lax.optimization_barrier((near_states, summed))
        (share,) = call(
            functools.partial(combine_kernel, axis, cores),
            (state, *near_states),
            (half(width + (PAD if chips > 2 else 0), width),),
        )
        shares = far(share)
        lin_qt, intra = call(
            functools.partial(linear_kernel, step), (lq, lk, lin_vt, cum_row, cum_col), (flat16, flat)
        )

        def scored(top, total, blocks, offsets):
            return call(
                functools.partial(score_kernel, scale, step, axis, cores, offsets),
                (qt, top, total, *blocks),
                (half(len(blocks) * rows, rows), row, row, row),
            )

        apart = tuple(range(1, chips))
        late_keys = passed(keys, (summed, intra))
        probs, top, factor, sums = scored(top, total, [*near([sk]), *keys], (0,) * (cores - 1) + apart)
        late_values = passed(values, (factor, shares))
        late_keys, _ = lax.optimization_barrier((late_keys, values))
        late_factor, late_sums = jnp.ones_like(factor), sums
        if late_keys:
            late_probs, _, late_factor, late_sums = scored(top, sums, late_keys, apart)
        linear, softmax, sofar = call(
            functools.partial(
                early_kernel, step, axis, cores, [len(x) for x in (near_states, shares, near_values, values)]
            ),
            (
                lin_qt, intra, cum_row, summed, factor, sums, probs, late_factor,
                *near_states, *shares, *near_values, *values,
            ),
            (flat,),
            written=(block, block),
        )
        (softmax,) = call(
            functools.partial(late_kernel, step, axis, cores),
            (sofar, late_sums, late_probs if late_keys else probs, *late_values),
            (),
            written=(block,),
            resumed=(softmax,),
        )
        return linear, softmax

    outs = [
        one_head(
            *(x[:, head] for x in (lin_query, lin_key, lin_value)),
            log_decay[head : head + 1],
            *(x[:, head] for x in (soft_query, soft_key, soft_value)),
        )
        for head in range(heads)
    ]
    linear = jnp.stack([pair[0] for pair in outs], axis=1)
    softmax = jnp.stack([pair[1] for pair in outs], axis=1)
    return linear, softmax


def solution(mesh):
    block = P("ctx", "tp", None)
    return jax.shard_map(
        functools.partial(on_device, "ctx"),
        mesh=mesh,
        in_specs=(block, block, block, P("tp", "ctx"), block, block, block),
        out_specs=(block, block),
        check_vma=False,
    )
```

```python
import functools
import math

import jax
import jax.numpy as jnp
from jax import lax
from jax.experimental import pallas as pl
from jax.experimental.pallas import tpu as pltpu
from jax.sharding import PartitionSpec as P

NEG = -1e30
TINY = 1e-6
PAD = 16
KERNEL_VMEM = 16 * 2**20
F32 = jnp.float32
BF16 = jnp.bfloat16
VMEM = pltpu.VMEM


def dot(a, b):
    return lax.dot_general(a, b, (((1,), (0,)), ((), ())), preferred_element_type=F32)


def three_parts(x):
    high = x.astype(BF16)
    rest = x - high.astype(F32)
    middle = rest.astype(BF16)
    low = (rest - middle.astype(F32)).astype(BF16)
    return high, middle, low


def iota(shape, dim):
    return lax.broadcasted_iota(jnp.int32, shape, dim)


def select_rows(parts, rows, width):
    row = iota((rows, width), 0)
    out = jnp.zeros((rows, width), F32)
    for number, part in enumerate(parts):
        out = jnp.where(row == number, part.astype(F32), out)
    return out.astype(BF16)


def side_by_side(ref, rows, width):
    pieces = [ref[left : left + width, :] for left in range(0, rows, width)]
    return pieces[0] if len(pieces) == 1 else jnp.concatenate(pieces, axis=1)


def state_kernel(
    decay_hbm, key_hbm, value_hbm, soft_value_hbm, query_hbm, soft_query_hbm, soft_key_hbm,
    soft_vt_ref, state_ref, cum_row_ref, cum_col_ref, value_t_ref, key_ref, query_ref, soft_query_ref, soft_key_ref,
    decay_ref, value_ref, soft_value_ref, sems,
):
    copies = [
        pltpu.make_async_copy(source, target, sems.at[place])
        for place, (source, target) in enumerate(
            (
                (decay_hbm, decay_ref),
                (key_hbm, key_ref),
                (value_hbm, value_ref),
                (soft_value_hbm, soft_value_ref),
                (soft_query_hbm, soft_query_ref),
                (soft_key_hbm, soft_key_ref),
                (query_hbm, query_ref),
            )
        )
    ]
    for copy in copies:
        copy.start()
    rows, width = key_ref.shape
    upto = (iota((rows, rows), 0) <= iota((rows, rows), 1)).astype(F32).astype(BF16)
    copies[0].wait()
    parts = select_rows(three_parts(decay_ref[...]), PAD, rows)
    cum_row = jnp.sum(dot(parts, upto), axis=0, keepdims=True)
    cum_row_ref[...] = cum_row
    cum_col = jnp.transpose(jnp.broadcast_to(cum_row, (width, rows)))
    cum_col_ref[...] = cum_col
    total = cum_col[rows - 1 :, :]
    for copy in copies[1:4]:
        copy.wait()
    decayed = (key_ref[...].astype(F32) * jnp.exp(total - cum_col)).astype(BF16)
    value_t = jnp.transpose(value_ref[...])
    value_t_ref[...] = value_t
    state_ref[:width, :] = dot(value_t, decayed).astype(BF16)
    state_ref[width:, :] = select_rows(three_parts(total), PAD, width)
    for left in range(0, rows, width):
        soft_vt_ref[left : left + width, :] = jnp.transpose(soft_value_ref[left : left + width, :])
    for copy in copies[4:]:
        copy.wait()


def sum_of_parts(tail):
    tail = tail.astype(F32)
    return tail[0:1] + tail[1:2] + tail[2:3]


def combine_kernel(axis, cores, *refs):
    *state_refs, soft_vt_ref, pack_ref = refs
    rows, width = soft_vt_ref.shape
    share = width // cores
    pack_ref[:rows, :] = soft_vt_ref[...]
    states = [ref[:width, :].astype(F32) for ref in state_refs]
    totals = [sum_of_parts(ref[width:, :]) for ref in state_refs]
    state, total = states[0], totals[0]
    if cores == 2:
        upper = lax.rem(lax.axis_index(axis), 2) == 1
        first, second = jnp.where(upper, states[1], state), jnp.where(upper, state, states[1])
        state = jnp.exp(jnp.where(upper, total, totals[1])) * first + second
        state = jnp.where(upper, state[share:], state[:share])
        total = total + totals[1]
    pack_ref[rows : rows + share, :] = state.astype(BF16)
    if pack_ref.shape[0] > rows + share:
        pack_ref[rows + share :, :] = select_rows(three_parts(total), PAD, width)


def sum_of_parts(tail):
    tail = tail.astype(F32)
    return tail[0:1] + tail[1:2] + tail[2:3]


def combine_kernel(axis, cores, *refs):
    *state_refs, share_ref = refs
    width = share_ref.shape[1]
    states = [ref[:width, :].astype(F32) for ref in state_refs]
    totals = [sum_of_parts(ref[width:, :]) for ref in state_refs]
    state, total = states[0], totals[0]
    if cores == 2:
        upper = lax.rem(lax.axis_index(axis), 2) == 1
        first, second = jnp.where(upper, states[1], state), jnp.where(upper, state, states[1])
        state = jnp.exp(jnp.where(upper, total, totals[1])) * first + second
        total = total + totals[1]
    share_ref[:width, :] = state.astype(BF16)
    if share_ref.shape[0] > width:
        share_ref[width:, :] = select_rows(three_parts(total), PAD, width)


def soft_kernel(scale, step, q_ref, k_ref, pack_ref, qt_ref, top_ref, total_ref, summed_ref):
    rows, width = q_ref.shape
    qt_ref[...] = jnp.transpose(q_ref[...])
    value_t = side_by_side(pack_ref, rows, width)
    keep = iota((step, step), 0) <= iota((step, step), 1)
    for start in range(0, rows, step):
        stop = start + step
        scores = dot(k_ref[:stop, :], qt_ref[:, start:stop])
        last = jnp.where(keep, scores[start:, :], NEG)
        scores = jnp.concatenate([scores[:start, :], last], axis=0) if start else last
        top = jnp.max(scores, axis=0, keepdims=True)
        probs = jnp.exp2((scores - top) * scale)
        top_ref[:, start:stop] = top
        total_ref[:, start:stop] = jnp.sum(probs, axis=0, keepdims=True)
        summed_ref[:, start:stop] = dot(value_t[:, :stop], probs.astype(BF16))


def linear_kernel(step, q_ref, k_ref, value_t_ref, cum_row_ref, cum_col_ref, qt_ref, intra_ref):
    rows, width = q_ref.shape
    qt_ref[...] = jnp.transpose(q_ref[...])
    keep = iota((step, step), 0) <= iota((step, step), 1)
    for start in range(0, rows, step):
        stop = start + step
        scores = dot(k_ref[:stop, :], qt_ref[:, start:stop])
        cum_t = cum_row_ref[:, start:stop]
        cum_s = jnp.concatenate([cum_col_ref[:stop, :]] * (step // width), axis=1)
        diff = cum_t - cum_s
        last = jnp.where(keep, diff[start:, :], NEG)
        diff = jnp.concatenate([diff[:start, :], last], axis=0) if start else last
        weights = (scores * jnp.exp(diff)).astype(BF16)
        intra_ref[:, start:stop] = dot(value_t_ref[:, :stop], weights)


def by_chip(position, cores, count, body):
    pl.when(position >= cores)(lambda: body(count))
    pl.when(position < cores)(lambda: body(cores - 1))


def score_kernel(scale, step, axis, cores, offsets, qt_ref, top_ref, total_ref, *refs):
    key_refs, (probs_ref, factor_ref, sum_ref, *new_top_ref) = refs[: len(offsets)], refs[len(offsets) :]
    rows = qt_ref.shape[1]
    position = lax.axis_index(axis)
    chip = position // cores
    away = [
        jnp.where(position - chip * cores >= 1 if apart == 0 else chip >= apart, 0.0, NEG) for apart in offsets
    ]

    def body(count):
        for start in range(0, rows, step):
            mine = slice(start, start + step)
            query = qt_ref[:, mine]
            old = top_ref[:, mine]
            scores = [dot(key_ref[...], query) for key_ref in key_refs[:count]]
            top = old
            for score, off in zip(scores, away):
                top = jnp.maximum(top, jnp.max(score, axis=0, keepdims=True) + off)
            factor = jnp.exp2((old - top) * scale)
            total = total_ref[:, mine] * factor
            for place, (score, off) in enumerate(zip(scores, away)):
                probs = jnp.exp2((score - (top - off)) * scale)
                total = total + jnp.sum(probs, axis=0, keepdims=True)
                probs_ref[place * rows : (place + 1) * rows, mine] = probs.astype(BF16)
            for ref in new_top_ref:
                ref[:, mine] = top
            factor_ref[:, mine] = factor
            sum_ref[:, mine] = total

    pl.when(chip >= 1)(lambda: body(len(offsets)))
    pl.when(chip < 1)(lambda: body(offsets.count(0)))


def carried_state(position, cores, near, shares, width):
    chip = position // cores
    carried = jnp.zeros((width, width), F32)
    between = jnp.zeros((1, width), F32)
    for apart, ref in enumerate(shares, 1):
        carried = carried + jnp.exp(between + jnp.where(chip >= apart, 0.0, NEG)) * ref[:width, :].astype(F32)
        if ref.shape[0] > width:
            between = between + sum_of_parts(ref[width:, :])
    for ref in near:
        passed = jnp.exp(sum_of_parts(ref[width:, :])) * carried + ref[:width, :].astype(F32)
        carried = jnp.where(position - chip * cores == 1, passed, carried)
    return carried.astype(BF16)


def put_linear(step, carried, qt_ref, intra_ref, cum_row_ref, buffer):
    width, rows = qt_ref.shape
    for start in range(0, rows, step):
        mine = slice(start, start + step)
        inter = dot(carried, qt_ref[:, mine])
        raw = intra_ref[:, mine] + inter * jnp.exp(cum_row_ref[:, mine])
        square = jnp.sum(raw * raw, axis=0, keepdims=True) * (1.0 / width)
        buffer[mine, :] = jnp.transpose((raw * lax.rsqrt(square + TINY)).astype(BF16))


def value_sum(values_t, probs_ref, mine):
    rows = values_t[0].shape[1]
    terms = [
        dot(value_t, probs_ref[place * rows : (place + 1) * rows, mine]) for place, value_t in enumerate(values_t)
    ]
    return functools.reduce(jnp.add, terms)


def early_kernel(step, axis, cores, counts, *refs):
    lin_qt_ref, intra_ref, cum_row_ref, summed_ref, factor_ref, sum_ref, probs_ref, late_factor_ref = refs[:8]
    linear_ref, softmax_ref, sofar_ref, linear_buffer, softmax_buffer, sems = refs[-6:]
    received, groups = list(refs[8:-6]), []
    for count in counts:
        groups.append(received[:count])
        received = received[count:]
    near_states, shares, near_values, values = groups
    width, rows = lin_qt_ref.shape
    position = lax.axis_index(axis)
    linear_copy = pltpu.make_async_copy(linear_buffer, linear_ref, sems.at[0])
    softmax_copy = pltpu.make_async_copy(softmax_buffer, softmax_ref, sems.at[1])

    def body(count):
        first = count == len(near_values)
        carried = carried_state(position, cores, near_states, () if first else shares, width)
        put_linear(step, carried, lin_qt_ref, intra_ref, cum_row_ref, linear_buffer)
        linear_copy.start()
        values_t = [side_by_side(ref, rows, width) for ref in (*near_values, *values)[:count]]
        for start in range(0, rows, step):
            mine = slice(start, start + step)
            summed = summed_ref[:, mine] * factor_ref[:, mine]
            if values_t:
                summed = summed + value_sum(values_t, probs_ref, mine)
            if first:
                softmax_buffer[mine, :] = jnp.transpose((summed / sum_ref[:, mine]).astype(BF16))
            else:
                sofar_ref[:, mine] = summed * late_factor_ref[:, mine]
        if first:
            softmax_copy.start()
            softmax_copy.wait()
        linear_copy.wait()

    by_chip(position, cores, len(near_values) + len(values), body)


def late_kernel(step, axis, cores, *refs):
    sofar_ref, sum_ref, probs_ref, *values, softmax_ref, softmax_buffer, sems = refs[1:]
    rows = sum_ref.shape[1]

    @pl.when(lax.axis_index(axis) >= cores)
    def _():
        softmax_copy = pltpu.make_async_copy(softmax_buffer, softmax_ref, sems.at[0])
        values_t = [side_by_side(ref, rows, sofar_ref.shape[0]) for ref in values]
        for start in range(0, rows, step):
            mine = slice(start, start + step)
            summed = sofar_ref[:, mine]
            if values_t:
                summed = summed + value_sum(values_t, probs_ref, mine)
            softmax_buffer[mine, :] = jnp.transpose((summed / sum_ref[:, mine]).astype(BF16))
        softmax_copy.start()
        softmax_copy.wait()


def keep_in_hbm(x):
    return pltpu.with_memory_space_constraint(x, pltpu.HBM)


def keep_in_vmem(x):
    return pltpu.with_memory_space_constraint(x, VMEM)


def kept_in_vmem(x):
    return VMEM(x.shape, x.dtype)


def kept_in_hbm(x):
    return pltpu.HBM(x.shape, x.dtype)


def call(body, operands, outs, given=(), written=(), resumed=(), scratch=()):
    size = sum(math.prod(x.shape) * x.dtype.itemsize for x in (*given, *operands, *outs))
    inside, outside = pl.BlockSpec(memory_space=VMEM), pl.BlockSpec(memory_space=pl.ANY)
    hbm = (*given, *resumed)
    scratch = [VMEM(x.shape, x.dtype) for x in (*scratch, *written)]
    moved = len(given) + len(written)
    return pl.pallas_call(
        body,
        out_shape=(*map(kept_in_hbm, written), *map(kept_in_vmem, outs)),
        in_specs=[outside] * len(hbm) + [inside] * len(operands),
        out_specs=(*[outside] * len(written), *[inside] * len(outs)),
        scratch_shapes=[*scratch, pltpu.SemaphoreType.DMA((moved,))] if moved else [],
        input_output_aliases={place: place for place in range(len(resumed))},
        cost_estimate=pl.CostEstimate(flops=0, bytes_accessed=size, transcendentals=0),
        compiler_params=pltpu.CompilerParams(vmem_limit_bytes=KERNEL_VMEM),
    )(*map(keep_in_hbm, hbm), *map(keep_in_vmem, operands))


def on_device(axis, lin_query, lin_key, lin_value, log_decay, soft_query, soft_key, soft_value):
    rows, heads, width = lin_query.shape
    count = lax.axis_size(axis)
    cores = 2 if count % 2 == 0 else 1
    chips = count // cores

    def across(x, apart):
        return lax.ppermute(x, axis, [(i, (i + apart * cores) % count) for i in range(count)])

    def swapped(x):
        return lax.ppermute(x, axis, [(i, i ^ 1) for i in range(count)])

    def near(blocks):
        return [swapped(block) for block in blocks] if cores == 2 else []

    def far(x):
        return [across(x, apart) for apart in range(1, chips)]

    def passed(blocks, after):
        return near(lax.optimization_barrier((block, after))[0] for block in blocks)

    def one_head(lq, lk, lv, decay, sq, sk, sv):
        step = math.gcd(rows, 256)
        scale = math.log2(math.e) / math.sqrt(width)

        def shape(*dims, dtype=F32):
            return jax.ShapeDtypeStruct(dims, dtype)

        def half(*dims):
            return shape(*dims, dtype=BF16)

        row, flat, flat16, block = shape(1, rows), shape(width, rows), half(width, rows), half(rows, width)
        keys = far(sk)
        soft_vt, state, cum_row, cum_col, lin_vt, lk, lq, sq, own_keys = call(
            state_kernel,
            (),
            (block, half(width + PAD, width), row, shape(rows, width), flat16, block, block, block, block),
            given=(decay, lk, lv, sv, lq, sq, sk),
            scratch=(row, block, block),
        )
        values, near_states, near_values = far(soft_vt), near([state]), near([soft_vt])
        qt, top, total, summed = call(
            functools.partial(soft_kernel, scale, step), (sq, own_keys, soft_vt), (flat16, row, row, flat)
        )
        near_states, _ = lax.optimization_barrier((near_states, summed))
        (share,) = call(
            functools.partial(combine_kernel, axis, cores),
            (state, *near_states),
            (half(width + (PAD if chips > 2 else 0), width),),
        )
        shares = far(share)
        lin_qt, intra = call(
            functools.partial(linear_kernel, step), (lq, lk, lin_vt, cum_row, cum_col), (flat16, flat)
        )

        def scored(top, total, blocks, offsets, more):
            return call(
                functools.partial(score_kernel, scale, step, axis, cores, offsets),
                (qt, top, total, *blocks),
                (half(len(blocks) * rows, rows), *[row] * (2 + more)),
            )

        apart = tuple(range(1, chips))
        late_keys = passed(keys, (summed, intra))
        probs, factor, sums, *top = scored(
            top, total, [*near([own_keys]), *keys], (0,) * (cores - 1) + apart, len(late_keys) > 0
        )
        late_values = passed(values, (factor, shares))
        late_keys, _ = lax.optimization_barrier((late_keys, values))
        late_factor, late_sums = jnp.ones_like(factor), sums
        if late_keys:
            late_probs, late_factor, late_sums = scored(*top, sums, late_keys, apart, False)
        linear, softmax, sofar = call(
            functools.partial(
                early_kernel, step, axis, cores, [len(x) for x in (near_states, shares, near_values, values)]
            ),
            (
                lin_qt, intra, cum_row, summed, factor, sums, probs, late_factor,
                *near_states, *shares, *near_values, *values,
            ),
            (flat,),
            written=(block, block),
        )
        (softmax,) = call(
            functools.partial(late_kernel, step, axis, cores),
            (sofar, late_sums, late_probs if late_keys else probs, *late_values),
            (),
            written=(block,),
            resumed=(softmax,),
        )
        return linear, softmax

    outs = [
        one_head(
            *(x[:, head] for x in (lin_query, lin_key, lin_value)),
            log_decay[head : head + 1],
            *(x[:, head] for x in (soft_query, soft_key, soft_value)),
        )
        for head in range(heads)
    ]
    linear = jnp.stack([pair[0] for pair in outs], axis=1)
    softmax = jnp.stack([pair[1] for pair in outs], axis=1)
    return linear, softmax


def solution(mesh):
    block = P("ctx", "tp", None)
    return jax.shard_map(
        functools.partial(on_device, "ctx"),
        mesh=mesh,
        in_specs=(block, block, block, P("tp", "ctx"), block, block, block),
        out_specs=(block, block),
        check_vma=False,
    )
```

```python
import functools
import math

import jax
import jax.numpy as jnp
from jax import lax
from jax.experimental import pallas as pl
from jax.experimental.pallas import tpu as pltpu
from jax.sharding import PartitionSpec as P

NEG = -1e30
TINY = 1e-6
PAD = 16
KERNEL_VMEM = 16 * 2**20
F32 = jnp.float32
BF16 = jnp.bfloat16
VMEM = pltpu.VMEM


def dot(a, b):
    return lax.dot_general(a, b, (((1,), (0,)), ((), ())), preferred_element_type=F32)


def three_parts(x):
    high = x.astype(BF16)
    rest = x - high.astype(F32)
    middle = rest.astype(BF16)
    low = (rest - middle.astype(F32)).astype(BF16)
    return high, middle, low


def iota(shape, dim):
    return lax.broadcasted_iota(jnp.int32, shape, dim)


def select_rows(parts, rows, width):
    row = iota((rows, width), 0)
    out = jnp.zeros((rows, width), F32)
    for number, part in enumerate(parts):
        out = jnp.where(row == number, part.astype(F32), out)
    return out.astype(BF16)


def side_by_side(ref, rows, width):
    pieces = [ref[left : left + width, :] for left in range(0, rows, width)]
    return pieces[0] if len(pieces) == 1 else jnp.concatenate(pieces, axis=1)


def state_kernel(
    decay_hbm, key_hbm, value_hbm, soft_value_hbm, query_hbm, soft_query_hbm, soft_key_hbm,
    soft_vt_ref, state_ref, cum_row_ref, cum_col_ref, value_t_ref, key_ref, query_ref, soft_query_ref, soft_key_ref,
    decay_ref, value_ref, soft_value_ref, sems,
):
    copies = [
        pltpu.make_async_copy(source, target, sems.at[place])
        for place, (source, target) in enumerate(
            (
                (decay_hbm, decay_ref),
                (key_hbm, key_ref),
                (value_hbm, value_ref),
                (soft_value_hbm, soft_value_ref),
                (soft_query_hbm, soft_query_ref),
                (soft_key_hbm, soft_key_ref),
                (query_hbm, query_ref),
            )
        )
    ]
    for copy in copies:
        copy.start()
    rows, width = key_ref.shape
    upto = (iota((rows, rows), 0) <= iota((rows, rows), 1)).astype(F32).astype(BF16)
    copies[0].wait()
    parts = select_rows(three_parts(decay_ref[...]), PAD, rows)
    cum_row = jnp.sum(dot(parts, upto), axis=0, keepdims=True)
    cum_row_ref[...] = cum_row
    cum_col = jnp.transpose(jnp.broadcast_to(cum_row, (width, rows)))
    cum_col_ref[...] = cum_col
    total = cum_col[rows - 1 :, :]
    for copy in copies[1:4]:
        copy.wait()
    decayed = (key_ref[...].astype(F32) * jnp.exp(total - cum_col)).astype(BF16)
    value_t = jnp.transpose(value_ref[...])
    value_t_ref[...] = value_t
    state_ref[:width, :] = dot(value_t, decayed).astype(BF16)
    state_ref[width:, :] = select_rows(three_parts(total), PAD, width)
    for left in range(0, rows, width):
        soft_vt_ref[left : left + width, :] = jnp.transpose(soft_value_ref[left : left + width, :])
    for copy in copies[4:]:
        copy.wait()


def sum_of_parts(tail):
    tail = tail.astype(F32)
    return tail[0:1] + tail[1:2] + tail[2:3]


def combine_kernel(axis, cores, *refs):
    *state_refs, share_ref = refs
    width = share_ref.shape[1]
    share = width // cores
    states = [ref[:width, :].astype(F32) for ref in state_refs]
    totals = [sum_of_parts(ref[width:, :]) for ref in state_refs]
    state, total = states[0], totals[0]
    if cores == 2:
        upper = lax.rem(lax.axis_index(axis), 2) == 1
        first, second = jnp.where(upper, states[1], state), jnp.where(upper, state, states[1])
        state = jnp.exp(jnp.where(upper, total, totals[1])) * first + second
        state = jnp.where(upper, state[share:], state[:share])
        total = total + totals[1]
    share_ref[:share, :] = state.astype(BF16)
    if share_ref.shape[0] > share:
        share_ref[share:, :] = select_rows(three_parts(total), PAD, width)


def soft_kernel(scale, step, q_ref, k_ref, pack_ref, qt_ref, top_ref, total_ref, summed_ref):
    rows, width = q_ref.shape
    qt_ref[...] = jnp.transpose(q_ref[...])
    value_t = side_by_side(pack_ref, rows, width)
    keep = iota((step, step), 0) <= iota((step, step), 1)
    for start in range(0, rows, step):
        stop = start + step
        scores = dot(k_ref[:stop, :], qt_ref[:, start:stop])
        last = jnp.where(keep, scores[start:, :], NEG)
        scores = jnp.concatenate([scores[:start, :], last], axis=0) if start else last
        top = jnp.max(scores, axis=0, keepdims=True)
        probs = jnp.exp2((scores - top) * scale)
        top_ref[:, start:stop] = top
        total_ref[:, start:stop] = jnp.sum(probs, axis=0, keepdims=True)
        summed_ref[:, start:stop] = dot(value_t[:, :stop], probs.astype(BF16))


def linear_kernel(step, q_ref, k_ref, value_t_ref, cum_row_ref, cum_col_ref, qt_ref, intra_ref):
    rows, width = q_ref.shape
    qt_ref[...] = jnp.transpose(q_ref[...])
    keep = iota((step, step), 0) <= iota((step, step), 1)
    for start in range(0, rows, step):
        stop = start + step
        scores = dot(k_ref[:stop, :], qt_ref[:, start:stop])
        cum_t = cum_row_ref[:, start:stop]
        cum_s = jnp.concatenate([cum_col_ref[:stop, :]] * (step // width), axis=1)
        diff = cum_t - cum_s
        last = jnp.where(keep, diff[start:, :], NEG)
        diff = jnp.concatenate([diff[:start, :], last], axis=0) if start else last
        weights = (scores * jnp.exp(diff)).astype(BF16)
        intra_ref[:, start:stop] = dot(value_t_ref[:, :stop], weights)


def by_chip(position, cores, count, body):
    pl.when(position >= cores)(lambda: body(count))
    pl.when(position < cores)(lambda: body(cores - 1))


def score_kernel(scale, step, axis, cores, offsets, qt_ref, top_ref, total_ref, *refs):
    key_refs, (probs_ref, factor_ref, sum_ref, *new_top_ref) = refs[: len(offsets)], refs[len(offsets) :]
    rows = qt_ref.shape[1]
    position = lax.axis_index(axis)
    chip = position // cores
    away = [
        jnp.where(position - chip * cores >= 1 if apart == 0 else chip >= apart, 0.0, NEG) for apart in offsets
    ]

    def body(count):
        for start in range(0, rows, step):
            mine = slice(start, start + step)
            query = qt_ref[:, mine]
            old = top_ref[:, mine]
            scores = [dot(key_ref[...], query) for key_ref in key_refs[:count]]
            top = old
            for score, off in zip(scores, away):
                top = jnp.maximum(top, jnp.max(score, axis=0, keepdims=True) + off)
            factor = jnp.exp2((old - top) * scale)
            total = total_ref[:, mine] * factor
            for place, (score, off) in enumerate(zip(scores, away)):
                probs = jnp.exp2((score - (top - off)) * scale)
                total = total + jnp.sum(probs, axis=0, keepdims=True)
                probs_ref[place * rows : (place + 1) * rows, mine] = probs.astype(BF16)
            for ref in new_top_ref:
                ref[:, mine] = top
            factor_ref[:, mine] = factor
            sum_ref[:, mine] = total

    pl.when(chip >= 1)(lambda: body(len(offsets)))
    pl.when(chip < 1)(lambda: body(offsets.count(0)))


def carried_state(position, cores, near, shares, width):
    share = width // cores
    chip = position // cores
    upper = position - chip * cores == 1
    carried = jnp.zeros((width, width), F32)
    between = jnp.zeros((1, width), F32)
    for apart in range(1, len(shares) // cores + 1):
        parts = shares[(apart - 1) * cores : apart * cores]
        state = [ref[:share, :].astype(F32) for ref in parts]
        if cores == 2:
            halves = jnp.where(upper, state[1], state[0]), jnp.where(upper, state[0], state[1])
            state = [jnp.concatenate(halves, axis=0)]
        carried = carried + jnp.exp(between + jnp.where(chip >= apart, 0.0, NEG)) * state[0]
        if parts[0].shape[0] > share:
            between = between + sum_of_parts(parts[0][share:, :])
    for ref in near:
        passed = jnp.exp(sum_of_parts(ref[width:, :])) * carried + ref[:width, :].astype(F32)
        carried = jnp.where(upper, passed, carried)
    return carried.astype(BF16)


def put_linear(step, carried, qt_ref, intra_ref, cum_row_ref, buffer):
    width, rows = qt_ref.shape
    for start in range(0, rows, step):
        mine = slice(start, start + step)
        inter = dot(carried, qt_ref[:, mine])
        raw = intra_ref[:, mine] + inter * jnp.exp(cum_row_ref[:, mine])
        square = jnp.sum(raw * raw, axis=0, keepdims=True) * (1.0 / width)
        buffer[mine, :] = jnp.transpose((raw * lax.rsqrt(square + TINY)).astype(BF16))


def value_sum(values_t, probs_ref, mine):
    rows = values_t[0].shape[1]
    terms = [
        dot(value_t, probs_ref[place * rows : (place + 1) * rows, mine]) for place, value_t in enumerate(values_t)
    ]
    return functools.reduce(jnp.add, terms)


def write_out(step, sofar, values_t, probs_ref, sum_ref, carried, linear_refs, outs, buffers, sems):
    lin_qt_ref, intra_ref, cum_row_ref = linear_refs
    linear_buffer, softmax_buffer = buffers
    rows = sum_ref.shape[1]
    linear_copy = pltpu.make_async_copy(linear_buffer, outs[0], sems.at[0])
    softmax_copy = pltpu.make_async_copy(softmax_buffer, outs[1], sems.at[1])
    for start in range(0, rows, step):
        mine = slice(start, start + step)
        summed = sofar(mine)
        if values_t:
            summed = summed + value_sum(values_t, probs_ref, mine)
        softmax_buffer[mine, :] = jnp.transpose((summed / sum_ref[:, mine]).astype(BF16))
    softmax_copy.start()
    put_linear(step, carried(), lin_qt_ref, intra_ref, cum_row_ref, linear_buffer)
    linear_copy.start()
    softmax_copy.wait()
    linear_copy.wait()


def early_kernel(step, axis, cores, near_count, *refs):
    lin_qt_ref, intra_ref, cum_row_ref, summed_ref, factor_ref, sum_ref, probs_ref, late_factor_ref = refs[:8]
    linear_ref, softmax_ref, sofar_ref, *scratch, sems = refs[-6:]
    near_states, values = refs[8 : 8 + near_count], refs[8 + near_count : -6]
    width, rows = lin_qt_ref.shape
    position = lax.axis_index(axis)

    def scaled(mine):
        return summed_ref[:, mine] * factor_ref[:, mine]

    @pl.when(position >= cores)
    def _():
        values_t = [side_by_side(ref, rows, width) for ref in values]
        for start in range(0, rows, step):
            mine = slice(start, start + step)
            summed = scaled(mine) + value_sum(values_t, probs_ref, mine)
            sofar_ref[:, mine] = summed * late_factor_ref[:, mine]

    @pl.when(position < cores)
    def _():
        write_out(
            step, scaled, [side_by_side(ref, rows, width) for ref in values[:near_count]], probs_ref, sum_ref,
            lambda: carried_state(position, cores, near_states, (), width),
            (lin_qt_ref, intra_ref, cum_row_ref), (linear_ref, softmax_ref), scratch, sems,
        )


def late_kernel(step, axis, cores, counts, *refs):
    refs = refs[2:]
    lin_qt_ref, intra_ref, cum_row_ref, sofar_ref, sum_ref, probs_ref = refs[:6]
    linear_ref, softmax_ref, *scratch, sems = refs[-5:]
    near_states = refs[6 : 6 + counts[0]]
    shares = refs[6 + counts[0] : 6 + counts[0] + counts[1]]
    values = refs[6 + counts[0] + counts[1] : -5]
    width, rows = lin_qt_ref.shape
    position = lax.axis_index(axis)

    @pl.when(position >= cores)
    def _():
        write_out(
            step, lambda mine: sofar_ref[:, mine], [side_by_side(ref, rows, width) for ref in values],
            probs_ref, sum_ref, lambda: carried_state(position, cores, near_states, shares, width),
            (lin_qt_ref, intra_ref, cum_row_ref), (linear_ref, softmax_ref), scratch, sems,
        )


def keep_in_hbm(x):
    return pltpu.with_memory_space_constraint(x, pltpu.HBM)


def keep_in_vmem(x):
    return pltpu.with_memory_space_constraint(x, VMEM)


def kept_in_vmem(x):
    return VMEM(x.shape, x.dtype)


def kept_in_hbm(x):
    return pltpu.HBM(x.shape, x.dtype)


def call(body, operands, outs, given=(), written=(), resumed=(), scratch=()):
    size = sum(math.prod(x.shape) * x.dtype.itemsize for x in (*given, *operands, *outs))
    inside, outside = pl.BlockSpec(memory_space=VMEM), pl.BlockSpec(memory_space=pl.ANY)
    hbm = (*given, *resumed)
    scratch = [VMEM(x.shape, x.dtype) for x in (*scratch, *written)]
    moved = len(given) + len(written)
    return pl.pallas_call(
        body,
        out_shape=(*map(kept_in_hbm, written), *map(kept_in_vmem, outs)),
        in_specs=[outside] * len(hbm) + [inside] * len(operands),
        out_specs=(*[outside] * len(written), *[inside] * len(outs)),
        scratch_shapes=[*scratch, pltpu.SemaphoreType.DMA((moved,))] if moved else [],
        input_output_aliases={place: place for place in range(len(resumed))},
        cost_estimate=pl.CostEstimate(flops=0, bytes_accessed=size, transcendentals=0),
        compiler_params=pltpu.CompilerParams(vmem_limit_bytes=KERNEL_VMEM),
    )(*map(keep_in_hbm, hbm), *map(keep_in_vmem, operands))


def on_device(axis, lin_query, lin_key, lin_value, log_decay, soft_query, soft_key, soft_value):
    rows, heads, width = lin_query.shape
    count = lax.axis_size(axis)
    cores = 2 if count % 2 == 0 else 1
    chips = count // cores

    def across(x, apart):
        return lax.ppermute(x, axis, [(i, (i + apart * cores) % count) for i in range(count)])

    def swapped(x):
        return lax.ppermute(x, axis, [(i, i ^ 1) for i in range(count)])

    def near(blocks):
        return [swapped(block) for block in blocks] if cores == 2 else []

    def far(x):
        return [across(x, apart) for apart in range(1, chips)]

    def passed(blocks, after):
        return near(lax.optimization_barrier((block, after))[0] for block in blocks)

    def one_head(lq, lk, lv, decay, sq, sk, sv):
        step = math.gcd(rows, 256)
        scale = math.log2(math.e) / math.sqrt(width)

        def shape(*dims, dtype=F32):
            return jax.ShapeDtypeStruct(dims, dtype)

        def half(*dims):
            return shape(*dims, dtype=BF16)

        row, flat, flat16, block = shape(1, rows), shape(width, rows), half(width, rows), half(rows, width)
        keys = far(sk)
        soft_vt, state, cum_row, cum_col, lin_vt, lk, lq, sq, own_keys = call(
            state_kernel,
            (),
            (block, half(width + PAD, width), row, shape(rows, width), flat16, block, block, block, block),
            given=(decay, lk, lv, sv, lq, sq, sk),
            scratch=(row, block, block),
        )
        values, near_states, near_values = far(soft_vt), near([state]), near([soft_vt])
        qt, top, total, summed = call(
            functools.partial(soft_kernel, scale, step), (sq, own_keys, soft_vt), (flat16, row, row, flat)
        )
        near_states, _ = lax.optimization_barrier((near_states, summed))
        (share,) = call(
            functools.partial(combine_kernel, axis, cores),
            (state, *near_states),
            (half(width // cores + (PAD if chips > 2 else 0), width),),
        )
        shares = far(share)
        lin_qt, intra = call(
            functools.partial(linear_kernel, step), (lq, lk, lin_vt, cum_row, cum_col), (flat16, flat)
        )

        def scored(top, total, blocks, offsets, more):
            return call(
                functools.partial(score_kernel, scale, step, axis, cores, offsets),
                (qt, top, total, *blocks),
                (half(len(blocks) * rows, rows), *[row] * (2 + more)),
            )

        apart = tuple(range(1, chips))
        late_keys = passed(keys, (summed, intra))
        probs, factor, sums, *top = scored(
            top, total, [*near([own_keys]), *keys], (0,) * (cores - 1) + apart, len(late_keys) > 0
        )
        late_values = passed(values, (factor, shares))
        late_keys, _ = lax.optimization_barrier((late_keys, values))
        late_factor, late_sums = jnp.ones_like(factor), sums
        if late_keys:
            late_probs, late_factor, late_sums = scored(*top, sums, late_keys, apart, False)
        late_shares = passed(shares, values)
        if cores == 2:
            shares = [part for pair in zip(shares, late_shares) for part in pair]
        *began, sofar = call(
            functools.partial(early_kernel, step, axis, cores, len(near_states)),
            (
                lin_qt, intra, cum_row, summed, factor, sums, probs, late_factor,
                *near_states, *near_values, *values,
            ),
            (flat,),
            written=(block, block),
        )
        return call(
            functools.partial(late_kernel, step, axis, cores, (len(near_states), len(shares))),
            (
                lin_qt, intra, cum_row, sofar, late_sums, late_probs if late_keys else probs,
                *near_states, *shares, *late_values,
            ),
            (),
            written=(block, block),
            resumed=began,
        )

    outs = [
        one_head(
            *(x[:, head] for x in (lin_query, lin_key, lin_value)),
            log_decay[head : head + 1],
            *(x[:, head] for x in (soft_query, soft_key, soft_value)),
        )
        for head in range(heads)
    ]
    linear = jnp.stack([pair[0] for pair in outs], axis=1)
    softmax = jnp.stack([pair[1] for pair in outs], axis=1)
    return linear, softmax


def solution(mesh):
    block = P("ctx", "tp", None)
    return jax.shard_map(
        functools.partial(on_device, "ctx"),
        mesh=mesh,
        in_specs=(block, block, block, P("tp", "ctx"), block, block, block),
        out_specs=(block, block),
        check_vma=False,
    )
```

```python
import functools
import math

import jax
import jax.numpy as jnp
from jax import lax
from jax.experimental import pallas as pl
from jax.experimental.pallas import tpu as pltpu
from jax.sharding import PartitionSpec as P

NEG = -1e30
TINY = 1e-6
PAD = 16
KERNEL_VMEM = 16 * 2**20
F32 = jnp.float32
BF16 = jnp.bfloat16
VMEM = pltpu.VMEM


def dot(a, b):
    return lax.dot_general(a, b, (((1,), (0,)), ((), ())), preferred_element_type=F32)


def three_parts(x):
    high = x.astype(BF16)
    rest = x - high.astype(F32)
    middle = rest.astype(BF16)
    low = (rest - middle.astype(F32)).astype(BF16)
    return high, middle, low


def iota(shape, dim):
    return lax.broadcasted_iota(jnp.int32, shape, dim)


def select_rows(parts, rows, width):
    row = iota((rows, width), 0)
    out = jnp.zeros((rows, width), F32)
    for number, part in enumerate(parts):
        out = jnp.where(row == number, part.astype(F32), out)
    return out.astype(BF16)


def side_by_side(ref, rows, width):
    pieces = [ref[left : left + width, :] for left in range(0, rows, width)]
    return pieces[0] if len(pieces) == 1 else jnp.concatenate(pieces, axis=1)


def state_kernel(
    decay_hbm, key_hbm, value_hbm, soft_value_hbm, query_hbm, soft_query_hbm, soft_key_hbm,
    soft_vt_ref, state_ref, cum_row_ref, cum_col_ref, value_t_ref, key_ref, query_ref, soft_query_ref, soft_key_ref,
    decay_ref, value_ref, soft_value_ref, sems,
):
    copies = [
        pltpu.make_async_copy(source, target, sems.at[place])
        for place, (source, target) in enumerate(
            (
                (decay_hbm, decay_ref),
                (key_hbm, key_ref),
                (value_hbm, value_ref),
                (soft_value_hbm, soft_value_ref),
                (soft_query_hbm, soft_query_ref),
                (soft_key_hbm, soft_key_ref),
                (query_hbm, query_ref),
            )
        )
    ]
    for copy in copies:
        copy.start()
    rows, width = key_ref.shape
    upto = (iota((rows, rows), 0) <= iota((rows, rows), 1)).astype(F32).astype(BF16)
    copies[0].wait()
    parts = select_rows(three_parts(decay_ref[...]), PAD, rows)
    cum_row = jnp.sum(dot(parts, upto), axis=0, keepdims=True)
    cum_row_ref[...] = cum_row
    cum_col = jnp.transpose(jnp.broadcast_to(cum_row, (width, rows)))
    cum_col_ref[...] = cum_col
    total = cum_col[rows - 1 :, :]
    for copy in copies[1:4]:
        copy.wait()
    decayed = (key_ref[...].astype(F32) * jnp.exp(total - cum_col)).astype(BF16)
    value_t = jnp.transpose(value_ref[...])
    value_t_ref[...] = value_t
    state_ref[:width, :] = dot(value_t, decayed).astype(BF16)
    state_ref[width:, :] = select_rows(three_parts(total), PAD, width)
    for left in range(0, rows, width):
        soft_vt_ref[left : left + width, :] = jnp.transpose(soft_value_ref[left : left + width, :])
    for copy in copies[4:]:
        copy.wait()


def sum_of_parts(tail):
    tail = tail.astype(F32)
    return tail[0:1] + tail[1:2] + tail[2:3]


def combine_kernel(axis, cores, *refs):
    *state_refs, share_ref = refs
    width = share_ref.shape[1]
    share = width // cores
    states = [ref[:width, :].astype(F32) for ref in state_refs]
    totals = [sum_of_parts(ref[width:, :]) for ref in state_refs]
    state, total = states[0], totals[0]
    if cores == 2:
        upper = lax.rem(lax.axis_index(axis), 2) == 1
        first, second = jnp.where(upper, states[1], state), jnp.where(upper, state, states[1])
        state = jnp.exp(jnp.where(upper, total, totals[1])) * first + second
        state = jnp.where(upper, state[share:], state[:share])
        total = total + totals[1]
    share_ref[:share, :] = state.astype(BF16)
    if share_ref.shape[0] > share:
        share_ref[share:, :] = select_rows(three_parts(total), PAD, width)


def soft_kernel(scale, step, q_ref, k_ref, pack_ref, qt_ref, top_ref, total_ref, summed_ref):
    rows, width = q_ref.shape
    qt_ref[...] = jnp.transpose(q_ref[...])
    value_t = side_by_side(pack_ref, rows, width)
    keep = iota((step, step), 0) <= iota((step, step), 1)
    for start in range(0, rows, step):
        stop = start + step
        scores = dot(k_ref[:stop, :], qt_ref[:, start:stop])
        last = jnp.where(keep, scores[start:, :], NEG)
        scores = jnp.concatenate([scores[:start, :], last], axis=0) if start else last
        top = jnp.max(scores, axis=0, keepdims=True)
        probs = jnp.exp2((scores - top) * scale)
        top_ref[:, start:stop] = top
        total_ref[:, start:stop] = jnp.sum(probs, axis=0, keepdims=True)
        summed_ref[:, start:stop] = dot(value_t[:, :stop], probs.astype(BF16))


def linear_kernel(step, q_ref, k_ref, value_t_ref, cum_row_ref, cum_col_ref, qt_ref, intra_ref):
    rows, width = q_ref.shape
    qt_ref[...] = jnp.transpose(q_ref[...])
    keep = iota((step, step), 0) <= iota((step, step), 1)
    for start in range(0, rows, step):
        stop = start + step
        scores = dot(k_ref[:stop, :], qt_ref[:, start:stop])
        cum_t = cum_row_ref[:, start:stop]
        cum_s = jnp.concatenate([cum_col_ref[:stop, :]] * (step // width), axis=1)
        diff = cum_t - cum_s
        last = jnp.where(keep, diff[start:, :], NEG)
        diff = jnp.concatenate([diff[:start, :], last], axis=0) if start else last
        weights = (scores * jnp.exp(diff)).astype(BF16)
        intra_ref[:, start:stop] = dot(value_t_ref[:, :stop], weights)


def by_chip(position, cores, count, body):
    pl.when(position >= cores)(lambda: body(count))
    pl.when(position < cores)(lambda: body(cores - 1))


def score_kernel(scale, step, axis, cores, offsets, qt_ref, top_ref, total_ref, *refs):
    key_refs, (probs_ref, factor_ref, sum_ref, *new_top_ref) = refs[: len(offsets)], refs[len(offsets) :]
    rows = qt_ref.shape[1]
    position = lax.axis_index(axis)
    chip = position // cores
    away = [
        jnp.where(position - chip * cores >= 1 if apart == 0 else chip >= apart, 0.0, NEG) for apart in offsets
    ]

    def body(count):
        for start in range(0, rows, step):
            mine = slice(start, start + step)
            query = qt_ref[:, mine]
            old = top_ref[:, mine]
            scores = [dot(key_ref[...], query) for key_ref in key_refs[:count]]
            top = old
            for score, off in zip(scores, away):
                top = jnp.maximum(top, jnp.max(score, axis=0, keepdims=True) + off)
            factor = jnp.exp2((old - top) * scale)
            total = total_ref[:, mine] * factor
            for place, (score, off) in enumerate(zip(scores, away)):
                probs = jnp.exp2((score - (top - off)) * scale)
                total = total + jnp.sum(probs, axis=0, keepdims=True)
                probs_ref[place * rows : (place + 1) * rows, mine] = probs.astype(BF16)
            for ref in new_top_ref:
                ref[:, mine] = top
            factor_ref[:, mine] = factor
            sum_ref[:, mine] = total

    pl.when(chip >= 1)(lambda: body(len(offsets)))
    pl.when(chip < 1)(lambda: body(offsets.count(0)))


def carried_state(position, cores, near, shares, width):
    share = width // cores
    chip = position // cores
    upper = position - chip * cores == 1
    carried = jnp.zeros((width, width), F32)
    between = jnp.zeros((1, width), F32)
    for apart in range(1, len(shares) // cores + 1):
        parts = shares[(apart - 1) * cores : apart * cores]
        state = [ref[:share, :].astype(F32) for ref in parts]
        if cores == 2:
            halves = jnp.where(upper, state[1], state[0]), jnp.where(upper, state[0], state[1])
            state = [jnp.concatenate(halves, axis=0)]
        carried = carried + jnp.exp(between + jnp.where(chip >= apart, 0.0, NEG)) * state[0]
        if parts[0].shape[0] > share:
            between = between + sum_of_parts(parts[0][share:, :])
    for ref in near:
        passed = jnp.exp(sum_of_parts(ref[width:, :])) * carried + ref[:width, :].astype(F32)
        carried = jnp.where(upper, passed, carried)
    return carried.astype(BF16)


def put_linear(step, carried, qt_ref, intra_ref, cum_row_ref, buffer):
    width, rows = qt_ref.shape
    for start in range(0, rows, step):
        mine = slice(start, start + step)
        inter = dot(carried, qt_ref[:, mine])
        raw = intra_ref[:, mine] + inter * jnp.exp(cum_row_ref[:, mine])
        square = jnp.sum(raw * raw, axis=0, keepdims=True) * (1.0 / width)
        buffer[mine, :] = jnp.transpose((raw * lax.rsqrt(square + TINY)).astype(BF16))


def value_sum(values_t, probs_ref, mine):
    rows = values_t[0].shape[1]
    terms = [
        dot(value_t, probs_ref[place * rows : (place + 1) * rows, mine]) for place, value_t in enumerate(values_t)
    ]
    return functools.reduce(jnp.add, terms)


def write_out(step, sofar, values_t, probs_ref, sum_ref, carried, linear_refs, outs, buffers, sems):
    lin_qt_ref, intra_ref, cum_row_ref = linear_refs
    linear_buffer, softmax_buffer = buffers
    rows = sum_ref.shape[1]
    linear_copy = pltpu.make_async_copy(linear_buffer, outs[0], sems.at[0])
    softmax_copy = pltpu.make_async_copy(softmax_buffer, outs[1], sems.at[1])
    for start in range(0, rows, step):
        mine = slice(start, start + step)
        summed = sofar(mine)
        if values_t:
            summed = summed + value_sum(values_t, probs_ref, mine)
        softmax_buffer[mine, :] = jnp.transpose((summed / sum_ref[:, mine]).astype(BF16))
    put_linear(step, carried(), lin_qt_ref, intra_ref, cum_row_ref, linear_buffer)
    softmax_copy.start()
    linear_copy.start()
    softmax_copy.wait()
    linear_copy.wait()


def first_kernel(step, axis, cores, *refs):
    lin_qt_ref, intra_ref, cum_row_ref, summed_ref, factor_ref, sum_ref, probs_ref = refs[:7]
    linear_ref, softmax_ref, *scratch, sems = refs[-5:]
    near_states, near_values = refs[7 : 6 + cores], refs[6 + cores : -5]
    width, rows = lin_qt_ref.shape
    position = lax.axis_index(axis)

    @pl.when(position < cores)
    def _():
        write_out(
            step, lambda mine: summed_ref[:, mine] * factor_ref[:, mine],
            [side_by_side(ref, rows, width) for ref in near_values], probs_ref, sum_ref,
            lambda: carried_state(position, cores, near_states, (), width),
            (lin_qt_ref, intra_ref, cum_row_ref), (linear_ref, softmax_ref), scratch, sems,
        )


def early_kernel(step, axis, cores, *refs):
    summed_ref, factor_ref, probs_ref, late_factor_ref, *values, sofar_ref = refs
    width, rows = summed_ref.shape

    @pl.when(lax.axis_index(axis) >= cores)
    def _():
        values_t = [side_by_side(ref, rows, width) for ref in values]
        for start in range(0, rows, step):
            mine = slice(start, start + step)
            summed = summed_ref[:, mine] * factor_ref[:, mine] + value_sum(values_t, probs_ref, mine)
            sofar_ref[:, mine] = summed * late_factor_ref[:, mine]


def late_kernel(step, axis, cores, counts, *refs):
    refs = refs[2:]
    lin_qt_ref, intra_ref, cum_row_ref, sofar_ref, sum_ref, probs_ref = refs[:6]
    linear_ref, softmax_ref, *scratch, sems = refs[-5:]
    near_states = refs[6 : 6 + counts[0]]
    shares = refs[6 + counts[0] : 6 + counts[0] + counts[1]]
    values = refs[6 + counts[0] + counts[1] : -5]
    width, rows = lin_qt_ref.shape
    position = lax.axis_index(axis)

    @pl.when(position >= cores)
    def _():
        write_out(
            step, lambda mine: sofar_ref[:, mine], [side_by_side(ref, rows, width) for ref in values],
            probs_ref, sum_ref, lambda: carried_state(position, cores, near_states, shares, width),
            (lin_qt_ref, intra_ref, cum_row_ref), (linear_ref, softmax_ref), scratch, sems,
        )


def keep_in_hbm(x):
    return pltpu.with_memory_space_constraint(x, pltpu.HBM)


def keep_in_vmem(x):
    return pltpu.with_memory_space_constraint(x, VMEM)


def kept_in_vmem(x):
    return VMEM(x.shape, x.dtype)


def kept_in_hbm(x):
    return pltpu.HBM(x.shape, x.dtype)


def call(body, operands, outs, given=(), written=(), resumed=(), scratch=()):
    size = sum(math.prod(x.shape) * x.dtype.itemsize for x in (*given, *operands, *outs))
    inside, outside = pl.BlockSpec(memory_space=VMEM), pl.BlockSpec(memory_space=pl.ANY)
    hbm = (*given, *resumed)
    scratch = [VMEM(x.shape, x.dtype) for x in (*scratch, *written)]
    moved = len(given) + len(written)
    return pl.pallas_call(
        body,
        out_shape=(*map(kept_in_hbm, written), *map(kept_in_vmem, outs)),
        in_specs=[outside] * len(hbm) + [inside] * len(operands),
        out_specs=(*[outside] * len(written), *[inside] * len(outs)),
        scratch_shapes=[*scratch, pltpu.SemaphoreType.DMA((moved,))] if moved else [],
        input_output_aliases={place: place for place in range(len(resumed))},
        cost_estimate=pl.CostEstimate(flops=0, bytes_accessed=size, transcendentals=0),
        compiler_params=pltpu.CompilerParams(vmem_limit_bytes=KERNEL_VMEM),
    )(*map(keep_in_hbm, hbm), *map(keep_in_vmem, operands))


def on_device(axis, lin_query, lin_key, lin_value, log_decay, soft_query, soft_key, soft_value):
    rows, heads, width = lin_query.shape
    count = lax.axis_size(axis)
    cores = 2 if count % 2 == 0 else 1
    chips = count // cores

    def across(x, apart):
        return lax.ppermute(x, axis, [(i, (i + apart * cores) % count) for i in range(count)])

    def swapped(x):
        return lax.ppermute(x, axis, [(i, i ^ 1) for i in range(count)])

    def near(blocks):
        return [swapped(block) for block in blocks] if cores == 2 else []

    def far(x):
        return [across(x, apart) for apart in range(1, chips)]

    def passed(blocks, after):
        return near(lax.optimization_barrier((block, after))[0] for block in blocks)

    def one_head(lq, lk, lv, decay, sq, sk, sv):
        step = math.gcd(rows, 256)
        scale = math.log2(math.e) / math.sqrt(width)

        def shape(*dims, dtype=F32):
            return jax.ShapeDtypeStruct(dims, dtype)

        def half(*dims):
            return shape(*dims, dtype=BF16)

        row, flat, flat16, block = shape(1, rows), shape(width, rows), half(width, rows), half(rows, width)
        keys = far(sk)
        soft_vt, state, cum_row, cum_col, lin_vt, lk, lq, sq, own_keys = call(
            state_kernel,
            (),
            (block, half(width + PAD, width), row, shape(rows, width), flat16, block, block, block, block),
            given=(decay, lk, lv, sv, lq, sq, sk),
            scratch=(row, block, block),
        )
        values, near_states, near_values = far(soft_vt), near([state]), near([soft_vt])
        qt, top, total, summed = call(
            functools.partial(soft_kernel, scale, step), (sq, own_keys, soft_vt), (flat16, row, row, flat)
        )
        near_states, _ = lax.optimization_barrier((near_states, summed))
        (share,) = call(
            functools.partial(combine_kernel, axis, cores),
            (state, *near_states),
            (half(width // cores + (PAD if chips > 2 else 0), width),),
        )
        shares = far(share)
        lin_qt, intra = call(
            functools.partial(linear_kernel, step), (lq, lk, lin_vt, cum_row, cum_col), (flat16, flat)
        )

        def scored(top, total, blocks, offsets, more):
            return call(
                functools.partial(score_kernel, scale, step, axis, cores, offsets),
                (qt, top, total, *blocks),
                (half(len(blocks) * rows, rows), *[row] * (2 + more)),
            )

        apart = tuple(range(1, chips))
        late_keys = passed(keys, (summed, intra))
        probs, factor, sums, *top = scored(
            top, total, [*near([own_keys]), *keys], (0,) * (cores - 1) + apart, len(late_keys) > 0
        )
        began = call(
            functools.partial(first_kernel, step, axis, cores),
            (lin_qt, intra, cum_row, summed, factor, sums, probs, *near_states, *near_values),
            (),
            written=(block, block),
        )
        late_values = passed(values, (began, shares))
        late_keys, _ = lax.optimization_barrier((late_keys, values))
        late_factor, late_sums = jnp.ones_like(factor), sums
        if late_keys:
            late_probs, late_factor, late_sums = scored(*top, sums, late_keys, apart, False)
        late_shares = passed(shares, values)
        if cores == 2:
            shares = [part for pair in zip(shares, late_shares) for part in pair]
        (sofar,) = call(
            functools.partial(early_kernel, step, axis, cores),
            (summed, factor, probs, late_factor, *near_values, *values),
            (flat,),
        )
        return call(
            functools.partial(late_kernel, step, axis, cores, (len(near_states), len(shares))),
            (
                lin_qt, intra, cum_row, sofar, late_sums, late_probs if late_keys else probs,
                *near_states, *shares, *late_values,
            ),
            (),
            written=(block, block),
            resumed=began,
        )

    outs = [
        one_head(
            *(x[:, head] for x in (lin_query, lin_key, lin_value)),
            log_decay[head : head + 1],
            *(x[:, head] for x in (soft_query, soft_key, soft_value)),
        )
        for head in range(heads)
    ]
    linear = jnp.stack([pair[0] for pair in outs], axis=1)
    softmax = jnp.stack([pair[1] for pair in outs], axis=1)
    return linear, softmax


def solution(mesh):
    block = P("ctx", "tp", None)
    return jax.shard_map(
        functools.partial(on_device, "ctx"),
        mesh=mesh,
        in_specs=(block, block, block, P("tp", "ctx"), block, block, block),
        out_specs=(block, block),
        check_vma=False,
    )
```

```python
import functools
import math

import jax
import jax.numpy as jnp
from jax import lax
from jax.experimental import pallas as pl
from jax.experimental.pallas import tpu as pltpu
from jax.sharding import PartitionSpec as P

NEG = -1e30
TINY = 1e-6
PAD = 16
KERNEL_VMEM = 16 * 2**20
F32 = jnp.float32
BF16 = jnp.bfloat16
VMEM = pltpu.VMEM


def dot(a, b):
    return lax.dot_general(a, b, (((1,), (0,)), ((), ())), preferred_element_type=F32)


def three_parts(x):
    high = x.astype(BF16)
    rest = x - high.astype(F32)
    middle = rest.astype(BF16)
    low = (rest - middle.astype(F32)).astype(BF16)
    return high, middle, low


def iota(shape, dim):
    return lax.broadcasted_iota(jnp.int32, shape, dim)


def select_rows(parts, rows, width):
    row = iota((rows, width), 0)
    out = jnp.zeros((rows, width), F32)
    for number, part in enumerate(parts):
        out = jnp.where(row == number, part.astype(F32), out)
    return out.astype(BF16)


def side_by_side(ref, rows, width):
    pieces = [ref[left : left + width, :] for left in range(0, rows, width)]
    return pieces[0] if len(pieces) == 1 else jnp.concatenate(pieces, axis=1)


def state_kernel(
    decay_hbm, key_hbm, value_hbm, soft_value_hbm, query_hbm, soft_query_hbm, soft_key_hbm,
    soft_vt_ref, state_ref, cum_row_ref, cum_col_ref, value_t_ref, key_ref, query_ref, soft_query_ref, soft_key_ref,
    decay_ref, value_ref, soft_value_ref, sems,
):
    copies = [
        pltpu.make_async_copy(source, target, sems.at[place])
        for place, (source, target) in enumerate(
            (
                (decay_hbm, decay_ref),
                (key_hbm, key_ref),
                (value_hbm, value_ref),
                (soft_value_hbm, soft_value_ref),
                (soft_query_hbm, soft_query_ref),
                (soft_key_hbm, soft_key_ref),
                (query_hbm, query_ref),
            )
        )
    ]
    for copy in copies:
        copy.start()
    rows, width = key_ref.shape
    upto = (iota((rows, rows), 0) <= iota((rows, rows), 1)).astype(F32).astype(BF16)
    copies[0].wait()
    parts = select_rows(three_parts(decay_ref[...]), PAD, rows)
    cum_row = jnp.sum(dot(parts, upto), axis=0, keepdims=True)
    cum_row_ref[...] = cum_row
    cum_col = jnp.transpose(jnp.broadcast_to(cum_row, (width, rows)))
    cum_col_ref[...] = cum_col
    total = cum_col[rows - 1 :, :]
    for copy in copies[1:4]:
        copy.wait()
    decayed = (key_ref[...].astype(F32) * jnp.exp(total - cum_col)).astype(BF16)
    value_t = jnp.transpose(value_ref[...])
    value_t_ref[...] = value_t
    state_ref[:width, :] = dot(value_t, decayed).astype(BF16)
    state_ref[width:, :] = select_rows(three_parts(total), PAD, width)
    for left in range(0, rows, width):
        soft_vt_ref[left : left + width, :] = jnp.transpose(soft_value_ref[left : left + width, :])
    for copy in copies[4:]:
        copy.wait()


def sum_of_parts(tail):
    tail = tail.astype(F32)
    return tail[0:1] + tail[1:2] + tail[2:3]


def combine_kernel(axis, cores, *refs):
    *state_refs, share_ref = refs
    width = share_ref.shape[1]
    share = width // cores
    states = [ref[:width, :].astype(F32) for ref in state_refs]
    totals = [sum_of_parts(ref[width:, :]) for ref in state_refs]
    state, total = states[0], totals[0]
    if cores == 2:
        upper = lax.rem(lax.axis_index(axis), 2) == 1
        first, second = jnp.where(upper, states[1], state), jnp.where(upper, state, states[1])
        state = jnp.exp(jnp.where(upper, total, totals[1])) * first + second
        state = jnp.where(upper, state[share:], state[:share])
        total = total + totals[1]
    share_ref[:share, :] = state.astype(BF16)
    if share_ref.shape[0] > share:
        share_ref[share:, :] = select_rows(three_parts(total), PAD, width)


def soft_kernel(scale, step, q_ref, k_ref, pack_ref, qt_ref, top_ref, total_ref, summed_ref):
    rows, width = q_ref.shape
    qt_ref[...] = jnp.transpose(q_ref[...])
    value_t = side_by_side(pack_ref, rows, width)
    keep = iota((step, step), 0) <= iota((step, step), 1)
    for start in range(0, rows, step):
        stop = start + step
        scores = dot(k_ref[:stop, :], qt_ref[:, start:stop])
        last = jnp.where(keep, scores[start:, :], NEG)
        scores = jnp.concatenate([scores[:start, :], last], axis=0) if start else last
        top = jnp.max(scores, axis=0, keepdims=True)
        probs = jnp.exp2((scores - top) * scale)
        top_ref[:, start:stop] = top
        total_ref[:, start:stop] = jnp.sum(probs, axis=0, keepdims=True)
        summed_ref[:, start:stop] = dot(value_t[:, :stop], probs.astype(BF16))


def linear_kernel(step, q_ref, k_ref, value_t_ref, cum_row_ref, cum_col_ref, qt_ref, intra_ref):
    rows, width = q_ref.shape
    qt_ref[...] = jnp.transpose(q_ref[...])
    keep = iota((step, step), 0) <= iota((step, step), 1)
    for start in range(0, rows, step):
        stop = start + step
        scores = dot(k_ref[:stop, :], qt_ref[:, start:stop])
        cum_t = cum_row_ref[:, start:stop]
        cum_s = jnp.concatenate([cum_col_ref[:stop, :]] * (step // width), axis=1)
        diff = cum_t - cum_s
        last = jnp.where(keep, diff[start:, :], NEG)
        diff = jnp.concatenate([diff[:start, :], last], axis=0) if start else last
        weights = (scores * jnp.exp(diff)).astype(BF16)
        intra_ref[:, start:stop] = dot(value_t_ref[:, :stop], weights)


def by_chip(position, cores, count, body):
    pl.when(position >= cores)(lambda: body(count))
    pl.when(position < cores)(lambda: body(cores - 1))


def score_kernel(scale, step, axis, cores, offsets, qt_ref, top_ref, total_ref, *refs):
    key_refs, (probs_ref, factor_ref, sum_ref, *new_top_ref) = refs[: len(offsets)], refs[len(offsets) :]
    rows = qt_ref.shape[1]
    position = lax.axis_index(axis)
    chip = position // cores
    away = [
        jnp.where(position - chip * cores >= 1 if apart == 0 else chip >= apart, 0.0, NEG) for apart in offsets
    ]

    def body(count):
        for start in range(0, rows, step):
            mine = slice(start, start + step)
            query = qt_ref[:, mine]
            old = top_ref[:, mine]
            scores = [dot(key_ref[...], query) for key_ref in key_refs[:count]]
            top = old
            for score, off in zip(scores, away):
                top = jnp.maximum(top, jnp.max(score, axis=0, keepdims=True) + off)
            factor = jnp.exp2((old - top) * scale)
            total = total_ref[:, mine] * factor
            for place, (score, off) in enumerate(zip(scores, away)):
                probs = jnp.exp2((score - (top - off)) * scale)
                total = total + jnp.sum(probs, axis=0, keepdims=True)
                probs_ref[place * rows : (place + 1) * rows, mine] = probs.astype(BF16)
            for ref in new_top_ref:
                ref[:, mine] = top
            factor_ref[:, mine] = factor
            sum_ref[:, mine] = total

    pl.when(chip >= 1)(lambda: body(len(offsets)))
    pl.when(chip < 1)(lambda: body(offsets.count(0)))


def carried_state(position, cores, near, shares, width):
    share = width // cores
    chip = position // cores
    upper = position - chip * cores == 1
    carried = jnp.zeros((width, width), F32)
    between = jnp.zeros((1, width), F32)
    for apart in range(1, len(shares) // cores + 1):
        parts = shares[(apart - 1) * cores : apart * cores]
        state = [ref[:share, :].astype(F32) for ref in parts]
        if cores == 2:
            halves = jnp.where(upper, state[1], state[0]), jnp.where(upper, state[0], state[1])
            state = [jnp.concatenate(halves, axis=0)]
        carried = carried + jnp.exp(between + jnp.where(chip >= apart, 0.0, NEG)) * state[0]
        if parts[0].shape[0] > share:
            between = between + sum_of_parts(parts[0][share:, :])
    for ref in near:
        passed = jnp.exp(sum_of_parts(ref[width:, :])) * carried + ref[:width, :].astype(F32)
        carried = jnp.where(upper, passed, carried)
    return carried.astype(BF16)


def put_linear(step, carried, qt_ref, intra_ref, cum_row_ref, buffer):
    width, rows = qt_ref.shape
    for start in range(0, rows, step):
        mine = slice(start, start + step)
        inter = dot(carried, qt_ref[:, mine])
        raw = intra_ref[:, mine] + inter * jnp.exp(cum_row_ref[:, mine])
        square = jnp.sum(raw * raw, axis=0, keepdims=True) * (1.0 / width)
        buffer[mine, :] = jnp.transpose((raw * lax.rsqrt(square + TINY)).astype(BF16))


def value_sum(values_t, probs_ref, mine):
    rows = values_t[0].shape[1]
    terms = [
        dot(value_t, probs_ref[place * rows : (place + 1) * rows, mine]) for place, value_t in enumerate(values_t)
    ]
    return functools.reduce(jnp.add, terms)


def write_out(step, sofar, values_t, probs_ref, sum_ref, carried, linear_refs, outs, buffers, sems):
    lin_qt_ref, intra_ref, cum_row_ref = linear_refs
    linear_buffer, softmax_buffer = buffers
    rows = sum_ref.shape[1]
    linear_copy = pltpu.make_async_copy(linear_buffer, outs[0], sems.at[0])
    softmax_copy = pltpu.make_async_copy(softmax_buffer, outs[1], sems.at[1])
    for start in range(0, rows, step):
        mine = slice(start, start + step)
        summed = sofar(mine)
        if values_t:
            summed = summed + value_sum(values_t, probs_ref, mine)
        softmax_buffer[mine, :] = jnp.transpose((summed / sum_ref[:, mine]).astype(BF16))
    put_linear(step, carried(), lin_qt_ref, intra_ref, cum_row_ref, linear_buffer)
    softmax_copy.start()
    linear_copy.start()
    softmax_copy.wait()
    linear_copy.wait()


def first_kernel(step, axis, cores, *refs):
    lin_qt_ref, intra_ref, cum_row_ref, summed_ref, factor_ref, sum_ref, probs_ref = refs[:7]
    linear_ref, softmax_ref, *scratch, sems = refs[-5:]
    near_states, near_values = refs[7 : 6 + cores], refs[6 + cores : -5]
    width, rows = lin_qt_ref.shape
    position = lax.axis_index(axis)

    @pl.when(position < cores)
    def _():
        write_out(
            step, lambda mine: summed_ref[:, mine] * factor_ref[:, mine],
            [jnp.transpose(ref[...]) for ref in near_values], probs_ref, sum_ref,
            lambda: carried_state(position, cores, near_states, (), width),
            (lin_qt_ref, intra_ref, cum_row_ref), (linear_ref, softmax_ref), scratch, sems,
        )


def early_kernel(step, axis, cores, *refs):
    summed_ref, factor_ref, probs_ref, late_factor_ref, *values, sofar_ref = refs
    width, rows = summed_ref.shape

    @pl.when(lax.axis_index(axis) >= cores)
    def _():
        values_t = [jnp.transpose(ref[...]) for ref in values]
        for start in range(0, rows, step):
            mine = slice(start, start + step)
            summed = summed_ref[:, mine] * factor_ref[:, mine] + value_sum(values_t, probs_ref, mine)
            sofar_ref[:, mine] = summed * late_factor_ref[:, mine]


def late_kernel(step, axis, cores, counts, *refs):
    refs = refs[2:]
    lin_qt_ref, intra_ref, cum_row_ref, sofar_ref, sum_ref, probs_ref = refs[:6]
    linear_ref, softmax_ref, *scratch, sems = refs[-5:]
    near_states = refs[6 : 6 + counts[0]]
    shares = refs[6 + counts[0] : 6 + counts[0] + counts[1]]
    values = refs[6 + counts[0] + counts[1] : -5]
    width, rows = lin_qt_ref.shape
    position = lax.axis_index(axis)

    @pl.when(position >= cores)
    def _():
        write_out(
            step, lambda mine: sofar_ref[:, mine], [jnp.transpose(ref[...]) for ref in values],
            probs_ref, sum_ref, lambda: carried_state(position, cores, near_states, shares, width),
            (lin_qt_ref, intra_ref, cum_row_ref), (linear_ref, softmax_ref), scratch, sems,
        )


def keep_in_hbm(x):
    return pltpu.with_memory_space_constraint(x, pltpu.HBM)


def keep_in_vmem(x):
    return pltpu.with_memory_space_constraint(x, VMEM)


def kept_in_vmem(x):
    return VMEM(x.shape, x.dtype)


def kept_in_hbm(x):
    return pltpu.HBM(x.shape, x.dtype)


def call(body, operands, outs, given=(), written=(), resumed=(), scratch=()):
    size = sum(math.prod(x.shape) * x.dtype.itemsize for x in (*given, *operands, *outs))
    inside, outside = pl.BlockSpec(memory_space=VMEM), pl.BlockSpec(memory_space=pl.ANY)
    hbm = (*given, *resumed)
    scratch = [VMEM(x.shape, x.dtype) for x in (*scratch, *written)]
    moved = len(given) + len(written)
    return pl.pallas_call(
        body,
        out_shape=(*map(kept_in_hbm, written), *map(kept_in_vmem, outs)),
        in_specs=[outside] * len(hbm) + [inside] * len(operands),
        out_specs=(*[outside] * len(written), *[inside] * len(outs)),
        scratch_shapes=[*scratch, pltpu.SemaphoreType.DMA((moved,))] if moved else [],
        input_output_aliases={place: place for place in range(len(resumed))},
        cost_estimate=pl.CostEstimate(flops=0, bytes_accessed=size, transcendentals=0),
        compiler_params=pltpu.CompilerParams(vmem_limit_bytes=KERNEL_VMEM),
    )(*map(keep_in_hbm, hbm), *map(keep_in_vmem, operands))


def on_device(axis, lin_query, lin_key, lin_value, log_decay, soft_query, soft_key, soft_value):
    rows, heads, width = lin_query.shape
    count = lax.axis_size(axis)
    cores = 2 if count % 2 == 0 else 1
    chips = count // cores

    def across(x, apart):
        return lax.ppermute(x, axis, [(i, (i + apart * cores) % count) for i in range(count)])

    def swapped(x):
        return lax.ppermute(x, axis, [(i, i ^ 1) for i in range(count)])

    def near(blocks):
        return [swapped(block) for block in blocks] if cores == 2 else []

    def far(x):
        return [across(x, apart) for apart in range(1, chips)]

    def passed(blocks, after):
        return near(lax.optimization_barrier((block, after))[0] for block in blocks)

    def one_head(lq, lk, lv, decay, sq, sk, sv):
        step = math.gcd(rows, 256)
        scale = math.log2(math.e) / math.sqrt(width)

        def shape(*dims, dtype=F32):
            return jax.ShapeDtypeStruct(dims, dtype)

        def half(*dims):
            return shape(*dims, dtype=BF16)

        row, flat, flat16, block = shape(1, rows), shape(width, rows), half(width, rows), half(rows, width)
        keys, values = far(sk), far(sv)
        soft_vt, state, cum_row, cum_col, lin_vt, lk, lq, sq, own_keys = call(
            state_kernel,
            (),
            (block, half(width + PAD, width), row, shape(rows, width), flat16, block, block, block, block),
            given=(decay, lk, lv, sv, lq, sq, sk),
            scratch=(row, block, block),
        )
        near_states, near_values = near([state]), near([sv])
        qt, top, total, summed = call(
            functools.partial(soft_kernel, scale, step), (sq, own_keys, soft_vt), (flat16, row, row, flat)
        )
        near_states, _ = lax.optimization_barrier((near_states, summed))
        (share,) = call(
            functools.partial(combine_kernel, axis, cores),
            (state, *near_states),
            (half(width // cores + (PAD if chips > 2 else 0), width),),
        )
        shares = far(share)
        lin_qt, intra = call(
            functools.partial(linear_kernel, step), (lq, lk, lin_vt, cum_row, cum_col), (flat16, flat)
        )

        def scored(top, total, blocks, offsets, more):
            return call(
                functools.partial(score_kernel, scale, step, axis, cores, offsets),
                (qt, top, total, *blocks),
                (half(len(blocks) * rows, rows), *[row] * (2 + more)),
            )

        apart = tuple(range(1, chips))
        late_keys = passed(keys, (summed, intra))
        probs, factor, sums, *top = scored(
            top, total, [*near([sk]), *keys], (0,) * (cores - 1) + apart, len(late_keys) > 0
        )
        began = call(
            functools.partial(first_kernel, step, axis, cores),
            (lin_qt, intra, cum_row, summed, factor, sums, probs, *near_states, *near_values),
            (),
            written=(block, block),
        )
        late_values = passed(values, (began, shares))
        late_keys, _ = lax.optimization_barrier((late_keys, values))
        late_factor, late_sums = jnp.ones_like(factor), sums
        if late_keys:
            late_probs, late_factor, late_sums = scored(*top, sums, late_keys, apart, False)
        late_shares = passed(shares, values)
        if cores == 2:
            shares = [part for pair in zip(shares, late_shares) for part in pair]
        (sofar,) = call(
            functools.partial(early_kernel, step, axis, cores),
            (summed, factor, probs, late_factor, *near_values, *values),
            (flat,),
        )
        return call(
            functools.partial(late_kernel, step, axis, cores, (len(near_states), len(shares))),
            (
                lin_qt, intra, cum_row, sofar, late_sums, late_probs if late_keys else probs,
                *near_states, *shares, *late_values,
            ),
            (),
            written=(block, block),
            resumed=began,
        )

    outs = [
        one_head(
            *(x[:, head] for x in (lin_query, lin_key, lin_value)),
            log_decay[head : head + 1],
            *(x[:, head] for x in (soft_query, soft_key, soft_value)),
        )
        for head in range(heads)
    ]
    linear = jnp.stack([pair[0] for pair in outs], axis=1)
    softmax = jnp.stack([pair[1] for pair in outs], axis=1)
    return linear, softmax


def solution(mesh):
    block = P("ctx", "tp", None)
    return jax.shard_map(
        functools.partial(on_device, "ctx"),
        mesh=mesh,
        in_specs=(block, block, block, P("tp", "ctx"), block, block, block),
        out_specs=(block, block),
        check_vma=False,
    )
```

```python
import functools
import math

import jax
import jax.numpy as jnp
from jax import lax
from jax.experimental import pallas as pl
from jax.experimental.pallas import tpu as pltpu
from jax.sharding import PartitionSpec as P

NEG = -1e30
TINY = 1e-6
PAD = 16
KERNEL_VMEM = 16 * 2**20
F32 = jnp.float32
BF16 = jnp.bfloat16
VMEM = pltpu.VMEM


def dot(a, b):
    return lax.dot_general(a, b, (((1,), (0,)), ((), ())), preferred_element_type=F32)


def three_parts(x):
    high = x.astype(BF16)
    rest = x - high.astype(F32)
    middle = rest.astype(BF16)
    low = (rest - middle.astype(F32)).astype(BF16)
    return high, middle, low


def iota(shape, dim):
    return lax.broadcasted_iota(jnp.int32, shape, dim)


def select_rows(parts, rows, width):
    row = iota((rows, width), 0)
    out = jnp.zeros((rows, width), F32)
    for number, part in enumerate(parts):
        out = jnp.where(row == number, part.astype(F32), out)
    return out.astype(BF16)


def side_by_side(ref, rows, width):
    pieces = [ref[left : left + width, :] for left in range(0, rows, width)]
    return pieces[0] if len(pieces) == 1 else jnp.concatenate(pieces, axis=1)


def state_kernel(
    decay_hbm, key_hbm, value_hbm, soft_value_hbm, query_hbm, soft_query_hbm, soft_key_hbm,
    soft_vt_ref, state_ref, cum_row_ref, cum_col_ref, value_t_ref, key_ref, query_ref, soft_query_ref, soft_key_ref,
    decay_ref, value_ref, soft_value_ref, sems,
):
    copies = [
        pltpu.make_async_copy(source, target, sems.at[place])
        for place, (source, target) in enumerate(
            (
                (decay_hbm, decay_ref),
                (key_hbm, key_ref),
                (value_hbm, value_ref),
                (soft_value_hbm, soft_value_ref),
                (soft_query_hbm, soft_query_ref),
                (soft_key_hbm, soft_key_ref),
                (query_hbm, query_ref),
            )
        )
    ]
    for copy in copies:
        copy.start()
    rows, width = key_ref.shape
    upto = (iota((rows, rows), 0) <= iota((rows, rows), 1)).astype(F32).astype(BF16)
    copies[0].wait()
    parts = select_rows(three_parts(decay_ref[...]), PAD, rows)
    cum_row = jnp.sum(dot(parts, upto), axis=0, keepdims=True)
    cum_row_ref[...] = cum_row
    cum_col = jnp.transpose(jnp.broadcast_to(cum_row, (width, rows)))
    cum_col_ref[...] = cum_col
    total = cum_col[rows - 1 :, :]
    for copy in copies[1:4]:
        copy.wait()
    decayed = (key_ref[...].astype(F32) * jnp.exp(total - cum_col)).astype(BF16)
    value_t = jnp.transpose(value_ref[...])
    value_t_ref[...] = value_t
    state_ref[:width, :] = dot(value_t, decayed).astype(BF16)
    state_ref[width:, :] = select_rows(three_parts(total), PAD, width)
    for left in range(0, rows, width):
        soft_vt_ref[left : left + width, :] = jnp.transpose(soft_value_ref[left : left + width, :])
    for copy in copies[4:]:
        copy.wait()


def sum_of_parts(tail):
    tail = tail.astype(F32)
    return tail[0:1] + tail[1:2] + tail[2:3]


def combine_kernel(axis, cores, *refs):
    *state_refs, share_ref = refs
    width = share_ref.shape[1]
    share = width // cores
    states = [ref[:width, :].astype(F32) for ref in state_refs]
    totals = [sum_of_parts(ref[width:, :]) for ref in state_refs]
    state, total = states[0], totals[0]
    if cores == 2:
        upper = lax.rem(lax.axis_index(axis), 2) == 1
        first, second = jnp.where(upper, states[1], state), jnp.where(upper, state, states[1])
        state = jnp.exp(jnp.where(upper, total, totals[1])) * first + second
        state = jnp.where(upper, state[share:], state[:share])
        total = total + totals[1]
    share_ref[:share, :] = state.astype(BF16)
    if share_ref.shape[0] > share:
        share_ref[share:, :] = select_rows(three_parts(total), PAD, width)


def soft_kernel(scale, step, q_ref, k_ref, pack_ref, qt_ref, top_ref, total_ref, summed_ref):
    rows, width = q_ref.shape
    qt_ref[...] = jnp.transpose(q_ref[...])
    value_t = side_by_side(pack_ref, rows, width)
    keep = iota((step, step), 0) <= iota((step, step), 1)
    for start in range(0, rows, step):
        stop = start + step
        scores = dot(k_ref[:stop, :], qt_ref[:, start:stop])
        last = jnp.where(keep, scores[start:, :], NEG)
        scores = jnp.concatenate([scores[:start, :], last], axis=0) if start else last
        top = jnp.max(scores, axis=0, keepdims=True)
        probs = jnp.exp2((scores - top) * scale)
        top_ref[:, start:stop] = top
        total_ref[:, start:stop] = jnp.sum(probs, axis=0, keepdims=True)
        summed_ref[:, start:stop] = dot(value_t[:, :stop], probs.astype(BF16))


def linear_kernel(step, q_ref, k_ref, value_t_ref, cum_row_ref, cum_col_ref, qt_ref, intra_ref):
    rows, width = q_ref.shape
    qt_ref[...] = jnp.transpose(q_ref[...])
    keep = iota((step, step), 0) <= iota((step, step), 1)
    for start in range(0, rows, step):
        stop = start + step
        scores = dot(k_ref[:stop, :], qt_ref[:, start:stop])
        cum_t = cum_row_ref[:, start:stop]
        cum_s = jnp.concatenate([cum_col_ref[:stop, :]] * (step // width), axis=1)
        diff = cum_t - cum_s
        last = jnp.where(keep, diff[start:, :], NEG)
        diff = jnp.concatenate([diff[:start, :], last], axis=0) if start else last
        weights = (scores * jnp.exp(diff)).astype(BF16)
        intra_ref[:, start:stop] = dot(value_t_ref[:, :stop], weights)


def by_chip(position, cores, count, body):
    pl.when(position >= cores)(lambda: body(count))
    pl.when(position < cores)(lambda: body(cores - 1))


def score_kernel(scale, step, axis, cores, offsets, qt_ref, top_ref, total_ref, *refs):
    key_refs, (probs_ref, factor_ref, sum_ref, *new_top_ref) = refs[: len(offsets)], refs[len(offsets) :]
    rows = qt_ref.shape[1]
    position = lax.axis_index(axis)
    chip = position // cores
    away = [
        jnp.where(position - chip * cores >= 1 if apart == 0 else chip >= apart, 0.0, NEG) for apart in offsets
    ]

    def body(count):
        for start in range(0, rows, step):
            mine = slice(start, start + step)
            query = qt_ref[:, mine]
            old = top_ref[:, mine]
            scores = [dot(key_ref[...], query) for key_ref in key_refs[:count]]
            top = old
            for score, off in zip(scores, away):
                top = jnp.maximum(top, jnp.max(score, axis=0, keepdims=True) + off)
            factor = jnp.exp2((old - top) * scale)
            total = total_ref[:, mine] * factor
            for place, (score, off) in enumerate(zip(scores, away)):
                probs = jnp.exp2((score - (top - off)) * scale)
                total = total + jnp.sum(probs, axis=0, keepdims=True)
                probs_ref[place * rows : (place + 1) * rows, mine] = probs.astype(BF16)
            for ref in new_top_ref:
                ref[:, mine] = top
            factor_ref[:, mine] = factor
            sum_ref[:, mine] = total

    pl.when(chip >= 1)(lambda: body(len(offsets)))
    pl.when(chip < 1)(lambda: body(offsets.count(0)))


def carried_state(position, cores, near, shares, width):
    share = width // cores
    chip = position // cores
    upper = position - chip * cores == 1
    carried = jnp.zeros((width, width), F32)
    between = jnp.zeros((1, width), F32)
    for apart in range(1, len(shares) // cores + 1):
        parts = shares[(apart - 1) * cores : apart * cores]
        state = [ref[:share, :].astype(F32) for ref in parts]
        if cores == 2:
            halves = jnp.where(upper, state[1], state[0]), jnp.where(upper, state[0], state[1])
            state = [jnp.concatenate(halves, axis=0)]
        carried = carried + jnp.exp(between + jnp.where(chip >= apart, 0.0, NEG)) * state[0]
        if parts[0].shape[0] > share:
            between = between + sum_of_parts(parts[0][share:, :])
    for ref in near:
        passed = jnp.exp(sum_of_parts(ref[width:, :])) * carried + ref[:width, :].astype(F32)
        carried = jnp.where(upper, passed, carried)
    return carried.astype(BF16)


def put_linear(step, carried, qt_ref, intra_ref, cum_row_ref, buffer):
    width, rows = qt_ref.shape
    for start in range(0, rows, step):
        mine = slice(start, start + step)
        inter = dot(carried, qt_ref[:, mine])
        raw = intra_ref[:, mine] + inter * jnp.exp(cum_row_ref[:, mine])
        square = jnp.sum(raw * raw, axis=0, keepdims=True) * (1.0 / width)
        buffer[mine, :] = jnp.transpose((raw * lax.rsqrt(square + TINY)).astype(BF16))


def value_sum(values_t, probs_ref, mine):
    rows = values_t[0].shape[1]
    terms = [
        dot(value_t, probs_ref[place * rows : (place + 1) * rows, mine]) for place, value_t in enumerate(values_t)
    ]
    return functools.reduce(jnp.add, terms)


def write_out(step, sofar, values_t, probs_ref, sum_ref, carried, linear_refs, outs, buffers, sems):
    lin_qt_ref, intra_ref, cum_row_ref = linear_refs
    linear_buffer, softmax_buffer = buffers
    rows = sum_ref.shape[1]
    linear_copy = pltpu.make_async_copy(linear_buffer, outs[0], sems.at[0])
    softmax_copy = pltpu.make_async_copy(softmax_buffer, outs[1], sems.at[1])
    for start in range(0, rows, step):
        mine = slice(start, start + step)
        summed = sofar(mine)
        if values_t:
            summed = summed + value_sum(values_t, probs_ref, mine)
        softmax_buffer[mine, :] = jnp.transpose((summed / sum_ref[:, mine]).astype(BF16))
    softmax_copy.start()
    put_linear(step, carried(), lin_qt_ref, intra_ref, cum_row_ref, linear_buffer)
    linear_copy.start()
    softmax_copy.wait()
    linear_copy.wait()


def early_kernel(step, axis, cores, near_count, *refs):
    lin_qt_ref, intra_ref, cum_row_ref, summed_ref, factor_ref, sum_ref, probs_ref, late_factor_ref = refs[:8]
    linear_ref, softmax_ref, sofar_ref, *scratch, sems = refs[-6:]
    near_states, values = refs[8 : 8 + near_count], refs[8 + near_count : -6]
    width, rows = lin_qt_ref.shape
    position = lax.axis_index(axis)

    def scaled(mine):
        return summed_ref[:, mine] * factor_ref[:, mine]

    @pl.when(position >= cores)
    def _():
        values_t = [side_by_side(ref, rows, width) for ref in values[:near_count]]
        values_t += [jnp.transpose(ref[...]) for ref in values[near_count:]]
        for start in range(0, rows, step):
            mine = slice(start, start + step)
            summed = scaled(mine) + value_sum(values_t, probs_ref, mine)
            sofar_ref[:, mine] = summed * late_factor_ref[:, mine]

    @pl.when(position < cores)
    def _():
        write_out(
            step, scaled, [side_by_side(ref, rows, width) for ref in values[:near_count]], probs_ref, sum_ref,
            lambda: carried_state(position, cores, near_states, (), width),
            (lin_qt_ref, intra_ref, cum_row_ref), (linear_ref, softmax_ref), scratch, sems,
        )


def late_kernel(step, axis, cores, counts, *refs):
    refs = refs[2:]
    lin_qt_ref, intra_ref, cum_row_ref, sofar_ref, sum_ref, probs_ref = refs[:6]
    linear_ref, softmax_ref, *scratch, sems = refs[-5:]
    near_states = refs[6 : 6 + counts[0]]
    shares = refs[6 + counts[0] : 6 + counts[0] + counts[1]]
    values = refs[6 + counts[0] + counts[1] : -5]
    width, rows = lin_qt_ref.shape
    position = lax.axis_index(axis)

    @pl.when(position >= cores)
    def _():
        write_out(
            step, lambda mine: sofar_ref[:, mine], [jnp.transpose(ref[...]) for ref in values],
            probs_ref, sum_ref, lambda: carried_state(position, cores, near_states, shares, width),
            (lin_qt_ref, intra_ref, cum_row_ref), (linear_ref, softmax_ref), scratch, sems,
        )


def keep_in_hbm(x):
    return pltpu.with_memory_space_constraint(x, pltpu.HBM)


def keep_in_vmem(x):
    return pltpu.with_memory_space_constraint(x, VMEM)


def kept_in_vmem(x):
    return VMEM(x.shape, x.dtype)


def kept_in_hbm(x):
    return pltpu.HBM(x.shape, x.dtype)


def call(body, operands, outs, given=(), written=(), resumed=(), scratch=()):
    size = sum(math.prod(x.shape) * x.dtype.itemsize for x in (*given, *operands, *outs))
    inside, outside = pl.BlockSpec(memory_space=VMEM), pl.BlockSpec(memory_space=pl.ANY)
    hbm = (*given, *resumed)
    scratch = [VMEM(x.shape, x.dtype) for x in (*scratch, *written)]
    moved = len(given) + len(written)
    return pl.pallas_call(
        body,
        out_shape=(*map(kept_in_hbm, written), *map(kept_in_vmem, outs)),
        in_specs=[outside] * len(hbm) + [inside] * len(operands),
        out_specs=(*[outside] * len(written), *[inside] * len(outs)),
        scratch_shapes=[*scratch, pltpu.SemaphoreType.DMA((moved,))] if moved else [],
        input_output_aliases={place: place for place in range(len(resumed))},
        cost_estimate=pl.CostEstimate(flops=0, bytes_accessed=size, transcendentals=0),
        compiler_params=pltpu.CompilerParams(vmem_limit_bytes=KERNEL_VMEM),
    )(*map(keep_in_hbm, hbm), *map(keep_in_vmem, operands))


def on_device(axis, lin_query, lin_key, lin_value, log_decay, soft_query, soft_key, soft_value):
    rows, heads, width = lin_query.shape
    count = lax.axis_size(axis)
    cores = 2 if count % 2 == 0 else 1
    chips = count // cores

    def across(x, apart):
        return lax.ppermute(x, axis, [(i, (i + apart * cores) % count) for i in range(count)])

    def swapped(x):
        return lax.ppermute(x, axis, [(i, i ^ 1) for i in range(count)])

    def near(blocks):
        return [swapped(block) for block in blocks] if cores == 2 else []

    def far(x):
        return [across(x, apart) for apart in range(1, chips)]

    def passed(blocks, after):
        return near(lax.optimization_barrier((block, after))[0] for block in blocks)

    def one_head(lq, lk, lv, decay, sq, sk, sv):
        step = math.gcd(rows, 256)
        scale = math.log2(math.e) / math.sqrt(width)

        def shape(*dims, dtype=F32):
            return jax.ShapeDtypeStruct(dims, dtype)

        def half(*dims):
            return shape(*dims, dtype=BF16)

        row, flat, flat16, block = shape(1, rows), shape(width, rows), half(width, rows), half(rows, width)
        keys, values = far(sk), far(sv)
        soft_vt, state, cum_row, cum_col, lin_vt, lk, lq, sq, own_keys = call(
            state_kernel,
            (),
            (block, half(width + PAD, width), row, shape(rows, width), flat16, block, block, block, block),
            given=(decay, lk, lv, sv, lq, sq, sk),
            scratch=(row, block, block),
        )
        near_states, near_values = near([state]), near([soft_vt])
        qt, top, total, summed = call(
            functools.partial(soft_kernel, scale, step), (sq, own_keys, soft_vt), (flat16, row, row, flat)
        )
        (share,) = call(
            functools.partial(combine_kernel, axis, cores),
            (state, *near_states),
            (half(width // cores + (PAD if chips > 2 else 0), width),),
        )
        shares = far(share)
        lin_qt, intra = call(
            functools.partial(linear_kernel, step), (lq, lk, lin_vt, cum_row, cum_col), (flat16, flat)
        )

        def scored(top, total, blocks, offsets, more):
            return call(
                functools.partial(score_kernel, scale, step, axis, cores, offsets),
                (qt, top, total, *blocks),
                (half(len(blocks) * rows, rows), *[row] * (2 + more)),
            )

        apart = tuple(range(1, chips))
        late_keys = passed(keys, (summed, intra))
        probs, factor, sums, *top = scored(
            top, total, [*near([sk]), *keys], (0,) * (cores - 1) + apart, len(late_keys) > 0
        )
        late_values = passed(values, (factor, shares))
        late_keys, _ = lax.optimization_barrier((late_keys, values))
        late_factor, late_sums = jnp.ones_like(factor), sums
        if late_keys:
            late_probs, late_factor, late_sums = scored(*top, sums, late_keys, apart, False)
        late_shares = passed(shares, values)
        if cores == 2:
            shares = [part for pair in zip(shares, late_shares) for part in pair]
        *began, sofar = call(
            functools.partial(early_kernel, step, axis, cores, len(near_states)),
            (
                lin_qt, intra, cum_row, summed, factor, sums, probs, late_factor,
                *near_states, *near_values, *values,
            ),
            (flat,),
            written=(block, block),
        )
        return call(
            functools.partial(late_kernel, step, axis, cores, (len(near_states), len(shares))),
            (
                lin_qt, intra, cum_row, sofar, late_sums, late_probs if late_keys else probs,
                *near_states, *shares, *late_values,
            ),
            (),
            written=(block, block),
            resumed=began,
        )

    outs = [
        one_head(
            *(x[:, head] for x in (lin_query, lin_key, lin_value)),
            log_decay[head : head + 1],
            *(x[:, head] for x in (soft_query, soft_key, soft_value)),
        )
        for head in range(heads)
    ]
    linear = jnp.stack([pair[0] for pair in outs], axis=1)
    softmax = jnp.stack([pair[1] for pair in outs], axis=1)
    return linear, softmax


def solution(mesh):
    block = P("ctx", "tp", None)
    return jax.shard_map(
        functools.partial(on_device, "ctx"),
        mesh=mesh,
        in_specs=(block, block, block, P("tp", "ctx"), block, block, block),
        out_specs=(block, block),
        check_vma=False,
    )
```

```python
import functools
import math

import jax
import jax.numpy as jnp
from jax import lax
from jax.experimental import pallas as pl
from jax.experimental.pallas import tpu as pltpu
from jax.sharding import PartitionSpec as P

NEG = -1e30
TINY = 1e-6
PAD = 16
STEP = 256
KERNEL_VMEM = 16 * 2**20
F32 = jnp.float32
BF16 = jnp.bfloat16
VMEM = pltpu.VMEM


def dot(a, b):
    return lax.dot_general(a, b, (((1,), (0,)), ((), ())), preferred_element_type=F32)


def three_parts(x):
    high = x.astype(BF16)
    rest = x - high.astype(F32)
    middle = rest.astype(BF16)
    low = (rest - middle.astype(F32)).astype(BF16)
    return high, middle, low


def iota(shape, dim):
    return lax.broadcasted_iota(jnp.int32, shape, dim)


def select_rows(parts, rows, width):
    row = iota((rows, width), 0)
    out = jnp.zeros((rows, width), F32)
    for number, part in enumerate(parts):
        out = jnp.where(row == number, part.astype(F32), out)
    return out.astype(BF16)


def side_by_side(ref, rows, width):
    pieces = [ref[left : left + width, :] for left in range(0, rows, width)]
    return pieces[0] if len(pieces) == 1 else jnp.concatenate(pieces, axis=1)


def state_kernel(
    decay_hbm, key_hbm, value_hbm, soft_value_hbm, query_hbm, soft_query_hbm, soft_key_hbm,
    soft_vt_ref, state_ref, cum_row_ref, cum_col_ref, value_t_ref, key_ref, query_ref, soft_query_ref, soft_key_ref,
    decay_ref, value_ref, soft_value_ref, sems,
):
    copies = [
        pltpu.make_async_copy(source, target, sems.at[place])
        for place, (source, target) in enumerate(
            (
                (decay_hbm, decay_ref),
                (key_hbm, key_ref),
                (value_hbm, value_ref),
                (soft_value_hbm, soft_value_ref),
                (soft_query_hbm, soft_query_ref),
                (soft_key_hbm, soft_key_ref),
                (query_hbm, query_ref),
            )
        )
    ]
    for copy in copies:
        copy.start()
    rows, width = key_ref.shape
    upto = (iota((rows, rows), 0) <= iota((rows, rows), 1)).astype(F32).astype(BF16)
    copies[0].wait()
    parts = select_rows(three_parts(decay_ref[...]), PAD, rows)
    cum_row = jnp.sum(dot(parts, upto), axis=0, keepdims=True)
    cum_row_ref[...] = cum_row
    cum_col = jnp.transpose(jnp.broadcast_to(cum_row, (width, rows)))
    cum_col_ref[...] = cum_col
    total = cum_col[rows - 1 :, :]
    for copy in copies[1:4]:
        copy.wait()
    decayed = (key_ref[...].astype(F32) * jnp.exp(total - cum_col)).astype(BF16)
    value_t = jnp.transpose(value_ref[...])
    value_t_ref[...] = value_t
    state_ref[:width, :] = dot(value_t, decayed).astype(BF16)
    state_ref[width:, :] = select_rows(three_parts(total), PAD, width)
    for left in range(0, rows, width):
        soft_vt_ref[left : left + width, :] = jnp.transpose(soft_value_ref[left : left + width, :])
    for copy in copies[4:]:
        copy.wait()


def sum_of_parts(tail):
    tail = tail.astype(F32)
    return tail[0:1] + tail[1:2] + tail[2:3]


def combine_kernel(axis, cores, *refs):
    *state_refs, share_ref = refs
    width = share_ref.shape[1]
    share = width // cores
    states = [ref[:width, :].astype(F32) for ref in state_refs]
    totals = [sum_of_parts(ref[width:, :]) for ref in state_refs]
    state, total = states[0], totals[0]
    if cores == 2:
        upper = lax.rem(lax.axis_index(axis), 2) == 1
        first, second = jnp.where(upper, states[1], state), jnp.where(upper, state, states[1])
        state = jnp.exp(jnp.where(upper, total, totals[1])) * first + second
        state = jnp.where(upper, state[share:], state[:share])
        total = total + totals[1]
    share_ref[:share, :] = state.astype(BF16)
    if share_ref.shape[0] > share:
        share_ref[share:, :] = select_rows(three_parts(total), PAD, width)


def soft_kernel(scale, step, q_ref, k_ref, pack_ref, qt_ref, top_ref, total_ref, summed_ref):
    rows, width = q_ref.shape
    qt_ref[...] = jnp.transpose(q_ref[...])
    value_t = side_by_side(pack_ref, rows, width)
    keep = iota((step, step), 0) <= iota((step, step), 1)
    for start in range(0, rows, step):
        stop = start + step
        scores = dot(k_ref[:stop, :], qt_ref[:, start:stop])
        last = jnp.where(keep, scores[start:, :], NEG)
        scores = jnp.concatenate([scores[:start, :], last], axis=0) if start else last
        top = jnp.max(scores, axis=0, keepdims=True)
        probs = jnp.exp2((scores - top) * scale)
        top_ref[:, start:stop] = top
        total_ref[:, start:stop] = jnp.sum(probs, axis=0, keepdims=True)
        summed_ref[:, start:stop] = dot(value_t[:, :stop], probs.astype(BF16))


def linear_kernel(step, q_ref, k_ref, value_t_ref, cum_row_ref, cum_col_ref, qt_ref, intra_ref):
    rows, width = q_ref.shape
    qt_ref[...] = jnp.transpose(q_ref[...])
    keep = iota((step, step), 0) <= iota((step, step), 1)
    for start in range(0, rows, step):
        stop = start + step
        scores = dot(k_ref[:stop, :], qt_ref[:, start:stop])
        cum_t = cum_row_ref[:, start:stop]
        cum_s = jnp.concatenate([cum_col_ref[:stop, :]] * (step // width), axis=1)
        diff = cum_t - cum_s
        last = jnp.where(keep, diff[start:, :], NEG)
        diff = jnp.concatenate([diff[:start, :], last], axis=0) if start else last
        weights = (scores * jnp.exp(diff)).astype(BF16)
        intra_ref[:, start:stop] = dot(value_t_ref[:, :stop], weights)


def by_chip(position, cores, count, body):
    pl.when(position >= cores)(lambda: body(count))
    pl.when(position < cores)(lambda: body(cores - 1))


def score_kernel(scale, step, axis, cores, offsets, qt_ref, top_ref, total_ref, *refs):
    key_refs, (probs_ref, factor_ref, sum_ref, *new_top_ref) = refs[: len(offsets)], refs[len(offsets) :]
    rows = qt_ref.shape[1]
    position = lax.axis_index(axis)
    chip = position // cores
    away = [
        jnp.where(position - chip * cores >= 1 if apart == 0 else chip >= apart, 0.0, NEG) for apart in offsets
    ]

    def body(count):
        for start in range(0, rows, step):
            mine = slice(start, start + step)
            query = qt_ref[:, mine]
            old = top_ref[:, mine]
            scores = [dot(key_ref[...], query) for key_ref in key_refs[:count]]
            top = old
            for score, off in zip(scores, away):
                top = jnp.maximum(top, jnp.max(score, axis=0, keepdims=True) + off)
            factor = jnp.exp2((old - top) * scale)
            total = total_ref[:, mine] * factor
            for place, (score, off) in enumerate(zip(scores, away)):
                probs = jnp.exp2((score - (top - off)) * scale)
                total = total + jnp.sum(probs, axis=0, keepdims=True)
                probs_ref[place * rows : (place + 1) * rows, mine] = probs.astype(BF16)
            for ref in new_top_ref:
                ref[:, mine] = top
            factor_ref[:, mine] = factor
            sum_ref[:, mine] = total

    pl.when(chip >= 1)(lambda: body(len(offsets)))
    pl.when(chip < 1)(lambda: body(offsets.count(0)))


def carried_state(position, cores, near, shares, width):
    share = width // cores
    chip = position // cores
    upper = position - chip * cores == 1
    carried = jnp.zeros((width, width), F32)
    between = jnp.zeros((1, width), F32)
    for apart in range(1, len(shares) // cores + 1):
        parts = shares[(apart - 1) * cores : apart * cores]
        state = [ref[:share, :].astype(F32) for ref in parts]
        if cores == 2:
            halves = jnp.where(upper, state[1], state[0]), jnp.where(upper, state[0], state[1])
            state = [jnp.concatenate(halves, axis=0)]
        carried = carried + jnp.exp(between + jnp.where(chip >= apart, 0.0, NEG)) * state[0]
        if parts[0].shape[0] > share:
            between = between + sum_of_parts(parts[0][share:, :])
    for ref in near:
        passed = jnp.exp(sum_of_parts(ref[width:, :])) * carried + ref[:width, :].astype(F32)
        carried = jnp.where(upper, passed, carried)
    return carried.astype(BF16)


def value_sum(values_t, probs_ref, mine):
    rows = values_t[0].shape[1]
    terms = [
        dot(value_t, probs_ref[place * rows : (place + 1) * rows, mine]) for place, value_t in enumerate(values_t)
    ]
    return functools.reduce(jnp.add, terms)


def write_out(step, sofar, values_t, probs_ref, sum_ref, carried, linear_refs, outs, buffers, sems):
    lin_qt_ref, intra_ref, cum_row_ref = linear_refs
    width, rows = lin_qt_ref.shape
    copies = []

    def put(place, mine, block):
        buffers[place][mine, :] = jnp.transpose(block.astype(BF16))
        span = pl.ds(mine.start, step)
        copy = pltpu.make_async_copy(buffers[place].at[span], outs[place].at[span], sems.at[len(copies)])
        copy.start()
        copies.append(copy)

    for start in range(0, rows, step):
        mine = slice(start, start + step)
        inter = dot(carried, lin_qt_ref[:, mine])
        summed = sofar(mine)
        if values_t:
            summed = summed + value_sum(values_t, probs_ref, mine)
        raw = intra_ref[:, mine] + inter * jnp.exp(cum_row_ref[:, mine])
        square = jnp.sum(raw * raw, axis=0, keepdims=True) * (1.0 / width)
        put(0, mine, raw * lax.rsqrt(square + TINY))
        put(1, mine, summed * (1.0 / sum_ref[:, mine]))
    for copy in copies:
        copy.wait()


def early_kernel(step, axis, cores, near_count, *refs):
    lin_qt_ref, intra_ref, cum_row_ref, summed_ref, factor_ref, sum_ref, probs_ref, late_factor_ref = refs[:8]
    linear_ref, softmax_ref, sofar_ref, *scratch, sems = refs[-6:]
    near_states, values = refs[8 : 8 + near_count], refs[8 + near_count : -6]
    width, rows = lin_qt_ref.shape
    position = lax.axis_index(axis)

    def scaled(mine):
        return summed_ref[:, mine] * factor_ref[:, mine]

    @pl.when(position >= cores)
    def _():
        values_t = [side_by_side(ref, rows, width) for ref in values[:near_count]]
        values_t += [jnp.transpose(ref[...]) for ref in values[near_count:]]
        for start in range(0, rows, step):
            mine = slice(start, start + step)
            summed = scaled(mine) + value_sum(values_t, probs_ref, mine)
            sofar_ref[:, mine] = summed * late_factor_ref[:, mine]

    @pl.when(position < cores)
    def _():
        write_out(
            step, scaled, [side_by_side(ref, rows, width) for ref in values[:near_count]], probs_ref, sum_ref,
            carried_state(position, cores, near_states, (), width),
            (lin_qt_ref, intra_ref, cum_row_ref), (linear_ref, softmax_ref), scratch, sems,
        )


def late_kernel(step, axis, cores, counts, *refs):
    refs = refs[2:]
    lin_qt_ref, intra_ref, cum_row_ref, sofar_ref, sum_ref, probs_ref = refs[:6]
    linear_ref, softmax_ref, *scratch, sems = refs[-5:]
    near_states = refs[6 : 6 + counts[0]]
    shares = refs[6 + counts[0] : 6 + counts[0] + counts[1]]
    values = refs[6 + counts[0] + counts[1] : -5]
    width, rows = lin_qt_ref.shape
    position = lax.axis_index(axis)

    @pl.when(position >= cores)
    def _():
        write_out(
            step, lambda mine: sofar_ref[:, mine], [jnp.transpose(ref[...]) for ref in values],
            probs_ref, sum_ref, carried_state(position, cores, near_states, shares, width),
            (lin_qt_ref, intra_ref, cum_row_ref), (linear_ref, softmax_ref), scratch, sems,
        )


def keep_in_hbm(x):
    return pltpu.with_memory_space_constraint(x, pltpu.HBM)


def keep_in_vmem(x):
    return pltpu.with_memory_space_constraint(x, VMEM)


def kept_in_vmem(x):
    return VMEM(x.shape, x.dtype)


def kept_in_hbm(x):
    return pltpu.HBM(x.shape, x.dtype)


def call(body, operands, outs, given=(), written=(), resumed=(), scratch=()):
    size = sum(math.prod(x.shape) * x.dtype.itemsize for x in (*given, *operands, *outs))
    inside, outside = pl.BlockSpec(memory_space=VMEM), pl.BlockSpec(memory_space=pl.ANY)
    hbm = (*given, *resumed)
    scratch = [VMEM(x.shape, x.dtype) for x in (*scratch, *written)]
    moved = len(given) + sum(x.shape[0] // math.gcd(x.shape[0], STEP) for x in written)
    return pl.pallas_call(
        body,
        out_shape=(*map(kept_in_hbm, written), *map(kept_in_vmem, outs)),
        in_specs=[outside] * len(hbm) + [inside] * len(operands),
        out_specs=(*[outside] * len(written), *[inside] * len(outs)),
        scratch_shapes=[*scratch, pltpu.SemaphoreType.DMA((moved,))] if moved else [],
        input_output_aliases={place: place for place in range(len(resumed))},
        cost_estimate=pl.CostEstimate(flops=0, bytes_accessed=size, transcendentals=0),
        compiler_params=pltpu.CompilerParams(vmem_limit_bytes=KERNEL_VMEM),
    )(*map(keep_in_hbm, hbm), *map(keep_in_vmem, operands))


def on_device(axis, lin_query, lin_key, lin_value, log_decay, soft_query, soft_key, soft_value):
    rows, heads, width = lin_query.shape
    count = lax.axis_size(axis)
    cores = 2 if count % 2 == 0 else 1
    chips = count // cores

    def across(x, apart):
        return lax.ppermute(x, axis, [(i, (i + apart * cores) % count) for i in range(count)])

    def swapped(x):
        return lax.ppermute(x, axis, [(i, i ^ 1) for i in range(count)])

    def near(blocks):
        return [swapped(block) for block in blocks] if cores == 2 else []

    def far(x):
        return [across(x, apart) for apart in range(1, chips)]

    def passed(blocks, after):
        return near(lax.optimization_barrier((block, after))[0] for block in blocks)

    def one_head(lq, lk, lv, decay, sq, sk, sv):
        step = math.gcd(rows, STEP)
        scale = math.log2(math.e) / math.sqrt(width)

        def shape(*dims, dtype=F32):
            return jax.ShapeDtypeStruct(dims, dtype)

        def half(*dims):
            return shape(*dims, dtype=BF16)

        row, flat, flat16, block = shape(1, rows), shape(width, rows), half(width, rows), half(rows, width)
        keys, values = far(sk), far(sv)
        soft_vt, state, cum_row, cum_col, lin_vt, lk, lq, sq, own_keys = call(
            state_kernel,
            (),
            (block, half(width + PAD, width), row, shape(rows, width), flat16, block, block, block, block),
            given=(decay, lk, lv, sv, lq, sq, sk),
            scratch=(row, block, block),
        )
        near_states, near_values = near([state]), near([soft_vt])
        qt, top, total, summed = call(
            functools.partial(soft_kernel, scale, step), (sq, own_keys, soft_vt), (flat16, row, row, flat)
        )
        (share,) = call(
            functools.partial(combine_kernel, axis, cores),
            (state, *near_states),
            (half(width // cores + (PAD if chips > 2 else 0), width),),
        )
        shares = far(share)
        lin_qt, intra = call(
            functools.partial(linear_kernel, step), (lq, lk, lin_vt, cum_row, cum_col), (flat16, flat)
        )

        def scored(top, total, blocks, offsets, more):
            return call(
                functools.partial(score_kernel, scale, step, axis, cores, offsets),
                (qt, top, total, *blocks),
                (half(len(blocks) * rows, rows), *[row] * (2 + more)),
            )

        apart = tuple(range(1, chips))
        late_keys = passed(keys, (summed, intra))
        probs, factor, sums, *top = scored(
            top, total, [*near([sk]), *keys], (0,) * (cores - 1) + apart, len(late_keys) > 0
        )
        late_values = passed(values, (factor, shares))
        late_keys, _ = lax.optimization_barrier((late_keys, values))
        late_factor, late_sums = jnp.ones_like(factor), sums
        if late_keys:
            late_probs, late_factor, late_sums = scored(*top, sums, late_keys, apart, False)
        late_shares = passed(shares, values)
        if cores == 2:
            shares = [part for pair in zip(shares, late_shares) for part in pair]
        *began, sofar = call(
            functools.partial(early_kernel, step, axis, cores, len(near_states)),
            (
                lin_qt, intra, cum_row, summed, factor, sums, probs, late_factor,
                *near_states, *near_values, *values,
            ),
            (flat,),
            written=(block, block),
        )
        return call(
            functools.partial(late_kernel, step, axis, cores, (len(near_states), len(shares))),
            (
                lin_qt, intra, cum_row, sofar, late_sums, late_probs if late_keys else probs,
                *near_states, *shares, *late_values,
            ),
            (),
            written=(block, block),
            resumed=began,
        )

    outs = [
        one_head(
            *(x[:, head] for x in (lin_query, lin_key, lin_value)),
            log_decay[head : head + 1],
            *(x[:, head] for x in (soft_query, soft_key, soft_value)),
        )
        for head in range(heads)
    ]
    linear = jnp.stack([pair[0] for pair in outs], axis=1)
    softmax = jnp.stack([pair[1] for pair in outs], axis=1)
    return linear, softmax


def solution(mesh):
    block = P("ctx", "tp", None)
    return jax.shard_map(
        functools.partial(on_device, "ctx"),
        mesh=mesh,
        in_specs=(block, block, block, P("tp", "ctx"), block, block, block),
        out_specs=(block, block),
        check_vma=False,
    )
```

```python
import functools
import math

import jax
import jax.numpy as jnp
from jax import lax
from jax.experimental import pallas as pl
from jax.experimental.pallas import tpu as pltpu
from jax.sharding import PartitionSpec as P

NEG = -1e30
TINY = 1e-6
PAD = 16
STEP = 256
KERNEL_VMEM = 16 * 2**20
F32 = jnp.float32
BF16 = jnp.bfloat16
VMEM = pltpu.VMEM


def dot(a, b):
    return lax.dot_general(a, b, (((1,), (0,)), ((), ())), preferred_element_type=F32)


def three_parts(x):
    high = x.astype(BF16)
    rest = x - high.astype(F32)
    middle = rest.astype(BF16)
    low = (rest - middle.astype(F32)).astype(BF16)
    return high, middle, low


def iota(shape, dim):
    return lax.broadcasted_iota(jnp.int32, shape, dim)


def select_rows(parts, rows, width):
    row = iota((rows, width), 0)
    out = jnp.zeros((rows, width), F32)
    for number, part in enumerate(parts):
        out = jnp.where(row == number, part.astype(F32), out)
    return out.astype(BF16)


def side_by_side(ref, rows, width):
    pieces = [ref[left : left + width, :] for left in range(0, rows, width)]
    return pieces[0] if len(pieces) == 1 else jnp.concatenate(pieces, axis=1)


def state_kernel(
    decay_hbm, key_hbm, value_hbm, soft_value_hbm, query_hbm, soft_query_hbm, soft_key_hbm,
    soft_vt_ref, state_ref, cum_row_ref, cum_col_ref, value_t_ref, key_ref, query_ref, soft_query_ref, soft_key_ref,
    decay_ref, value_ref, soft_value_ref, sems,
):
    copies = [
        pltpu.make_async_copy(source, target, sems.at[place])
        for place, (source, target) in enumerate(
            (
                (decay_hbm, decay_ref),
                (key_hbm, key_ref),
                (value_hbm, value_ref),
                (soft_value_hbm, soft_value_ref),
                (soft_query_hbm, soft_query_ref),
                (soft_key_hbm, soft_key_ref),
                (query_hbm, query_ref),
            )
        )
    ]
    for copy in copies:
        copy.start()
    rows, width = key_ref.shape
    upto = (iota((rows, rows), 0) <= iota((rows, rows), 1)).astype(F32).astype(BF16)
    copies[0].wait()
    parts = select_rows(three_parts(decay_ref[...]), PAD, rows)
    cum_row = jnp.sum(dot(parts, upto), axis=0, keepdims=True)
    cum_row_ref[...] = cum_row
    cum_col = jnp.transpose(jnp.broadcast_to(cum_row, (width, rows)))
    cum_col_ref[...] = cum_col
    total = cum_col[rows - 1 :, :]
    for copy in copies[1:4]:
        copy.wait()
    decayed = (key_ref[...].astype(F32) * jnp.exp(total - cum_col)).astype(BF16)
    value_t = jnp.transpose(value_ref[...])
    value_t_ref[...] = value_t
    state_ref[:width, :] = dot(value_t, decayed).astype(BF16)
    state_ref[width:, :] = select_rows(three_parts(total), PAD, width)
    for left in range(0, rows, width):
        soft_vt_ref[left : left + width, :] = jnp.transpose(soft_value_ref[left : left + width, :])
    for copy in copies[4:]:
        copy.wait()


def sum_of_parts(tail):
    tail = tail.astype(F32)
    return tail[0:1] + tail[1:2] + tail[2:3]


def combine_kernel(axis, cores, *refs):
    *state_refs, share_ref = refs
    width = share_ref.shape[1]
    share = width // cores
    states = [ref[:width, :].astype(F32) for ref in state_refs]
    totals = [sum_of_parts(ref[width:, :]) for ref in state_refs]
    state, total = states[0], totals[0]
    if cores == 2:
        upper = lax.rem(lax.axis_index(axis), 2) == 1
        first, second = jnp.where(upper, states[1], state), jnp.where(upper, state, states[1])
        state = jnp.exp(jnp.where(upper, total, totals[1])) * first + second
        state = jnp.where(upper, state[share:], state[:share])
        total = total + totals[1]
    share_ref[:share, :] = state.astype(BF16)
    if share_ref.shape[0] > share:
        share_ref[share:, :] = select_rows(three_parts(total), PAD, width)


def soft_kernel(scale, step, q_ref, k_ref, pack_ref, qt_ref, top_ref, total_ref, summed_ref):
    rows, width = q_ref.shape
    qt_ref[...] = jnp.transpose(q_ref[...])
    value_t = side_by_side(pack_ref, rows, width)
    keep = iota((step, step), 0) <= iota((step, step), 1)
    for start in range(0, rows, step):
        stop = start + step
        scores = dot(k_ref[:stop, :], qt_ref[:, start:stop])
        last = jnp.where(keep, scores[start:, :], NEG)
        scores = jnp.concatenate([scores[:start, :], last], axis=0) if start else last
        top = jnp.max(scores, axis=0, keepdims=True)
        probs = jnp.exp2((scores - top) * scale)
        top_ref[:, start:stop] = top
        total_ref[:, start:stop] = jnp.sum(probs, axis=0, keepdims=True)
        summed_ref[:, start:stop] = dot(value_t[:, :stop], probs.astype(BF16))


def linear_kernel(step, q_ref, k_ref, value_t_ref, cum_row_ref, cum_col_ref, qt_ref, intra_ref):
    rows, width = q_ref.shape
    qt_ref[...] = jnp.transpose(q_ref[...])
    keep = iota((step, step), 0) <= iota((step, step), 1)
    for start in range(0, rows, step):
        stop = start + step
        scores = dot(k_ref[:stop, :], qt_ref[:, start:stop])
        cum_t = cum_row_ref[:, start:stop]
        cum_s = jnp.concatenate([cum_col_ref[:stop, :]] * (step // width), axis=1)
        diff = cum_t - cum_s
        last = jnp.where(keep, diff[start:, :], NEG)
        diff = jnp.concatenate([diff[:start, :], last], axis=0) if start else last
        weights = (scores * jnp.exp(diff)).astype(BF16)
        intra_ref[:, start:stop] = dot(value_t_ref[:, :stop], weights)


def by_chip(position, cores, count, body):
    pl.when(position >= cores)(lambda: body(count))
    pl.when(position < cores)(lambda: body(cores - 1))


def score_kernel(scale, step, axis, cores, offsets, qt_ref, top_ref, total_ref, *refs):
    key_refs, (probs_ref, factor_ref, sum_ref, *new_top_ref) = refs[: len(offsets)], refs[len(offsets) :]
    rows = qt_ref.shape[1]
    position = lax.axis_index(axis)
    chip = position // cores
    away = [
        jnp.where(position - chip * cores >= 1 if apart == 0 else chip >= apart, 0.0, NEG) for apart in offsets
    ]

    def body(count):
        for start in range(0, rows, step):
            mine = slice(start, start + step)
            query = qt_ref[:, mine]
            old = top_ref[:, mine]
            scores = [dot(key_ref[...], query) for key_ref in key_refs[:count]]
            top = old
            for score, off in zip(scores, away):
                top = jnp.maximum(top, jnp.max(score, axis=0, keepdims=True) + off)
            factor = jnp.exp2((old - top) * scale)
            total = total_ref[:, mine] * factor
            for place, (score, off) in enumerate(zip(scores, away)):
                probs = jnp.exp2((score - (top - off)) * scale)
                total = total + jnp.sum(probs, axis=0, keepdims=True)
                probs_ref[place * rows : (place + 1) * rows, mine] = probs.astype(BF16)
            for ref in new_top_ref:
                ref[:, mine] = top
            factor_ref[:, mine] = factor
            sum_ref[:, mine] = total

    pl.when(chip >= 1)(lambda: body(len(offsets)))
    pl.when(chip < 1)(lambda: body(offsets.count(0)))


def carried_state(position, cores, near, shares, width):
    share = width // cores
    chip = position // cores
    upper = position - chip * cores == 1
    carried = jnp.zeros((width, width), F32)
    between = jnp.zeros((1, width), F32)
    for apart in range(1, len(shares) // cores + 1):
        parts = shares[(apart - 1) * cores : apart * cores]
        state = [ref[:share, :].astype(F32) for ref in parts]
        if cores == 2:
            halves = jnp.where(upper, state[1], state[0]), jnp.where(upper, state[0], state[1])
            state = [jnp.concatenate(halves, axis=0)]
        carried = carried + jnp.exp(between + jnp.where(chip >= apart, 0.0, NEG)) * state[0]
        if parts[0].shape[0] > share:
            between = between + sum_of_parts(parts[0][share:, :])
    for ref in near:
        passed = jnp.exp(sum_of_parts(ref[width:, :])) * carried + ref[:width, :].astype(F32)
        carried = jnp.where(upper, passed, carried)
    return carried.astype(BF16)


def value_sum(values_t, probs_ref, mine):
    rows = values_t[0].shape[1]
    terms = [
        dot(value_t, probs_ref[place * rows : (place + 1) * rows, mine]) for place, value_t in enumerate(values_t)
    ]
    return functools.reduce(jnp.add, terms)


def write_out(step, sofar, values_t, probs_ref, sum_ref, carried, linear_refs, outs, buffers, sems):
    lin_qt_ref, intra_ref, cum_row_ref = linear_refs
    width, rows = lin_qt_ref.shape
    copies = []

    def put(place, mine, block):
        buffers[place][mine, :] = jnp.transpose(block.astype(BF16))
        span = pl.ds(mine.start, step)
        copy = pltpu.make_async_copy(buffers[place].at[span], outs[place].at[span], sems.at[len(copies)])
        copy.start()
        copies.append(copy)

    for start in range(0, rows, step):
        mine = slice(start, start + step)
        inter = dot(carried, lin_qt_ref[:, mine])
        summed = sofar(mine)
        if values_t:
            summed = summed + value_sum(values_t, probs_ref, mine)
        raw = intra_ref[:, mine] + inter * jnp.exp(cum_row_ref[:, mine])
        square = jnp.sum(raw * raw, axis=0, keepdims=True) * (1.0 / width)
        put(0, mine, raw * lax.rsqrt(square + TINY))
        put(1, mine, summed * (1.0 / sum_ref[:, mine]))
    for copy in copies:
        copy.wait()


def early_kernel(step, axis, cores, near_count, *refs):
    lin_qt_ref, intra_ref, cum_row_ref, summed_ref, factor_ref, sum_ref, probs_ref, late_factor_ref = refs[:8]
    linear_ref, softmax_ref, sofar_ref, *scratch, sems = refs[-6:]
    near_states, values = refs[8 : 8 + near_count], refs[8 + near_count : -6]
    width, rows = lin_qt_ref.shape
    position = lax.axis_index(axis)

    def scaled(mine):
        return summed_ref[:, mine] * factor_ref[:, mine]

    @pl.when(position >= cores)
    def _():
        values_t = [side_by_side(ref, rows, width) for ref in values[:near_count]]
        values_t += [jnp.transpose(ref[...]) for ref in values[near_count:]]
        for start in range(0, rows, step):
            mine = slice(start, start + step)
            summed = scaled(mine) + value_sum(values_t, probs_ref, mine)
            sofar_ref[:, mine] = summed * late_factor_ref[:, mine]

    @pl.when(position < cores)
    def _():
        write_out(
            step, scaled, [side_by_side(ref, rows, width) for ref in values[:near_count]], probs_ref, sum_ref,
            carried_state(position, cores, near_states, (), width),
            (lin_qt_ref, intra_ref, cum_row_ref), (linear_ref, softmax_ref), scratch, sems,
        )


def late_kernel(step, axis, cores, counts, *refs):
    refs = refs[2:]
    lin_qt_ref, intra_ref, cum_row_ref, sofar_ref, sum_ref, probs_ref = refs[:6]
    linear_ref, softmax_ref, *scratch, sems = refs[-5:]
    near_states = refs[6 : 6 + counts[0]]
    shares = refs[6 + counts[0] : 6 + counts[0] + counts[1]]
    values = refs[6 + counts[0] + counts[1] : -5]
    width, rows = lin_qt_ref.shape
    position = lax.axis_index(axis)

    @pl.when(position >= cores)
    def _():
        write_out(
            step, lambda mine: sofar_ref[:, mine], [jnp.transpose(ref[...]) for ref in values],
            probs_ref, sum_ref, carried_state(position, cores, near_states, shares, width),
            (lin_qt_ref, intra_ref, cum_row_ref), (linear_ref, softmax_ref), scratch, sems,
        )


def keep_in_hbm(x):
    return pltpu.with_memory_space_constraint(x, pltpu.HBM)


def keep_in_vmem(x):
    return pltpu.with_memory_space_constraint(x, VMEM)


def kept_in_vmem(x):
    return VMEM(x.shape, x.dtype)


def kept_in_hbm(x):
    return pltpu.HBM(x.shape, x.dtype)


def call(body, operands, outs, given=(), written=(), resumed=(), scratch=()):
    size = sum(math.prod(x.shape) * x.dtype.itemsize for x in (*given, *operands, *outs))
    inside, outside = pl.BlockSpec(memory_space=VMEM), pl.BlockSpec(memory_space=pl.ANY)
    hbm = (*given, *resumed)
    scratch = [VMEM(x.shape, x.dtype) for x in (*scratch, *written)]
    moved = len(given) + sum(x.shape[0] // math.gcd(x.shape[0], STEP) for x in written)
    return pl.pallas_call(
        body,
        out_shape=(*map(kept_in_hbm, written), *map(kept_in_vmem, outs)),
        in_specs=[outside] * len(hbm) + [inside] * len(operands),
        out_specs=(*[outside] * len(written), *[inside] * len(outs)),
        scratch_shapes=[*scratch, pltpu.SemaphoreType.DMA((moved,))] if moved else [],
        input_output_aliases={place: place for place in range(len(resumed))},
        cost_estimate=pl.CostEstimate(flops=0, bytes_accessed=size, transcendentals=0),
        compiler_params=pltpu.CompilerParams(vmem_limit_bytes=KERNEL_VMEM),
    )(*map(keep_in_hbm, hbm), *map(keep_in_vmem, operands))


def on_device(axis, lin_query, lin_key, lin_value, log_decay, soft_query, soft_key, soft_value):
    rows, heads, width = lin_query.shape
    count = lax.axis_size(axis)
    cores = 2 if count % 2 == 0 else 1
    chips = count // cores

    def across(x, apart):
        return lax.ppermute(x, axis, [(i, (i + apart * cores) % count) for i in range(count)])

    def swapped(x):
        return lax.ppermute(x, axis, [(i, i ^ 1) for i in range(count)])

    def near(blocks):
        return [swapped(block) for block in blocks] if cores == 2 else []

    def far(x):
        return [across(x, apart) for apart in range(1, chips)]

    def passed(blocks, after):
        return near(lax.optimization_barrier((block, after))[0] for block in blocks)

    def one_head(lq, lk, lv, decay, sq, sk, sv):
        step = math.gcd(rows, STEP)
        scale = math.log2(math.e) / math.sqrt(width)

        def shape(*dims, dtype=F32):
            return jax.ShapeDtypeStruct(dims, dtype)

        def half(*dims):
            return shape(*dims, dtype=BF16)

        row, flat, flat16, block = shape(1, rows), shape(width, rows), half(width, rows), half(rows, width)
        keys, values = far(sk), far(sv)
        soft_vt, state, cum_row, cum_col, lin_vt, lk, lq, sq, own_keys = call(
            state_kernel,
            (),
            (block, half(width + PAD, width), row, shape(rows, width), flat16, block, block, block, block),
            given=(decay, lk, lv, sv, lq, sq, sk),
            scratch=(row, block, block),
        )
        near_states, near_values = near([state]), near([soft_vt])
        qt, top, total, summed = call(
            functools.partial(soft_kernel, scale, step), (sq, own_keys, soft_vt), (flat16, row, row, flat)
        )
        near_states, _ = lax.optimization_barrier((near_states, summed))
        (share,) = call(
            functools.partial(combine_kernel, axis, cores),
            (state, *near_states),
            (half(width // cores + (PAD if chips > 2 else 0), width),),
        )
        shares = far(share)
        lin_qt, intra = call(
            functools.partial(linear_kernel, step), (lq, lk, lin_vt, cum_row, cum_col), (flat16, flat)
        )

        def scored(top, total, blocks, offsets, more):
            return call(
                functools.partial(score_kernel, scale, step, axis, cores, offsets),
                (qt, top, total, *blocks),
                (half(len(blocks) * rows, rows), *[row] * (2 + more)),
            )

        apart = tuple(range(1, chips))
        late_keys = passed(keys, (summed, intra))
        probs, factor, sums, *top = scored(
            top, total, [*near([sk]), *keys], (0,) * (cores - 1) + apart, len(late_keys) > 0
        )
        late_values = passed(values, (factor, shares))
        late_keys, _ = lax.optimization_barrier((late_keys, values))
        late_factor, late_sums = jnp.ones_like(factor), sums
        if late_keys:
            late_probs, late_factor, late_sums = scored(*top, sums, late_keys, apart, False)
        late_shares = passed(shares, values)
        if cores == 2:
            shares = [part for pair in zip(shares, late_shares) for part in pair]
        *began, sofar = call(
            functools.partial(early_kernel, step, axis, cores, len(near_states)),
            (
                lin_qt, intra, cum_row, summed, factor, sums, probs, late_factor,
                *near_states, *near_values, *values,
            ),
            (flat,),
            written=(block, block),
        )
        return call(
            functools.partial(late_kernel, step, axis, cores, (len(near_states), len(shares))),
            (
                lin_qt, intra, cum_row, sofar, late_sums, late_probs if late_keys else probs,
                *near_states, *shares, *late_values,
            ),
            (),
            written=(block, block),
            resumed=began,
        )

    outs = [
        one_head(
            *(x[:, head] for x in (lin_query, lin_key, lin_value)),
            log_decay[head : head + 1],
            *(x[:, head] for x in (soft_query, soft_key, soft_value)),
        )
        for head in range(heads)
    ]
    linear = jnp.stack([pair[0] for pair in outs], axis=1)
    softmax = jnp.stack([pair[1] for pair in outs], axis=1)
    return linear, softmax


def solution(mesh):
    block = P("ctx", "tp", None)
    return jax.shard_map(
        functools.partial(on_device, "ctx"),
        mesh=mesh,
        in_specs=(block, block, block, P("tp", "ctx"), block, block, block),
        out_specs=(block, block),
        check_vma=False,
    )
```

```python
import functools
import itertools
import math

import jax
import jax.numpy as jnp
from jax import lax
from jax.experimental import pallas as pl
from jax.experimental.pallas import tpu as pltpu
from jax.sharding import PartitionSpec as P

NEG = -1e30
TINY = 1e-6
PAD = 16
STEP = 256
PARTS = 4
KERNEL_VMEM = 16 * 2**20
F32 = jnp.float32
BF16 = jnp.bfloat16
VMEM = pltpu.VMEM


def dot(a, b):
    return lax.dot_general(a, b, (((1,), (0,)), ((), ())), preferred_element_type=F32)


def three_parts(x):
    high = x.astype(BF16)
    rest = x - high.astype(F32)
    middle = rest.astype(BF16)
    low = (rest - middle.astype(F32)).astype(BF16)
    return high, middle, low


def iota(shape, dim):
    return lax.broadcasted_iota(jnp.int32, shape, dim)


def select_rows(parts, rows, width):
    row = iota((rows, width), 0)
    out = jnp.zeros((rows, width), F32)
    for number, part in enumerate(parts):
        out = jnp.where(row == number, part.astype(F32), out)
    return out.astype(BF16)


def side_by_side(ref, rows, width):
    pieces = [ref[left : left + width, :] for left in range(0, rows, width)]
    return pieces[0] if len(pieces) == 1 else jnp.concatenate(pieces, axis=1)


def copies_of(source, target, sems, first):
    rows = source.shape[0]
    part = rows // PARTS if rows % (PARTS * 16) == 0 else rows
    return [
        pltpu.make_async_copy(source.at[pl.ds(start, part)], target.at[pl.ds(start, part)], sems.at[first + place])
        for place, start in enumerate(range(0, rows, part))
    ]


def state_kernel(
    decay_hbm, key_hbm, value_hbm, soft_value_hbm, query_hbm, soft_query_hbm, soft_key_hbm,
    soft_vt_ref, state_ref, cum_row_ref, cum_col_ref, value_t_ref, key_ref, query_ref, soft_query_ref, soft_key_ref,
    decay_ref, value_ref, soft_value_ref, sems,
):
    rows, width = key_ref.shape
    pairs = (
        (decay_hbm, decay_ref),
        (key_hbm, key_ref),
        (value_hbm, value_ref),
        (soft_value_hbm, soft_value_ref),
        (soft_query_hbm, soft_query_ref),
        (soft_key_hbm, soft_key_ref),
        (query_hbm, query_ref),
    )
    copies = [copies_of(*pair, sems, place * PARTS) for place, pair in enumerate(pairs)]
    for copy in itertools.chain(*copies):
        copy.start()
    upto = (iota((rows, rows), 0) <= iota((rows, rows), 1)).astype(F32).astype(BF16)
    copies[0][0].wait()
    parts = select_rows(three_parts(decay_ref[...]), PAD, rows)
    cum_row = jnp.sum(dot(parts, upto), axis=0, keepdims=True)
    cum_row_ref[...] = cum_row
    cum_col = jnp.transpose(jnp.broadcast_to(cum_row, (width, rows)))
    cum_col_ref[...] = cum_col
    total = cum_col[rows - 1 :, :]
    for copy in itertools.chain(*copies[1:4]):
        copy.wait()
    decayed = (key_ref[...].astype(F32) * jnp.exp(total - cum_col)).astype(BF16)
    value_t = jnp.transpose(value_ref[...])
    value_t_ref[...] = value_t
    state_ref[:width, :] = dot(value_t, decayed).astype(BF16)
    state_ref[width:, :] = select_rows(three_parts(total), PAD, width)
    for left in range(0, rows, width):
        soft_vt_ref[left : left + width, :] = jnp.transpose(soft_value_ref[left : left + width, :])
    for copy in itertools.chain(*copies[4:]):
        copy.wait()


def sum_of_parts(tail):
    tail = tail.astype(F32)
    return tail[0:1] + tail[1:2] + tail[2:3]


def combine_kernel(axis, cores, *refs):
    *state_refs, share_ref = refs
    width = share_ref.shape[1]
    share = width // cores
    states = [ref[:width, :].astype(F32) for ref in state_refs]
    totals = [sum_of_parts(ref[width:, :]) for ref in state_refs]
    state, total = states[0], totals[0]
    if cores == 2:
        upper = lax.rem(lax.axis_index(axis), 2) == 1
        first, second = jnp.where(upper, states[1], state), jnp.where(upper, state, states[1])
        state = jnp.exp(jnp.where(upper, total, totals[1])) * first + second
        state = jnp.where(upper, state[share:], state[:share])
        total = total + totals[1]
    share_ref[:share, :] = state.astype(BF16)
    if share_ref.shape[0] > share:
        share_ref[share:, :] = select_rows(three_parts(total), PAD, width)


def soft_kernel(scale, step, q_ref, k_ref, pack_ref, qt_ref, top_ref, total_ref, summed_ref):
    rows, width = q_ref.shape
    qt_ref[...] = jnp.transpose(q_ref[...])
    value_t = side_by_side(pack_ref, rows, width)
    keep = iota((step, step), 0) <= iota((step, step), 1)
    for start in range(0, rows, step):
        stop = start + step
        scores = dot(k_ref[:stop, :], qt_ref[:, start:stop])
        last = jnp.where(keep, scores[start:, :], NEG)
        scores = jnp.concatenate([scores[:start, :], last], axis=0) if start else last
        top = jnp.max(scores, axis=0, keepdims=True)
        probs = jnp.exp2((scores - top) * scale)
        top_ref[:, start:stop] = top
        total_ref[:, start:stop] = jnp.sum(probs, axis=0, keepdims=True)
        summed_ref[:, start:stop] = dot(value_t[:, :stop], probs.astype(BF16))


def linear_kernel(step, q_ref, k_ref, value_t_ref, cum_row_ref, cum_col_ref, qt_ref, intra_ref):
    rows, width = q_ref.shape
    qt_ref[...] = jnp.transpose(q_ref[...])
    keep = iota((step, step), 0) <= iota((step, step), 1)
    for start in range(0, rows, step):
        stop = start + step
        scores = dot(k_ref[:stop, :], qt_ref[:, start:stop])
        cum_t = cum_row_ref[:, start:stop]
        cum_s = jnp.concatenate([cum_col_ref[:stop, :]] * (step // width), axis=1)
        diff = cum_t - cum_s
        last = jnp.where(keep, diff[start:, :], NEG)
        diff = jnp.concatenate([diff[:start, :], last], axis=0) if start else last
        weights = (scores * jnp.exp(diff)).astype(BF16)
        intra_ref[:, start:stop] = dot(value_t_ref[:, :stop], weights)


def by_chip(position, cores, count, body):
    pl.when(position >= cores)(lambda: body(count))
    pl.when(position < cores)(lambda: body(cores - 1))


def score_kernel(scale, step, axis, cores, offsets, qt_ref, top_ref, total_ref, *refs):
    key_refs, (probs_ref, factor_ref, sum_ref, *new_top_ref) = refs[: len(offsets)], refs[len(offsets) :]
    rows = qt_ref.shape[1]
    position = lax.axis_index(axis)
    chip = position // cores
    away = [
        jnp.where(position - chip * cores >= 1 if apart == 0 else chip >= apart, 0.0, NEG) for apart in offsets
    ]

    def body(count):
        for start in range(0, rows, step):
            mine = slice(start, start + step)
            query = qt_ref[:, mine]
            old = top_ref[:, mine]
            scores = [dot(key_ref[...], query) for key_ref in key_refs[:count]]
            top = old
            for score, off in zip(scores, away):
                top = jnp.maximum(top, jnp.max(score, axis=0, keepdims=True) + off)
            factor = jnp.exp2((old - top) * scale)
            total = total_ref[:, mine] * factor
            for place, (score, off) in enumerate(zip(scores, away)):
                probs = jnp.exp2((score - (top - off)) * scale)
                total = total + jnp.sum(probs, axis=0, keepdims=True)
                probs_ref[place * rows : (place + 1) * rows, mine] = probs.astype(BF16)
            for ref in new_top_ref:
                ref[:, mine] = top
            factor_ref[:, mine] = factor
            sum_ref[:, mine] = total

    pl.when(chip >= 1)(lambda: body(len(offsets)))
    pl.when(chip < 1)(lambda: body(offsets.count(0)))


def carried_state(position, cores, near, shares, width):
    share = width // cores
    chip = position // cores
    upper = position - chip * cores == 1
    carried = jnp.zeros((width, width), F32)
    between = jnp.zeros((1, width), F32)
    for apart in range(1, len(shares) // cores + 1):
        parts = shares[(apart - 1) * cores : apart * cores]
        state = [ref[:share, :].astype(F32) for ref in parts]
        if cores == 2:
            halves = jnp.where(upper, state[1], state[0]), jnp.where(upper, state[0], state[1])
            state = [jnp.concatenate(halves, axis=0)]
        carried = carried + jnp.exp(between + jnp.where(chip >= apart, 0.0, NEG)) * state[0]
        if parts[0].shape[0] > share:
            between = between + sum_of_parts(parts[0][share:, :])
    for ref in near:
        passed = jnp.exp(sum_of_parts(ref[width:, :])) * carried + ref[:width, :].astype(F32)
        carried = jnp.where(upper, passed, carried)
    return carried.astype(BF16)


def value_sum(values_t, probs_ref, mine):
    rows = values_t[0].shape[1]
    terms = [
        dot(value_t, probs_ref[place * rows : (place + 1) * rows, mine]) for place, value_t in enumerate(values_t)
    ]
    return functools.reduce(jnp.add, terms)


def write_out(step, sofar, values_t, probs_ref, sum_ref, carried, linear_refs, outs, buffers, sems):
    lin_qt_ref, intra_ref, cum_row_ref = linear_refs
    width, rows = lin_qt_ref.shape
    copies = []

    def put(place, mine, block):
        buffers[place][mine, :] = jnp.transpose(block.astype(BF16))
        span = pl.ds(mine.start, step)
        for copy in copies_of(buffers[place].at[span], outs[place].at[span], sems, len(copies)):
            copy.start()
            copies.append(copy)

    for start in range(0, rows, step):
        mine = slice(start, start + step)
        inter = dot(carried, lin_qt_ref[:, mine])
        summed = sofar(mine)
        if values_t:
            summed = summed + value_sum(values_t, probs_ref, mine)
        raw = intra_ref[:, mine] + inter * jnp.exp(cum_row_ref[:, mine])
        square = jnp.sum(raw * raw, axis=0, keepdims=True) * (1.0 / width)
        put(0, mine, raw * lax.rsqrt(square + TINY))
        put(1, mine, summed * (1.0 / sum_ref[:, mine]))
    for copy in copies:
        copy.wait()


def early_kernel(step, axis, cores, near_count, *refs):
    lin_qt_ref, intra_ref, cum_row_ref, summed_ref, factor_ref, sum_ref, probs_ref, late_factor_ref = refs[:8]
    linear_ref, softmax_ref, sofar_ref, *scratch, sems = refs[-6:]
    near_states, values = refs[8 : 8 + near_count], refs[8 + near_count : -6]
    width, rows = lin_qt_ref.shape
    position = lax.axis_index(axis)

    def scaled(mine):
        return summed_ref[:, mine] * factor_ref[:, mine]

    @pl.when(position >= cores)
    def _():
        values_t = [side_by_side(ref, rows, width) for ref in values[:near_count]]
        values_t += [jnp.transpose(ref[...]) for ref in values[near_count:]]
        for start in range(0, rows, step):
            mine = slice(start, start + step)
            summed = scaled(mine) + value_sum(values_t, probs_ref, mine)
            sofar_ref[:, mine] = summed * late_factor_ref[:, mine]

    @pl.when(position < cores)
    def _():
        write_out(
            step, scaled, [side_by_side(ref, rows, width) for ref in values[:near_count]], probs_ref, sum_ref,
            carried_state(position, cores, near_states, (), width),
            (lin_qt_ref, intra_ref, cum_row_ref), (linear_ref, softmax_ref), scratch, sems,
        )


def late_kernel(step, axis, cores, counts, *refs):
    refs = refs[2:]
    lin_qt_ref, intra_ref, cum_row_ref, sofar_ref, sum_ref, probs_ref = refs[:6]
    linear_ref, softmax_ref, *scratch, sems = refs[-5:]
    near_states = refs[6 : 6 + counts[0]]
    shares = refs[6 + counts[0] : 6 + counts[0] + counts[1]]
    values = refs[6 + counts[0] + counts[1] : -5]
    width, rows = lin_qt_ref.shape
    position = lax.axis_index(axis)

    @pl.when(position >= cores)
    def _():
        write_out(
            step, lambda mine: sofar_ref[:, mine], [jnp.transpose(ref[...]) for ref in values],
            probs_ref, sum_ref, carried_state(position, cores, near_states, shares, width),
            (lin_qt_ref, intra_ref, cum_row_ref), (linear_ref, softmax_ref), scratch, sems,
        )


def keep_in_hbm(x):
    return pltpu.with_memory_space_constraint(x, pltpu.HBM)


def keep_in_vmem(x):
    return pltpu.with_memory_space_constraint(x, VMEM)


def kept_in_vmem(x):
    return VMEM(x.shape, x.dtype)


def kept_in_hbm(x):
    return pltpu.HBM(x.shape, x.dtype)


def call(body, operands, outs, given=(), written=(), resumed=(), scratch=()):
    size = sum(math.prod(x.shape) * x.dtype.itemsize for x in (*given, *operands, *outs))
    inside, outside = pl.BlockSpec(memory_space=VMEM), pl.BlockSpec(memory_space=pl.ANY)
    hbm = (*given, *resumed)
    scratch = [VMEM(x.shape, x.dtype) for x in (*scratch, *written)]
    moved = PARTS * (len(given) + sum(x.shape[0] // math.gcd(x.shape[0], STEP) for x in written))
    return pl.pallas_call(
        body,
        out_shape=(*map(kept_in_hbm, written), *map(kept_in_vmem, outs)),
        in_specs=[outside] * len(hbm) + [inside] * len(operands),
        out_specs=(*[outside] * len(written), *[inside] * len(outs)),
        scratch_shapes=[*scratch, pltpu.SemaphoreType.DMA((moved,))] if moved else [],
        input_output_aliases={place: place for place in range(len(resumed))},
        cost_estimate=pl.CostEstimate(flops=0, bytes_accessed=size, transcendentals=0),
        compiler_params=pltpu.CompilerParams(vmem_limit_bytes=KERNEL_VMEM),
    )(*map(keep_in_hbm, hbm), *map(keep_in_vmem, operands))


def on_device(axis, lin_query, lin_key, lin_value, log_decay, soft_query, soft_key, soft_value):
    rows, heads, width = lin_query.shape
    count = lax.axis_size(axis)
    cores = 2 if count % 2 == 0 else 1
    chips = count // cores

    def across(x, apart):
        return lax.ppermute(x, axis, [(i, (i + apart * cores) % count) for i in range(count)])

    def swapped(x):
        return lax.ppermute(x, axis, [(i, i ^ 1) for i in range(count)])

    def near(blocks):
        return [swapped(block) for block in blocks] if cores == 2 else []

    def far(x):
        return [across(x, apart) for apart in range(1, chips)]

    def passed(blocks, after):
        return near(lax.optimization_barrier((block, after))[0] for block in blocks)

    def one_head(lq, lk, lv, decay, sq, sk, sv):
        step = math.gcd(rows, STEP)
        scale = math.log2(math.e) / math.sqrt(width)

        def shape(*dims, dtype=F32):
            return jax.ShapeDtypeStruct(dims, dtype)

        def half(*dims):
            return shape(*dims, dtype=BF16)

        row, flat, flat16, block = shape(1, rows), shape(width, rows), half(width, rows), half(rows, width)
        keys, values = far(sk), far(sv)
        soft_vt, state, cum_row, cum_col, lin_vt, lk, lq, sq, own_keys = call(
            state_kernel,
            (),
            (block, half(width + PAD, width), row, shape(rows, width), flat16, block, block, block, block),
            given=(decay, lk, lv, sv, lq, sq, sk),
            scratch=(row, block, block),
        )
        near_states, near_values = near([state]), near([soft_vt])
        qt, top, total, summed = call(
            functools.partial(soft_kernel, scale, step), (sq, own_keys, soft_vt), (flat16, row, row, flat)
        )
        near_states, _ = lax.optimization_barrier((near_states, summed))
        (share,) = call(
            functools.partial(combine_kernel, axis, cores),
            (state, *near_states),
            (half(width // cores + (PAD if chips > 2 else 0), width),),
        )
        shares = far(share)
        lin_qt, intra = call(
            functools.partial(linear_kernel, step), (lq, lk, lin_vt, cum_row, cum_col), (flat16, flat)
        )

        def scored(top, total, blocks, offsets, more):
            return call(
                functools.partial(score_kernel, scale, step, axis, cores, offsets),
                (qt, top, total, *blocks),
                (half(len(blocks) * rows, rows), *[row] * (2 + more)),
            )

        apart = tuple(range(1, chips))
        late_keys = passed(keys, (summed, intra))
        probs, factor, sums, *top = scored(
            top, total, [*near([sk]), *keys], (0,) * (cores - 1) + apart, len(late_keys) > 0
        )
        late_values = passed(values, (factor, shares))
        late_keys, _ = lax.optimization_barrier((late_keys, values))
        late_factor, late_sums = jnp.ones_like(factor), sums
        if late_keys:
            late_probs, late_factor, late_sums = scored(*top, sums, late_keys, apart, False)
        late_shares = passed(shares, values)
        if cores == 2:
            shares = [part for pair in zip(shares, late_shares) for part in pair]
        *began, sofar = call(
            functools.partial(early_kernel, step, axis, cores, len(near_states)),
            (
                lin_qt, intra, cum_row, summed, factor, sums, probs, late_factor,
                *near_states, *near_values, *values,
            ),
            (flat,),
            written=(block, block),
        )
        return call(
            functools.partial(late_kernel, step, axis, cores, (len(near_states), len(shares))),
            (
                lin_qt, intra, cum_row, sofar, late_sums, late_probs if late_keys else probs,
                *near_states, *shares, *late_values,
            ),
            (),
            written=(block, block),
            resumed=began,
        )

    outs = [
        one_head(
            *(x[:, head] for x in (lin_query, lin_key, lin_value)),
            log_decay[head : head + 1],
            *(x[:, head] for x in (soft_query, soft_key, soft_value)),
        )
        for head in range(heads)
    ]
    linear = jnp.stack([pair[0] for pair in outs], axis=1)
    softmax = jnp.stack([pair[1] for pair in outs], axis=1)
    return linear, softmax


def solution(mesh):
    block = P("ctx", "tp", None)
    return jax.shard_map(
        functools.partial(on_device, "ctx"),
        mesh=mesh,
        in_specs=(block, block, block, P("tp", "ctx"), block, block, block),
        out_specs=(block, block),
        check_vma=False,
    )
```

```python
import functools
import math

import jax
import jax.numpy as jnp
from jax import lax
from jax.experimental import pallas as pl
from jax.experimental.pallas import tpu as pltpu
from jax.sharding import PartitionSpec as P

NEG = -1e30
TINY = 1e-6
PAD = 16
STEP = 256
KERNEL_VMEM = 16 * 2**20
F32 = jnp.float32
BF16 = jnp.bfloat16
VMEM = pltpu.VMEM


def dot(a, b):
    return lax.dot_general(a, b, (((1,), (0,)), ((), ())), preferred_element_type=F32)


def three_parts(x):
    high = x.astype(BF16)
    rest = x - high.astype(F32)
    middle = rest.astype(BF16)
    low = (rest - middle.astype(F32)).astype(BF16)
    return high, middle, low


def iota(shape, dim):
    return lax.broadcasted_iota(jnp.int32, shape, dim)


def select_rows(parts, rows, width):
    row = iota((rows, width), 0)
    out = jnp.zeros((rows, width), F32)
    for number, part in enumerate(parts):
        out = jnp.where(row == number, part.astype(F32), out)
    return out.astype(BF16)


def side_by_side(ref, rows, width):
    pieces = [ref[left : left + width, :] for left in range(0, rows, width)]
    return pieces[0] if len(pieces) == 1 else jnp.concatenate(pieces, axis=1)


def state_kernel(
    decay_hbm, key_hbm, value_hbm, soft_value_hbm, query_hbm, soft_query_hbm, soft_key_hbm,
    soft_vt_ref, state_ref, cum_row_ref, cum_col_ref, value_t_ref, key_ref, query_ref, soft_query_ref, soft_key_ref,
    decay_ref, value_ref, soft_value_ref, sems,
):
    copies = [
        pltpu.make_async_copy(source, target, sems.at[place])
        for place, (source, target) in enumerate(
            (
                (decay_hbm, decay_ref),
                (key_hbm, key_ref),
                (value_hbm, value_ref),
                (soft_value_hbm, soft_value_ref),
                (soft_query_hbm, soft_query_ref),
                (soft_key_hbm, soft_key_ref),
                (query_hbm, query_ref),
            )
        )
    ]
    for copy in copies:
        copy.start()
    rows, width = key_ref.shape
    upto = (iota((rows, rows), 0) <= iota((rows, rows), 1)).astype(F32).astype(BF16)
    copies[0].wait()
    parts = select_rows(three_parts(decay_ref[...]), PAD, rows)
    cum_row = jnp.sum(dot(parts, upto), axis=0, keepdims=True)
    cum_row_ref[...] = cum_row
    cum_col = jnp.transpose(jnp.broadcast_to(cum_row, (width, rows)))
    cum_col_ref[...] = cum_col
    total = cum_col[rows - 1 :, :]
    for copy in copies[1:4]:
        copy.wait()
    decayed = (key_ref[...].astype(F32) * jnp.exp(total - cum_col)).astype(BF16)
    value_t = jnp.transpose(value_ref[...])
    value_t_ref[...] = value_t
    state_ref[:width, :] = dot(value_t, decayed).astype(BF16)
    state_ref[width:, :] = select_rows(three_parts(total), PAD, width)
    for left in range(0, rows, width):
        soft_vt_ref[left : left + width, :] = jnp.transpose(soft_value_ref[left : left + width, :])
    for copy in copies[4:]:
        copy.wait()


def sum_of_parts(tail):
    tail = tail.astype(F32)
    return tail[0:1] + tail[1:2] + tail[2:3]


def combine_kernel(axis, cores, *refs):
    *state_refs, share_ref = refs
    width = share_ref.shape[1]
    share = width // cores
    states = [ref[:width, :].astype(F32) for ref in state_refs]
    totals = [sum_of_parts(ref[width:, :]) for ref in state_refs]
    state, total = states[0], totals[0]
    if cores == 2:
        upper = lax.rem(lax.axis_index(axis), 2) == 1
        first, second = jnp.where(upper, states[1], state), jnp.where(upper, state, states[1])
        state = jnp.exp(jnp.where(upper, total, totals[1])) * first + second
        state = jnp.where(upper, state[share:], state[:share])
        total = total + totals[1]
    share_ref[:share, :] = state.astype(BF16)
    if share_ref.shape[0] > share:
        share_ref[share:, :] = select_rows(three_parts(total), PAD, width)


def soft_kernel(scale, step, q_ref, k_ref, pack_ref, qt_ref, top_ref, total_ref, summed_ref):
    rows, width = q_ref.shape
    qt_ref[...] = jnp.transpose(q_ref[...])
    value_t = side_by_side(pack_ref, rows, width)
    keep = iota((step, step), 0) <= iota((step, step), 1)
    for start in range(0, rows, step):
        stop = start + step
        scores = dot(k_ref[:stop, :], qt_ref[:, start:stop])
        last = jnp.where(keep, scores[start:, :], NEG)
        scores = jnp.concatenate([scores[:start, :], last], axis=0) if start else last
        top = jnp.max(scores, axis=0, keepdims=True)
        probs = jnp.exp2((scores - top) * scale)
        top_ref[:, start:stop] = top
        total_ref[:, start:stop] = jnp.sum(probs, axis=0, keepdims=True)
        summed_ref[:, start:stop] = dot(value_t[:, :stop], probs.astype(BF16))


def linear_kernel(step, q_ref, k_ref, value_t_ref, cum_row_ref, cum_col_ref, qt_ref, intra_ref):
    rows, width = q_ref.shape
    qt_ref[...] = jnp.transpose(q_ref[...])
    keep = iota((step, step), 0) <= iota((step, step), 1)
    for start in range(0, rows, step):
        stop = start + step
        scores = dot(k_ref[:stop, :], qt_ref[:, start:stop])
        cum_t = cum_row_ref[:, start:stop]
        cum_s = jnp.concatenate([cum_col_ref[:stop, :]] * (step // width), axis=1)
        diff = cum_t - cum_s
        last = jnp.where(keep, diff[start:, :], NEG)
        diff = jnp.concatenate([diff[:start, :], last], axis=0) if start else last
        weights = (scores * jnp.exp(diff)).astype(BF16)
        intra_ref[:, start:stop] = dot(value_t_ref[:, :stop], weights)


def by_chip(position, cores, count, body):
    pl.when(position >= cores)(lambda: body(count))
    pl.when(position < cores)(lambda: body(cores - 1))


def score_kernel(scale, step, axis, cores, offsets, qt_ref, top_ref, total_ref, *refs):
    key_refs, (probs_ref, factor_ref, sum_ref, *new_top_ref) = refs[: len(offsets)], refs[len(offsets) :]
    rows = qt_ref.shape[1]
    position = lax.axis_index(axis)
    chip = position // cores
    away = [
        jnp.where(position - chip * cores >= 1 if apart == 0 else chip >= apart, 0.0, NEG) for apart in offsets
    ]

    def body(count):
        for start in range(0, rows, step):
            mine = slice(start, start + step)
            query = qt_ref[:, mine]
            old = top_ref[:, mine]
            scores = [dot(key_ref[...], query) for key_ref in key_refs[:count]]
            top = old
            for score, off in zip(scores, away):
                top = jnp.maximum(top, jnp.max(score, axis=0, keepdims=True) + off)
            factor = jnp.exp2((old - top) * scale)
            total = total_ref[:, mine] * factor
            for place, (score, off) in enumerate(zip(scores, away)):
                probs = jnp.exp2((score - (top - off)) * scale)
                total = total + jnp.sum(probs, axis=0, keepdims=True)
                probs_ref[place * rows : (place + 1) * rows, mine] = probs.astype(BF16)
            for ref in new_top_ref:
                ref[:, mine] = top
            factor_ref[:, mine] = factor
            sum_ref[:, mine] = total

    pl.when(chip >= 1)(lambda: body(len(offsets)))
    pl.when(chip < 1)(lambda: body(offsets.count(0)))


def carried_state(position, cores, near, shares, width):
    share = width // cores
    chip = position // cores
    upper = position - chip * cores == 1
    carried = jnp.zeros((width, width), F32)
    between = jnp.zeros((1, width), F32)
    for apart in range(1, len(shares) // cores + 1):
        parts = shares[(apart - 1) * cores : apart * cores]
        state = [ref[:share, :].astype(F32) for ref in parts]
        if cores == 2:
            halves = jnp.where(upper, state[1], state[0]), jnp.where(upper, state[0], state[1])
            state = [jnp.concatenate(halves, axis=0)]
        carried = carried + jnp.exp(between + jnp.where(chip >= apart, 0.0, NEG)) * state[0]
        if parts[0].shape[0] > share:
            between = between + sum_of_parts(parts[0][share:, :])
    for ref in near:
        passed = jnp.exp(sum_of_parts(ref[width:, :])) * carried + ref[:width, :].astype(F32)
        carried = jnp.where(upper, passed, carried)
    return carried.astype(BF16)


def value_sum(values_t, probs_ref, mine):
    rows = values_t[0].shape[1]
    terms = [
        dot(value_t, probs_ref[place * rows : (place + 1) * rows, mine]) for place, value_t in enumerate(values_t)
    ]
    return functools.reduce(jnp.add, terms)


def write_out(step, sofar, values_t, probs_ref, sum_ref, carried, linear_refs, outs, buffers, sems):
    lin_qt_ref, intra_ref, cum_row_ref = linear_refs
    width, rows = lin_qt_ref.shape
    copies = []

    def put(place, mine, block):
        buffers[place][mine, :] = jnp.transpose(block.astype(BF16))
        span = pl.ds(mine.start, step)
        copy = pltpu.make_async_copy(buffers[place].at[span], outs[place].at[span], sems.at[len(copies)])
        copy.start()
        copies.append(copy)

    for start in range(0, rows, step):
        mine = slice(start, start + step)
        inter = dot(carried, lin_qt_ref[:, mine])
        summed = sofar(mine)
        if values_t:
            summed = summed + value_sum(values_t, probs_ref, mine)
        raw = intra_ref[:, mine] + inter * jnp.exp(cum_row_ref[:, mine])
        square = jnp.sum(raw * raw, axis=0, keepdims=True) * (1.0 / width)
        put(0, mine, raw * lax.rsqrt(square + TINY))
        put(1, mine, summed * (1.0 / sum_ref[:, mine]))
    for copy in copies:
        copy.wait()


def early_kernel(step, axis, cores, near_count, *refs):
    lin_qt_ref, intra_ref, cum_row_ref, summed_ref, factor_ref, sum_ref, probs_ref, late_factor_ref = refs[:8]
    linear_ref, softmax_ref, sofar_ref, *scratch, sems = refs[-6:]
    near_states, values = refs[8 : 8 + near_count], refs[8 + near_count : -6]
    width, rows = lin_qt_ref.shape
    position = lax.axis_index(axis)

    def scaled(mine):
        return summed_ref[:, mine] * factor_ref[:, mine]

    @pl.when(position >= cores)
    def _():
        values_t = [side_by_side(ref, rows, width) for ref in values[:near_count]]
        values_t += [jnp.transpose(ref[...]) for ref in values[near_count:]]
        for start in range(0, rows, step):
            mine = slice(start, start + step)
            summed = scaled(mine) + value_sum(values_t, probs_ref, mine)
            sofar_ref[:, mine] = summed * late_factor_ref[:, mine]

    @pl.when(position < cores)
    def _():
        write_out(
            rows, scaled, [side_by_side(ref, rows, width) for ref in values[:near_count]], probs_ref, sum_ref,
            carried_state(position, cores, near_states, (), width),
            (lin_qt_ref, intra_ref, cum_row_ref), (linear_ref, softmax_ref), scratch, sems,
        )


def late_kernel(step, axis, cores, counts, *refs):
    refs = refs[2:]
    lin_qt_ref, intra_ref, cum_row_ref, sofar_ref, sum_ref, probs_ref = refs[:6]
    linear_ref, softmax_ref, *scratch, sems = refs[-5:]
    near_states = refs[6 : 6 + counts[0]]
    shares = refs[6 + counts[0] : 6 + counts[0] + counts[1]]
    values = refs[6 + counts[0] + counts[1] : -5]
    width, rows = lin_qt_ref.shape
    position = lax.axis_index(axis)

    @pl.when(position >= cores)
    def _():
        write_out(
            rows, lambda mine: sofar_ref[:, mine], [jnp.transpose(ref[...]) for ref in values],
            probs_ref, sum_ref, carried_state(position, cores, near_states, shares, width),
            (lin_qt_ref, intra_ref, cum_row_ref), (linear_ref, softmax_ref), scratch, sems,
        )


def keep_in_hbm(x):
    return pltpu.with_memory_space_constraint(x, pltpu.HBM)


def keep_in_vmem(x):
    return pltpu.with_memory_space_constraint(x, VMEM)


def kept_in_vmem(x):
    return VMEM(x.shape, x.dtype)


def kept_in_hbm(x):
    return pltpu.HBM(x.shape, x.dtype)


def call(body, operands, outs, given=(), written=(), resumed=(), scratch=()):
    size = sum(math.prod(x.shape) * x.dtype.itemsize for x in (*given, *operands, *outs))
    inside, outside = pl.BlockSpec(memory_space=VMEM), pl.BlockSpec(memory_space=pl.ANY)
    hbm = (*given, *resumed)
    scratch = [VMEM(x.shape, x.dtype) for x in (*scratch, *written)]
    moved = len(given) + sum(x.shape[0] // math.gcd(x.shape[0], STEP) for x in written)
    return pl.pallas_call(
        body,
        out_shape=(*map(kept_in_hbm, written), *map(kept_in_vmem, outs)),
        in_specs=[outside] * len(hbm) + [inside] * len(operands),
        out_specs=(*[outside] * len(written), *[inside] * len(outs)),
        scratch_shapes=[*scratch, pltpu.SemaphoreType.DMA((moved,))] if moved else [],
        input_output_aliases={place: place for place in range(len(resumed))},
        cost_estimate=pl.CostEstimate(flops=0, bytes_accessed=size, transcendentals=0),
        compiler_params=pltpu.CompilerParams(vmem_limit_bytes=KERNEL_VMEM),
    )(*map(keep_in_hbm, hbm), *map(keep_in_vmem, operands))


def on_device(axis, lin_query, lin_key, lin_value, log_decay, soft_query, soft_key, soft_value):
    rows, heads, width = lin_query.shape
    count = lax.axis_size(axis)
    cores = 2 if count % 2 == 0 else 1
    chips = count // cores

    def across(x, apart):
        return lax.ppermute(x, axis, [(i, (i + apart * cores) % count) for i in range(count)])

    def swapped(x):
        return lax.ppermute(x, axis, [(i, i ^ 1) for i in range(count)])

    def near(blocks):
        return [swapped(block) for block in blocks] if cores == 2 else []

    def far(x):
        return [across(x, apart) for apart in range(1, chips)]

    def passed(blocks, after):
        return near(lax.optimization_barrier((block, after))[0] for block in blocks)

    def one_head(lq, lk, lv, decay, sq, sk, sv):
        step = math.gcd(rows, STEP)
        scale = math.log2(math.e) / math.sqrt(width)

        def shape(*dims, dtype=F32):
            return jax.ShapeDtypeStruct(dims, dtype)

        def half(*dims):
            return shape(*dims, dtype=BF16)

        row, flat, flat16, block = shape(1, rows), shape(width, rows), half(width, rows), half(rows, width)
        keys, values = far(sk), far(sv)
        soft_vt, state, cum_row, cum_col, lin_vt, lk, lq, sq, own_keys = call(
            state_kernel,
            (),
            (block, half(width + PAD, width), row, shape(rows, width), flat16, block, block, block, block),
            given=(decay, lk, lv, sv, lq, sq, sk),
            scratch=(row, block, block),
        )
        near_states, near_values = near([state]), near([soft_vt])
        qt, top, total, summed = call(
            functools.partial(soft_kernel, scale, step), (sq, own_keys, soft_vt), (flat16, row, row, flat)
        )
        near_states, _ = lax.optimization_barrier((near_states, summed))
        (share,) = call(
            functools.partial(combine_kernel, axis, cores),
            (state, *near_states),
            (half(width // cores + (PAD if chips > 2 else 0), width),),
        )
        shares = far(share)
        lin_qt, intra = call(
            functools.partial(linear_kernel, step), (lq, lk, lin_vt, cum_row, cum_col), (flat16, flat)
        )

        def scored(top, total, blocks, offsets, more):
            return call(
                functools.partial(score_kernel, scale, step, axis, cores, offsets),
                (qt, top, total, *blocks),
                (half(len(blocks) * rows, rows), *[row] * (2 + more)),
            )

        apart = tuple(range(1, chips))
        late_keys = passed(keys, (summed, intra))
        probs, factor, sums, *top = scored(
            top, total, [*near([sk]), *keys], (0,) * (cores - 1) + apart, len(late_keys) > 0
        )
        late_values = passed(values, (factor, shares))
        late_keys, _ = lax.optimization_barrier((late_keys, values))
        late_factor, late_sums = jnp.ones_like(factor), sums
        if late_keys:
            late_probs, late_factor, late_sums = scored(*top, sums, late_keys, apart, False)
        late_shares = passed(shares, values)
        if cores == 2:
            shares = [part for pair in zip(shares, late_shares) for part in pair]
        *began, sofar = call(
            functools.partial(early_kernel, step, axis, cores, len(near_states)),
            (
                lin_qt, intra, cum_row, summed, factor, sums, probs, late_factor,
                *near_states, *near_values, *values,
            ),
            (flat,),
            written=(block, block),
        )
        return call(
            functools.partial(late_kernel, step, axis, cores, (len(near_states), len(shares))),
            (
                lin_qt, intra, cum_row, sofar, late_sums, late_probs if late_keys else probs,
                *near_states, *shares, *late_values,
            ),
            (),
            written=(block, block),
            resumed=began,
        )

    outs = [
        one_head(
            *(x[:, head] for x in (lin_query, lin_key, lin_value)),
            log_decay[head : head + 1],
            *(x[:, head] for x in (soft_query, soft_key, soft_value)),
        )
        for head in range(heads)
    ]
    linear = jnp.stack([pair[0] for pair in outs], axis=1)
    softmax = jnp.stack([pair[1] for pair in outs], axis=1)
    return linear, softmax


def solution(mesh):
    block = P("ctx", "tp", None)
    return jax.shard_map(
        functools.partial(on_device, "ctx"),
        mesh=mesh,
        in_specs=(block, block, block, P("tp", "ctx"), block, block, block),
        out_specs=(block, block),
        check_vma=False,
    )
```

```python
import functools
import math

import jax
import jax.numpy as jnp
from jax import lax
from jax.experimental import pallas as pl
from jax.experimental.pallas import tpu as pltpu
from jax.sharding import PartitionSpec as P

NEG = -1e30
TINY = 1e-6
PAD = 16
STEP = 256
KERNEL_VMEM = 16 * 2**20
F32 = jnp.float32
BF16 = jnp.bfloat16
VMEM = pltpu.VMEM


def dot(a, b):
    return lax.dot_general(a, b, (((1,), (0,)), ((), ())), preferred_element_type=F32)


def three_parts(x):
    high = x.astype(BF16)
    rest = x - high.astype(F32)
    middle = rest.astype(BF16)
    low = (rest - middle.astype(F32)).astype(BF16)
    return high, middle, low


def iota(shape, dim):
    return lax.broadcasted_iota(jnp.int32, shape, dim)


def select_rows(parts, rows, width):
    row = iota((rows, width), 0)
    out = jnp.zeros((rows, width), F32)
    for number, part in enumerate(parts):
        out = jnp.where(row == number, part.astype(F32), out)
    return out.astype(BF16)


def side_by_side(ref, rows, width):
    pieces = [ref[left : left + width, :] for left in range(0, rows, width)]
    return pieces[0] if len(pieces) == 1 else jnp.concatenate(pieces, axis=1)


def state_kernel(
    decay_hbm, key_hbm, value_hbm, soft_value_hbm, query_hbm, soft_query_hbm, soft_key_hbm,
    soft_value_ref, state_ref, cum_row_ref, cum_col_ref, value_t_ref, key_ref, query_ref, soft_query_ref, soft_key_ref,
    decay_ref, value_ref, sems,
):
    copies = [
        pltpu.make_async_copy(source, target, sems.at[place])
        for place, (source, target) in enumerate(
            (
                (decay_hbm, decay_ref),
                (key_hbm, key_ref),
                (value_hbm, value_ref),
                (soft_value_hbm, soft_value_ref),
                (soft_query_hbm, soft_query_ref),
                (soft_key_hbm, soft_key_ref),
                (query_hbm, query_ref),
            )
        )
    ]
    for copy in copies:
        copy.start()
    rows, width = key_ref.shape
    upto = (iota((rows, rows), 0) <= iota((rows, rows), 1)).astype(F32).astype(BF16)
    copies[0].wait()
    parts = select_rows(three_parts(decay_ref[...]), PAD, rows)
    cum_row = jnp.sum(dot(parts, upto), axis=0, keepdims=True)
    cum_row_ref[...] = cum_row
    cum_col = jnp.transpose(jnp.broadcast_to(cum_row, (width, rows)))
    cum_col_ref[...] = cum_col
    total = cum_col[rows - 1 :, :]
    for copy in copies[1:3]:
        copy.wait()
    decayed = (key_ref[...].astype(F32) * jnp.exp(total - cum_col)).astype(BF16)
    value_t = jnp.transpose(value_ref[...])
    value_t_ref[...] = value_t
    state_ref[:width, :] = dot(value_t, decayed).astype(BF16)
    state_ref[width:, :] = select_rows(three_parts(total), PAD, width)
    for copy in copies[3:]:
        copy.wait()


def sum_of_parts(tail):
    tail = tail.astype(F32)
    return tail[0:1] + tail[1:2] + tail[2:3]


def combine_kernel(axis, cores, *refs):
    *state_refs, share_ref = refs
    width = share_ref.shape[1]
    share = width // cores
    states = [ref[:width, :].astype(F32) for ref in state_refs]
    totals = [sum_of_parts(ref[width:, :]) for ref in state_refs]
    state, total = states[0], totals[0]
    if cores == 2:
        upper = lax.rem(lax.axis_index(axis), 2) == 1
        first, second = jnp.where(upper, states[1], state), jnp.where(upper, state, states[1])
        state = jnp.exp(jnp.where(upper, total, totals[1])) * first + second
        state = jnp.where(upper, state[share:], state[:share])
        total = total + totals[1]
    share_ref[:share, :] = state.astype(BF16)
    if share_ref.shape[0] > share:
        share_ref[share:, :] = select_rows(three_parts(total), PAD, width)


def soft_kernel(scale, step, q_ref, k_ref, v_ref, soft_vt_ref, qt_ref, top_ref, total_ref, summed_ref):
    rows, width = q_ref.shape
    qt_ref[...] = jnp.transpose(q_ref[...])
    value_t = jnp.transpose(v_ref[...])
    for left in range(0, rows, width):
        soft_vt_ref[left : left + width, :] = value_t[:, left : left + width]
    keep = iota((step, step), 0) <= iota((step, step), 1)
    for start in range(0, rows, step):
        stop = start + step
        scores = dot(k_ref[:stop, :], qt_ref[:, start:stop])
        last = jnp.where(keep, scores[start:, :], NEG)
        scores = jnp.concatenate([scores[:start, :], last], axis=0) if start else last
        top = jnp.max(scores, axis=0, keepdims=True)
        probs = jnp.exp2((scores - top) * scale)
        top_ref[:, start:stop] = top
        total_ref[:, start:stop] = jnp.sum(probs, axis=0, keepdims=True)
        summed_ref[:, start:stop] = dot(value_t[:, :stop], probs.astype(BF16))


def linear_kernel(step, q_ref, k_ref, value_t_ref, cum_row_ref, cum_col_ref, qt_ref, intra_ref):
    rows, width = q_ref.shape
    qt_ref[...] = jnp.transpose(q_ref[...])
    keep = iota((step, step), 0) <= iota((step, step), 1)
    for start in range(0, rows, step):
        stop = start + step
        scores = dot(k_ref[:stop, :], qt_ref[:, start:stop])
        cum_t = cum_row_ref[:, start:stop]
        cum_s = jnp.concatenate([cum_col_ref[:stop, :]] * (step // width), axis=1)
        diff = cum_t - cum_s
        last = jnp.where(keep, diff[start:, :], NEG)
        diff = jnp.concatenate([diff[:start, :], last], axis=0) if start else last
        weights = (scores * jnp.exp(diff)).astype(BF16)
        intra_ref[:, start:stop] = dot(value_t_ref[:, :stop], weights)


def by_chip(position, cores, count, body):
    pl.when(position >= cores)(lambda: body(count))
    pl.when(position < cores)(lambda: body(cores - 1))


def score_kernel(scale, step, axis, cores, offsets, qt_ref, top_ref, total_ref, *refs):
    key_refs, (probs_ref, factor_ref, sum_ref, *new_top_ref) = refs[: len(offsets)], refs[len(offsets) :]
    rows = qt_ref.shape[1]
    position = lax.axis_index(axis)
    chip = position // cores
    away = [
        jnp.where(position - chip * cores >= 1 if apart == 0 else chip >= apart, 0.0, NEG) for apart in offsets
    ]

    def body(count):
        for start in range(0, rows, step):
            mine = slice(start, start + step)
            query = qt_ref[:, mine]
            old = top_ref[:, mine]
            scores = [dot(key_ref[...], query) for key_ref in key_refs[:count]]
            top = old
            for score, off in zip(scores, away):
                top = jnp.maximum(top, jnp.max(score, axis=0, keepdims=True) + off)
            factor = jnp.exp2((old - top) * scale)
            total = total_ref[:, mine] * factor
            for place, (score, off) in enumerate(zip(scores, away)):
                probs = jnp.exp2((score - (top - off)) * scale)
                total = total + jnp.sum(probs, axis=0, keepdims=True)
                probs_ref[place * rows : (place + 1) * rows, mine] = probs.astype(BF16)
            for ref in new_top_ref:
                ref[:, mine] = top
            factor_ref[:, mine] = factor
            sum_ref[:, mine] = total

    pl.when(chip >= 1)(lambda: body(len(offsets)))
    pl.when(chip < 1)(lambda: body(offsets.count(0)))


def carried_state(position, cores, near, shares, width):
    share = width // cores
    chip = position // cores
    upper = position - chip * cores == 1
    carried = jnp.zeros((width, width), F32)
    between = jnp.zeros((1, width), F32)
    for apart in range(1, len(shares) // cores + 1):
        parts = shares[(apart - 1) * cores : apart * cores]
        state = [ref[:share, :].astype(F32) for ref in parts]
        if cores == 2:
            halves = jnp.where(upper, state[1], state[0]), jnp.where(upper, state[0], state[1])
            state = [jnp.concatenate(halves, axis=0)]
        carried = carried + jnp.exp(between + jnp.where(chip >= apart, 0.0, NEG)) * state[0]
        if parts[0].shape[0] > share:
            between = between + sum_of_parts(parts[0][share:, :])
    for ref in near:
        passed = jnp.exp(sum_of_parts(ref[width:, :])) * carried + ref[:width, :].astype(F32)
        carried = jnp.where(upper, passed, carried)
    return carried.astype(BF16)


def value_sum(values_t, probs_ref, mine):
    rows = values_t[0].shape[1]
    terms = [
        dot(value_t, probs_ref[place * rows : (place + 1) * rows, mine]) for place, value_t in enumerate(values_t)
    ]
    return functools.reduce(jnp.add, terms)


def write_out(step, sofar, values_t, probs_ref, sum_ref, carried, linear_refs, outs, buffers, sems):
    lin_qt_ref, intra_ref, cum_row_ref = linear_refs
    width, rows = lin_qt_ref.shape
    copies = []

    def put(place, mine, block):
        buffers[place][mine, :] = jnp.transpose(block.astype(BF16))
        span = pl.ds(mine.start, step)
        copy = pltpu.make_async_copy(buffers[place].at[span], outs[place].at[span], sems.at[len(copies)])
        copy.start()
        copies.append(copy)

    for start in range(0, rows, step):
        mine = slice(start, start + step)
        inter = dot(carried, lin_qt_ref[:, mine])
        summed = sofar(mine)
        if values_t:
            summed = summed + value_sum(values_t, probs_ref, mine)
        raw = intra_ref[:, mine] + inter * jnp.exp(cum_row_ref[:, mine])
        square = jnp.sum(raw * raw, axis=0, keepdims=True) * (1.0 / width)
        put(0, mine, raw * lax.rsqrt(square + TINY))
        put(1, mine, summed * (1.0 / sum_ref[:, mine]))
    for copy in copies:
        copy.wait()


def early_kernel(step, axis, cores, near_count, *refs):
    lin_qt_ref, intra_ref, cum_row_ref, summed_ref, factor_ref, sum_ref, probs_ref, late_factor_ref = refs[:8]
    linear_ref, softmax_ref, sofar_ref, *scratch, sems = refs[-6:]
    near_states, values = refs[8 : 8 + near_count], refs[8 + near_count : -6]
    width, rows = lin_qt_ref.shape
    position = lax.axis_index(axis)

    def scaled(mine):
        return summed_ref[:, mine] * factor_ref[:, mine]

    @pl.when(position >= cores)
    def _():
        values_t = [side_by_side(ref, rows, width) for ref in values[:near_count]]
        values_t += [jnp.transpose(ref[...]) for ref in values[near_count:]]
        for start in range(0, rows, step):
            mine = slice(start, start + step)
            summed = scaled(mine) + value_sum(values_t, probs_ref, mine)
            sofar_ref[:, mine] = summed * late_factor_ref[:, mine]

    @pl.when(position < cores)
    def _():
        write_out(
            rows, scaled, [side_by_side(ref, rows, width) for ref in values[:near_count]], probs_ref, sum_ref,
            carried_state(position, cores, near_states, (), width),
            (lin_qt_ref, intra_ref, cum_row_ref), (linear_ref, softmax_ref), scratch, sems,
        )


def late_kernel(step, axis, cores, counts, *refs):
    refs = refs[2:]
    lin_qt_ref, intra_ref, cum_row_ref, sofar_ref, sum_ref, probs_ref = refs[:6]
    linear_ref, softmax_ref, *scratch, sems = refs[-5:]
    near_states = refs[6 : 6 + counts[0]]
    shares = refs[6 + counts[0] : 6 + counts[0] + counts[1]]
    values = refs[6 + counts[0] + counts[1] : -5]
    width, rows = lin_qt_ref.shape
    position = lax.axis_index(axis)

    @pl.when(position >= cores)
    def _():
        write_out(
            rows, lambda mine: sofar_ref[:, mine], [jnp.transpose(ref[...]) for ref in values],
            probs_ref, sum_ref, carried_state(position, cores, near_states, shares, width),
            (lin_qt_ref, intra_ref, cum_row_ref), (linear_ref, softmax_ref), scratch, sems,
        )


def keep_in_hbm(x):
    return pltpu.with_memory_space_constraint(x, pltpu.HBM)


def keep_in_vmem(x):
    return pltpu.with_memory_space_constraint(x, VMEM)


def kept_in_vmem(x):
    return VMEM(x.shape, x.dtype)


def kept_in_hbm(x):
    return pltpu.HBM(x.shape, x.dtype)


def call(body, operands, outs, given=(), written=(), resumed=(), scratch=()):
    size = sum(math.prod(x.shape) * x.dtype.itemsize for x in (*given, *operands, *outs))
    inside, outside = pl.BlockSpec(memory_space=VMEM), pl.BlockSpec(memory_space=pl.ANY)
    hbm = (*given, *resumed)
    scratch = [VMEM(x.shape, x.dtype) for x in (*scratch, *written)]
    moved = len(given) + sum(x.shape[0] // math.gcd(x.shape[0], STEP) for x in written)
    return pl.pallas_call(
        body,
        out_shape=(*map(kept_in_hbm, written), *map(kept_in_vmem, outs)),
        in_specs=[outside] * len(hbm) + [inside] * len(operands),
        out_specs=(*[outside] * len(written), *[inside] * len(outs)),
        scratch_shapes=[*scratch, pltpu.SemaphoreType.DMA((moved,))] if moved else [],
        input_output_aliases={place: place for place in range(len(resumed))},
        cost_estimate=pl.CostEstimate(flops=0, bytes_accessed=size, transcendentals=0),
        compiler_params=pltpu.CompilerParams(vmem_limit_bytes=KERNEL_VMEM),
    )(*map(keep_in_hbm, hbm), *map(keep_in_vmem, operands))


def on_device(axis, lin_query, lin_key, lin_value, log_decay, soft_query, soft_key, soft_value):
    rows, heads, width = lin_query.shape
    count = lax.axis_size(axis)
    cores = 2 if count % 2 == 0 else 1
    chips = count // cores

    def across(x, apart):
        return lax.ppermute(x, axis, [(i, (i + apart * cores) % count) for i in range(count)])

    def swapped(x):
        return lax.ppermute(x, axis, [(i, i ^ 1) for i in range(count)])

    def near(blocks):
        return [swapped(block) for block in blocks] if cores == 2 else []

    def far(x):
        return [across(x, apart) for apart in range(1, chips)]

    def passed(blocks, after):
        return near(lax.optimization_barrier((block, after))[0] for block in blocks)

    def one_head(lq, lk, lv, decay, sq, sk, sv):
        step = math.gcd(rows, STEP)
        scale = math.log2(math.e) / math.sqrt(width)

        def shape(*dims, dtype=F32):
            return jax.ShapeDtypeStruct(dims, dtype)

        def half(*dims):
            return shape(*dims, dtype=BF16)

        row, flat, flat16, block = shape(1, rows), shape(width, rows), half(width, rows), half(rows, width)
        keys, values = far(sk), far(sv)
        own_values, state, cum_row, cum_col, lin_vt, lk, lq, sq, own_keys = call(
            state_kernel,
            (),
            (block, half(width + PAD, width), row, shape(rows, width), flat16, block, block, block, block),
            given=(decay, lk, lv, sv, lq, sq, sk),
            scratch=(row, block),
        )
        near_states = near([state])
        soft_vt, qt, top, total, summed = call(
            functools.partial(soft_kernel, scale, step), (sq, own_keys, own_values), (block, flat16, row, row, flat)
        )
        near_values = near([soft_vt])
        near_states, _ = lax.optimization_barrier((near_states, summed))
        (share,) = call(
            functools.partial(combine_kernel, axis, cores),
            (state, *near_states),
            (half(width // cores + (PAD if chips > 2 else 0), width),),
        )
        shares = far(share)
        lin_qt, intra = call(
            functools.partial(linear_kernel, step), (lq, lk, lin_vt, cum_row, cum_col), (flat16, flat)
        )

        def scored(top, total, blocks, offsets, more):
            return call(
                functools.partial(score_kernel, scale, step, axis, cores, offsets),
                (qt, top, total, *blocks),
                (half(len(blocks) * rows, rows), *[row] * (2 + more)),
            )

        apart = tuple(range(1, chips))
        late_keys = passed(keys, (summed, intra))
        probs, factor, sums, *top = scored(
            top, total, [*near([sk]), *keys], (0,) * (cores - 1) + apart, len(late_keys) > 0
        )
        late_values = passed(values, (factor, shares))
        late_keys, _ = lax.optimization_barrier((late_keys, values))
        late_factor, late_sums = jnp.ones_like(factor), sums
        if late_keys:
            late_probs, late_factor, late_sums = scored(*top, sums, late_keys, apart, False)
        late_shares = passed(shares, values)
        if cores == 2:
            shares = [part for pair in zip(shares, late_shares) for part in pair]
        *began, sofar = call(
            functools.partial(early_kernel, step, axis, cores, len(near_states)),
            (
                lin_qt, intra, cum_row, summed, factor, sums, probs, late_factor,
                *near_states, *near_values, *values,
            ),
            (flat,),
            written=(block, block),
        )
        return call(
            functools.partial(late_kernel, step, axis, cores, (len(near_states), len(shares))),
            (
                lin_qt, intra, cum_row, sofar, late_sums, late_probs if late_keys else probs,
                *near_states, *shares, *late_values,
            ),
            (),
            written=(block, block),
            resumed=began,
        )

    outs = [
        one_head(
            *(x[:, head] for x in (lin_query, lin_key, lin_value)),
            log_decay[head : head + 1],
            *(x[:, head] for x in (soft_query, soft_key, soft_value)),
        )
        for head in range(heads)
    ]
    linear = jnp.stack([pair[0] for pair in outs], axis=1)
    softmax = jnp.stack([pair[1] for pair in outs], axis=1)
    return linear, softmax


def solution(mesh):
    block = P("ctx", "tp", None)
    return jax.shard_map(
        functools.partial(on_device, "ctx"),
        mesh=mesh,
        in_specs=(block, block, block, P("tp", "ctx"), block, block, block),
        out_specs=(block, block),
        check_vma=False,
    )
```

```python
import functools
import math

import jax
import jax.numpy as jnp
from jax import lax
from jax.experimental import pallas as pl
from jax.experimental.pallas import tpu as pltpu
from jax.sharding import PartitionSpec as P

NEG = -1e30
TINY = 1e-6
PAD = 16
STEP = 256
KERNEL_VMEM = 16 * 2**20
F32 = jnp.float32
BF16 = jnp.bfloat16
VMEM = pltpu.VMEM


def dot(a, b):
    return lax.dot_general(a, b, (((1,), (0,)), ((), ())), preferred_element_type=F32)


def three_parts(x):
    high = x.astype(BF16)
    rest = x - high.astype(F32)
    middle = rest.astype(BF16)
    low = (rest - middle.astype(F32)).astype(BF16)
    return high, middle, low


def iota(shape, dim):
    return lax.broadcasted_iota(jnp.int32, shape, dim)


def select_rows(parts, rows, width):
    row = iota((rows, width), 0)
    out = jnp.zeros((rows, width), F32)
    for number, part in enumerate(parts):
        out = jnp.where(row == number, part.astype(F32), out)
    return out.astype(BF16)


def side_by_side(ref, rows, width):
    pieces = [ref[left : left + width, :] for left in range(0, rows, width)]
    return pieces[0] if len(pieces) == 1 else jnp.concatenate(pieces, axis=1)


def state_kernel(
    decay_hbm, key_hbm, value_hbm, soft_value_hbm, query_hbm, soft_query_hbm, soft_key_hbm,
    soft_value_ref, state_ref, cum_row_ref, cum_col_ref, value_t_ref, key_ref, query_ref, soft_query_ref, soft_key_ref,
    decay_ref, value_ref, sems,
):
    copies = [
        pltpu.make_async_copy(source, target, sems.at[place])
        for place, (source, target) in enumerate(
            (
                (decay_hbm, decay_ref),
                (key_hbm, key_ref),
                (value_hbm, value_ref),
                (soft_value_hbm, soft_value_ref),
                (soft_query_hbm, soft_query_ref),
                (soft_key_hbm, soft_key_ref),
                (query_hbm, query_ref),
            )
        )
    ]
    for copy in copies:
        copy.start()
    rows, width = key_ref.shape
    upto = (iota((rows, rows), 0) <= iota((rows, rows), 1)).astype(F32).astype(BF16)
    copies[0].wait()
    parts = select_rows(three_parts(decay_ref[...]), PAD, rows)
    cum_row = jnp.sum(dot(parts, upto), axis=0, keepdims=True)
    cum_row_ref[...] = cum_row
    cum_col = jnp.transpose(jnp.broadcast_to(cum_row, (width, rows)))
    cum_col_ref[...] = cum_col
    total = cum_col[rows - 1 :, :]
    for copy in copies[1:3]:
        copy.wait()
    decayed = (key_ref[...].astype(F32) * jnp.exp(total - cum_col)).astype(BF16)
    value_t = jnp.transpose(value_ref[...])
    value_t_ref[...] = value_t
    state_ref[:width, :] = dot(value_t, decayed).astype(BF16)
    state_ref[width:, :] = select_rows(three_parts(total), PAD, width)
    for copy in copies[3:]:
        copy.wait()


def sum_of_parts(tail):
    tail = tail.astype(F32)
    return tail[0:1] + tail[1:2] + tail[2:3]


def combine_kernel(axis, cores, *refs):
    *state_refs, share_ref = refs
    width = share_ref.shape[1]
    share = width // cores
    states = [ref[:width, :].astype(F32) for ref in state_refs]
    totals = [sum_of_parts(ref[width:, :]) for ref in state_refs]
    state, total = states[0], totals[0]
    if cores == 2:
        upper = lax.rem(lax.axis_index(axis), 2) == 1
        first, second = jnp.where(upper, states[1], state), jnp.where(upper, state, states[1])
        state = jnp.exp(jnp.where(upper, total, totals[1])) * first + second
        state = jnp.where(upper, state[share:], state[:share])
        total = total + totals[1]
    share_ref[:share, :] = state.astype(BF16)
    if share_ref.shape[0] > share:
        share_ref[share:, :] = select_rows(three_parts(total), PAD, width)


def soft_kernel(scale, step, q_ref, k_ref, v_ref, soft_vt_ref, qt_ref, top_ref, total_ref, summed_ref):
    rows, width = q_ref.shape
    qt_ref[...] = jnp.transpose(q_ref[...])
    value_t = jnp.transpose(v_ref[...])
    for left in range(0, rows, width):
        soft_vt_ref[left : left + width, :] = value_t[:, left : left + width]
    keep = iota((step, step), 0) <= iota((step, step), 1)
    for start in range(0, rows, step):
        stop = start + step
        scores = dot(k_ref[:stop, :], qt_ref[:, start:stop])
        last = jnp.where(keep, scores[start:, :], NEG)
        scores = jnp.concatenate([scores[:start, :], last], axis=0) if start else last
        top = jnp.max(scores, axis=0, keepdims=True)
        probs = jnp.exp2((scores - top) * scale)
        top_ref[:, start:stop] = top
        total_ref[:, start:stop] = jnp.sum(probs, axis=0, keepdims=True)
        summed_ref[:, start:stop] = dot(value_t[:, :stop], probs.astype(BF16))


def linear_kernel(step, q_ref, k_ref, value_t_ref, cum_row_ref, cum_col_ref, qt_ref, intra_ref):
    rows, width = q_ref.shape
    qt_ref[...] = jnp.transpose(q_ref[...])
    keep = iota((step, step), 0) <= iota((step, step), 1)
    for start in range(0, rows, step):
        stop = start + step
        scores = dot(k_ref[:stop, :], qt_ref[:, start:stop])
        cum_t = cum_row_ref[:, start:stop]
        cum_s = jnp.concatenate([cum_col_ref[:stop, :]] * (step // width), axis=1)
        diff = cum_t - cum_s
        last = jnp.where(keep, diff[start:, :], NEG)
        diff = jnp.concatenate([diff[:start, :], last], axis=0) if start else last
        weights = (scores * jnp.exp(diff)).astype(BF16)
        intra_ref[:, start:stop] = dot(value_t_ref[:, :stop], weights)


def by_chip(position, cores, count, body):
    pl.when(position >= cores)(lambda: body(count))
    pl.when(position < cores)(lambda: body(cores - 1))


def score_kernel(scale, step, axis, cores, offsets, qt_ref, top_ref, total_ref, *refs):
    key_refs, (probs_ref, factor_ref, sum_ref, *new_top_ref) = refs[: len(offsets)], refs[len(offsets) :]
    rows = qt_ref.shape[1]
    position = lax.axis_index(axis)
    chip = position // cores
    away = [
        jnp.where(position - chip * cores >= 1 if apart == 0 else chip >= apart, 0.0, NEG) for apart in offsets
    ]

    def body(count):
        for start in range(0, rows, step):
            mine = slice(start, start + step)
            query = qt_ref[:, mine]
            old = top_ref[:, mine]
            scores = [dot(key_ref[...], query) for key_ref in key_refs[:count]]
            top = old
            for score, off in zip(scores, away):
                top = jnp.maximum(top, jnp.max(score, axis=0, keepdims=True) + off)
            factor = jnp.exp2((old - top) * scale)
            total = total_ref[:, mine] * factor
            for place, (score, off) in enumerate(zip(scores, away)):
                probs = jnp.exp2((score - (top - off)) * scale)
                total = total + jnp.sum(probs, axis=0, keepdims=True)
                probs_ref[place * rows : (place + 1) * rows, mine] = probs.astype(BF16)
            for ref in new_top_ref:
                ref[:, mine] = top
            factor_ref[:, mine] = factor
            sum_ref[:, mine] = total

    pl.when(chip >= 1)(lambda: body(len(offsets)))
    pl.when(chip < 1)(lambda: body(offsets.count(0)))


def carried_state(position, cores, near, shares, width):
    share = width // cores
    chip = position // cores
    upper = position - chip * cores == 1
    carried = jnp.zeros((width, width), F32)
    between = jnp.zeros((1, width), F32)
    for apart in range(1, len(shares) // cores + 1):
        parts = shares[(apart - 1) * cores : apart * cores]
        state = [ref[:share, :].astype(F32) for ref in parts]
        if cores == 2:
            halves = jnp.where(upper, state[1], state[0]), jnp.where(upper, state[0], state[1])
            state = [jnp.concatenate(halves, axis=0)]
        carried = carried + jnp.exp(between + jnp.where(chip >= apart, 0.0, NEG)) * state[0]
        if parts[0].shape[0] > share:
            between = between + sum_of_parts(parts[0][share:, :])
    for ref in near:
        passed = jnp.exp(sum_of_parts(ref[width:, :])) * carried + ref[:width, :].astype(F32)
        carried = jnp.where(upper, passed, carried)
    return carried.astype(BF16)


def value_sum(values_t, probs_ref, mine):
    rows = values_t[0].shape[1]
    terms = [
        dot(value_t, probs_ref[place * rows : (place + 1) * rows, mine]) for place, value_t in enumerate(values_t)
    ]
    return functools.reduce(jnp.add, terms)


def write_out(step, sofar, values_t, probs_ref, sum_ref, carried, linear_refs, outs, buffers, sems):
    lin_qt_ref, intra_ref, cum_row_ref = linear_refs
    width, rows = lin_qt_ref.shape
    copies = []

    def put(place, mine, block):
        buffers[place][mine, :] = jnp.transpose(block.astype(BF16))
        span = pl.ds(mine.start, step)
        copy = pltpu.make_async_copy(buffers[place].at[span], outs[place].at[span], sems.at[len(copies)])
        copy.start()
        copies.append(copy)

    for start in range(0, rows, step):
        mine = slice(start, start + step)
        inter = dot(carried, lin_qt_ref[:, mine])
        summed = sofar(mine)
        if values_t:
            summed = summed + value_sum(values_t, probs_ref, mine)
        raw = intra_ref[:, mine] + inter * jnp.exp(cum_row_ref[:, mine])
        square = jnp.sum(raw * raw, axis=0, keepdims=True) * (1.0 / width)
        put(0, mine, raw * lax.rsqrt(square + TINY))
        put(1, mine, summed * (1.0 / sum_ref[:, mine]))
    for copy in copies:
        copy.wait()


def early_kernel(step, axis, cores, near_count, *refs):
    lin_qt_ref, intra_ref, cum_row_ref, summed_ref, factor_ref, sum_ref, probs_ref, late_factor_ref = refs[:8]
    linear_ref, softmax_ref, sofar_ref, *scratch, sems = refs[-6:]
    near_states, values = refs[8 : 8 + near_count], refs[8 + near_count : -6]
    width, rows = lin_qt_ref.shape
    position = lax.axis_index(axis)

    def scaled(mine):
        return summed_ref[:, mine] * factor_ref[:, mine]

    @pl.when(position >= cores)
    def _():
        values_t = [side_by_side(ref, rows, width) for ref in values[:near_count]]
        values_t += [jnp.transpose(ref[...]) for ref in values[near_count:]]
        for start in range(0, rows, step):
            mine = slice(start, start + step)
            summed = scaled(mine) + value_sum(values_t, probs_ref, mine)
            sofar_ref[:, mine] = summed * late_factor_ref[:, mine]

    @pl.when(position < cores)
    def _():
        write_out(
            step, scaled, [side_by_side(ref, rows, width) for ref in values[:near_count]], probs_ref, sum_ref,
            carried_state(position, cores, near_states, (), width),
            (lin_qt_ref, intra_ref, cum_row_ref), (linear_ref, softmax_ref), scratch, sems,
        )


def late_kernel(step, axis, cores, counts, *refs):
    refs = refs[2:]
    lin_qt_ref, intra_ref, cum_row_ref, sofar_ref, sum_ref, probs_ref = refs[:6]
    linear_ref, softmax_ref, *scratch, sems = refs[-5:]
    near_states = refs[6 : 6 + counts[0]]
    shares = refs[6 + counts[0] : 6 + counts[0] + counts[1]]
    values = refs[6 + counts[0] + counts[1] : -5]
    width, rows = lin_qt_ref.shape
    position = lax.axis_index(axis)

    @pl.when(position >= cores)
    def _():
        write_out(
            step, lambda mine: sofar_ref[:, mine], [jnp.transpose(ref[...]) for ref in values],
            probs_ref, sum_ref, carried_state(position, cores, near_states, shares, width),
            (lin_qt_ref, intra_ref, cum_row_ref), (linear_ref, softmax_ref), scratch, sems,
        )


def keep_in_hbm(x):
    return pltpu.with_memory_space_constraint(x, pltpu.HBM)


def keep_in_vmem(x):
    return pltpu.with_memory_space_constraint(x, VMEM)


def kept_in_vmem(x):
    return VMEM(x.shape, x.dtype)


def kept_in_hbm(x):
    return pltpu.HBM(x.shape, x.dtype)


def call(body, operands, outs, given=(), written=(), resumed=(), scratch=()):
    size = sum(math.prod(x.shape) * x.dtype.itemsize for x in (*given, *operands, *outs))
    inside, outside = pl.BlockSpec(memory_space=VMEM), pl.BlockSpec(memory_space=pl.ANY)
    hbm = (*given, *resumed)
    scratch = [VMEM(x.shape, x.dtype) for x in (*scratch, *written)]
    moved = len(given) + sum(x.shape[0] // math.gcd(x.shape[0], STEP) for x in written)
    return pl.pallas_call(
        body,
        out_shape=(*map(kept_in_hbm, written), *map(kept_in_vmem, outs)),
        in_specs=[outside] * len(hbm) + [inside] * len(operands),
        out_specs=(*[outside] * len(written), *[inside] * len(outs)),
        scratch_shapes=[*scratch, pltpu.SemaphoreType.DMA((moved,))] if moved else [],
        input_output_aliases={place: place for place in range(len(resumed))},
        cost_estimate=pl.CostEstimate(flops=0, bytes_accessed=size, transcendentals=0),
        compiler_params=pltpu.CompilerParams(vmem_limit_bytes=KERNEL_VMEM),
    )(*map(keep_in_hbm, hbm), *map(keep_in_vmem, operands))


def on_device(axis, lin_query, lin_key, lin_value, log_decay, soft_query, soft_key, soft_value):
    rows, heads, width = lin_query.shape
    count = lax.axis_size(axis)
    cores = 2 if count % 2 == 0 else 1
    chips = count // cores

    def across(x, apart):
        return lax.ppermute(x, axis, [(i, (i + apart * cores) % count) for i in range(count)])

    def swapped(x):
        return lax.ppermute(x, axis, [(i, i ^ 1) for i in range(count)])

    def near(blocks):
        return [swapped(block) for block in blocks] if cores == 2 else []

    def far(x):
        return [across(x, apart) for apart in range(1, chips)]

    def passed(blocks, after):
        return near(lax.optimization_barrier((block, after))[0] for block in blocks)

    def one_head(lq, lk, lv, decay, sq, sk, sv):
        step = math.gcd(rows, STEP)
        scale = math.log2(math.e) / math.sqrt(width)

        def shape(*dims, dtype=F32):
            return jax.ShapeDtypeStruct(dims, dtype)

        def half(*dims):
            return shape(*dims, dtype=BF16)

        row, flat, flat16, block = shape(1, rows), shape(width, rows), half(width, rows), half(rows, width)
        keys, values = far(sk), far(sv)
        own_values, state, cum_row, cum_col, lin_vt, lk, lq, sq, own_keys = call(
            state_kernel,
            (),
            (block, half(width + PAD, width), row, shape(rows, width), flat16, block, block, block, block),
            given=(decay, lk, lv, sv, lq, sq, sk),
            scratch=(row, block),
        )
        near_states = near([state])
        soft_vt, qt, top, total, summed = call(
            functools.partial(soft_kernel, scale, step), (sq, own_keys, own_values), (block, flat16, row, row, flat)
        )
        near_values = near([soft_vt])
        near_states, _ = lax.optimization_barrier((near_states, summed))
        (share,) = call(
            functools.partial(combine_kernel, axis, cores),
            (state, *near_states),
            (half(width // cores + (PAD if chips > 2 else 0), width),),
        )
        shares = far(share)
        lin_qt, intra = call(
            functools.partial(linear_kernel, step), (lq, lk, lin_vt, cum_row, cum_col), (flat16, flat)
        )

        def scored(top, total, blocks, offsets, more):
            return call(
                functools.partial(score_kernel, scale, step, axis, cores, offsets),
                (qt, top, total, *blocks),
                (half(len(blocks) * rows, rows), *[row] * (2 + more)),
            )

        apart = tuple(range(1, chips))
        late_keys = passed(keys, (summed, intra))
        probs, factor, sums, *top = scored(
            top, total, [*near([sk]), *keys], (0,) * (cores - 1) + apart, len(late_keys) > 0
        )
        late_values = passed(values, (factor, shares))
        late_keys, _ = lax.optimization_barrier((late_keys, values))
        late_factor, late_sums = jnp.ones_like(factor), sums
        if late_keys:
            late_probs, late_factor, late_sums = scored(*top, sums, late_keys, apart, False)
        late_shares = passed(shares, values)
        if cores == 2:
            shares = [part for pair in zip(shares, late_shares) for part in pair]
        *began, sofar = call(
            functools.partial(early_kernel, step, axis, cores, len(near_states)),
            (
                lin_qt, intra, cum_row, summed, factor, sums, probs, late_factor,
                *near_states, *near_values, *values,
            ),
            (flat,),
            written=(block, block),
        )
        return call(
            functools.partial(late_kernel, step, axis, cores, (len(near_states), len(shares))),
            (
                lin_qt, intra, cum_row, sofar, late_sums, late_probs if late_keys else probs,
                *near_states, *shares, *late_values,
            ),
            (),
            written=(block, block),
            resumed=began,
        )

    outs = [
        one_head(
            *(x[:, head] for x in (lin_query, lin_key, lin_value)),
            log_decay[head : head + 1],
            *(x[:, head] for x in (soft_query, soft_key, soft_value)),
        )
        for head in range(heads)
    ]
    linear = jnp.stack([pair[0] for pair in outs], axis=1)
    softmax = jnp.stack([pair[1] for pair in outs], axis=1)
    return linear, softmax


def solution(mesh):
    block = P("ctx", "tp", None)
    return jax.shard_map(
        functools.partial(on_device, "ctx"),
        mesh=mesh,
        in_specs=(block, block, block, P("tp", "ctx"), block, block, block),
        out_specs=(block, block),
        check_vma=False,
    )
```
